32 devices in a mesh: seq: 4 (over y, x), ctx: 8 (over z, core).
Axes of the slice: x: 2, y: 2, z: 4, core: 2. Of those that a mesh axis runs over, the one named last changes fastest.
Arguments:
- tokens: bfloat16 [4096, 1024], P(('seq', 'ctx')), may hold values from -6 to 6
- cotangent: bfloat16 [4096, 1024], P(('seq', 'ctx')), may hold values from -6 to 6
- gain_input: bfloat16 [1024], P('seq'), may hold values from 0.5 to 1.5
- w_query: bfloat16 [1024, 512], P('seq'), may hold values from -0.1875 to 0.1875
- key_weight: bfloat16 [1024, 128], P('seq'), may hold values from -0.1875 to 0.1875
- value_weight: bfloat16 [1024, 128], P('seq'), may hold values from -0.1875 to 0.1875
- w_mixin: bfloat16 [1024, 3352], P('seq'), may hold values from -0.1875 to 0.1875
- conv_taps: bfloat16 [4, 1792], P(None, 'seq'), may hold values from -3 to 3
- conv_bias: bfloat16 [1792], P('seq'), may hold values from -3 to 3
- step_offset: float32 [24], replicated, may hold values from -1 to 1
- decay_rate: float32 [24], replicated, may hold values from 0.0001953125 to 0.06
- skip_gain: float32 [24], replicated, may hold values from 0.5 to 1.5
- gain_mixer: bfloat16 [1536], P('seq'), may hold values from 0.5 to 1.5
- w_mixout: bfloat16 [1536, 1024], P('seq'), may hold values from -0.15625 to 0.15625
- w_attnout: bfloat16 [512, 1024], P('seq'), may hold values from -2 to 2
- gain_feed: bfloat16 [1024], P('seq'), may hold values from 0.5 to 1.5
- w_gate: bfloat16 [1024, 2048], P('seq'), may hold values from -0.1875 to 0.1875
- w_up: bfloat16 [1024, 2048], P('seq'), may hold values from -0.1875 to 0.1875
- w_down: bfloat16 [2048, 1024], P('seq'), may hold values from -0.125 to 0.125
Outputs:
- layer_out: bfloat16 [4096, 1024], P(('seq', 'ctx'))
- grad_tokens: float32 [4096, 1024], P(('seq', 'ctx'))
- grad_normin: float32 [1024], P('seq')
- grad_query: float32 [1024, 512], P('seq')
- grad_key: float32 [1024, 128], P('seq')
- grad_value: float32 [1024, 128], P('seq')
- grad_mixin: float32 [1024, 3352], P('seq')
- grad_taps: float32 [4, 1792], P(None, 'seq')
- grad_convbias: float32 [1792], P('seq')
- grad_offset: float32 [24], replicated
- grad_rate: float32 [24], replicated
- grad_skip: float32 [24], replicated
- grad_normmix: float32 [1536], P('seq')
- grad_mixout: float32 [1536, 1024], P('seq')
- grad_attnout: float32 [512, 1024], P('seq')
- grad_normffn: float32 [1024], P('seq')
- grad_gate: float32 [1024, 2048], P('seq')
- grad_up: float32 [1024, 2048], P('seq')
- grad_down: float32 [2048, 1024], P('seq')
The draws below stay inside these ranges and needn't reach their ends.
All inputs are finite; a program needn't handle non-finite values.
Results may differ from the reference program's by a relative error of at most 0.017.
Values may be sent and summed in bfloat16 or wider, within the bound.
No kernel may reach another device: no remote copies, remote signals or barrier semaphores. Data moves between devices by JAX's collectives and lax.ppermute only.
A program may use at most 256 MiB of HBM per device.

```python
import math
import jax
import jax.numpy as jnp
from jax import lax

MODEL_WIDTH = 1024
FF = 2048
QUERY_HEADS = 8
VALUE_HEADS = 2
HEAD_SIZE = 64
MH = 24
MP = 64
NS = 128
KC = 4
TOK_DEV = 128
SEQ_LEN = 1024
SEQS = 4
TOKENS = 4096
CONVCH = 1792
WIN_OUT = 3352


def levels(key, shape, shards, least, high):
    factor_of = 1.0
    for dim, shards_of in shards:
        draws = jax.random.uniform(jax.random.fold_in(jax.random.fold_in(key, 6), dim), (shards_of,), jnp.float32, least / len(shards), high / len(shards))
        factor_of = factor_of * jnp.repeat(jnp.exp(draws), shape[dim] // shards_of).reshape((-1,) + (1,) * (len(shape) - 1 - dim))
    return factor_of


def normal_values(rng, shape, deviation, reach, cuts=(), held_as=jnp.bfloat16):
    drawn = deviation * jax.random.normal(rng, shape, jnp.float32)
    if cuts:
        drawn = drawn * levels(rng, shape, cuts, -0.22, 0.18)
    return jnp.clip(drawn, -reach, reach).astype(held_as)


def setup_inputs(seed: int = 0) -> dict:
    streams_of = jax.random.split(jax.random.key(seed), 20)
    return {
        "tokens": normal_values(streams_of[0], (TOKENS, MODEL_WIDTH), 1.0, 6.0, ((0, 32),)),
        "cotangent": normal_values(streams_of[1], (TOKENS, MODEL_WIDTH), 1.0, 6.0, ((0, 32),)),
        "gain_input": jnp.clip(1.0 + 0.1 * jax.random.normal(streams_of[2], (MODEL_WIDTH,), jnp.float32), 0.5, 1.5).astype(jnp.bfloat16),
        "w_query": normal_values(streams_of[3], (MODEL_WIDTH, QUERY_HEADS * HEAD_SIZE), MODEL_WIDTH ** -0.5, 0.1875, ((0, 4),)),
        "key_weight": normal_values(streams_of[4], (MODEL_WIDTH, VALUE_HEADS * HEAD_SIZE), MODEL_WIDTH ** -0.5, 0.1875, ((0, 4),)),
        "value_weight": normal_values(streams_of[5], (MODEL_WIDTH, VALUE_HEADS * HEAD_SIZE), MODEL_WIDTH ** -0.5, 0.1875, ((0, 4),)),
        "w_mixin": normal_values(streams_of[6], (MODEL_WIDTH, WIN_OUT), MODEL_WIDTH ** -0.5, 0.1875, ((0, 4),)),
        "conv_taps": normal_values(streams_of[7], (KC, CONVCH), 0.5, 3.0, ((1, 4),)),
        "conv_bias": normal_values(streams_of[8], (CONVCH,), 0.5, 3.0, ((0, 4),)),
        "step_offset": jnp.clip(jax.random.uniform(streams_of[9], (MH,), jnp.float32, -1.0, 1.0), -1.0, 1.0),
        "decay_rate": jnp.clip(jnp.exp(jax.random.uniform(streams_of[10], (MH,), jnp.float32, math.log(0.0001953125), math.log(0.06))), 0.0001953125, 0.06),
        "skip_gain": jnp.clip(jax.random.uniform(streams_of[11], (MH,), jnp.float32, 0.5, 1.5), 0.5, 1.5),
        "gain_mixer": jnp.clip(1.0 + 0.1 * jax.random.normal(streams_of[12], (MH * MP,), jnp.float32), 0.5, 1.5).astype(jnp.bfloat16),
        "w_mixout": normal_values(streams_of[13], (MH * MP, MODEL_WIDTH), (MH * MP) ** -0.5, 0.15625, ((0, 4),)),
        "w_attnout": normal_values(streams_of[14], (QUERY_HEADS * HEAD_SIZE, MODEL_WIDTH), (QUERY_HEADS * HEAD_SIZE // 64) ** -0.5, 2.0, ((0, 4),)),
        "gain_feed": jnp.clip(1.0 + 0.1 * jax.random.normal(streams_of[15], (MODEL_WIDTH,), jnp.float32), 0.5, 1.5).astype(jnp.bfloat16),
        "w_gate": normal_values(streams_of[16], (MODEL_WIDTH, FF), MODEL_WIDTH ** -0.5, 0.1875, ((0, 4),)),
        "w_up": normal_values(streams_of[17], (MODEL_WIDTH, FF), MODEL_WIDTH ** -0.5, 0.1875, ((0, 4),)),
        "w_down": normal_values(streams_of[18], (FF, MODEL_WIDTH), FF ** -0.5, 0.125, ((0, 4),)),
    }


norm_epsilon = 1e-06
rope_base = 100000000000.0
highest = lax.Precision.HIGHEST

@jax.custom_vjp
def lowered_forward(v):
    return lax.optimization_barrier(v.astype(jnp.bfloat16)).astype(jnp.float32)

@jax.custom_vjp
def lowered_backward(v):
    return v

def low_keep(v):
    return (lowered_forward(v), None)

def low_pass(kept, grad):
    return (grad,)

def back_keep(v):
    return (v, None)

def back_low(kept, grad):
    return (lowered_forward(grad),)
lowered_forward.defvjp(low_keep, low_pass)
lowered_backward.defvjp(back_keep, back_low)

def rms_scale(signal, gain_vec):
    return signal * lax.rsqrt(lax.optimization_barrier(jnp.mean(signal * signal, axis=-1, keepdims=True)) + norm_epsilon) * gain_vec

def rotary_apply(head_rows, token_positions):
    half_dim = head_rows.shape[-1] // 2
    frequency = rope_base ** (-(jnp.arange(half_dim, dtype=jnp.float32) * 2.0 / head_rows.shape[-1]))
    angles = token_positions.astype(jnp.float32)[:, None] * frequency[None, :]
    cosine = jnp.cos(angles)[:, None, :]
    sine_part = jnp.sin(angles)[:, None, :]
    lower_half = head_rows[..., :half_dim]
    upper_half = head_rows[..., half_dim:]
    return jnp.concatenate([lower_half * cosine - upper_half * sine_part, upper_half * cosine + lower_half * sine_part], axis=-1)

def conv_mix(extended, taps, shift):
    sequence_length = extended.shape[0] - taps.shape[0] + 1
    summed = shift[None, :] + jnp.zeros((sequence_length, taps.shape[1]), jnp.float32)
    for tap_index in range(taps.shape[0]):
        summed = summed + taps[tap_index][None, :] * extended[tap_index:tap_index + sequence_length]
    return jax.nn.silu(summed)

def ssm_part(mixed, raw_steps, offset, rates, skip_gain, inner_width):
    head_count = raw_steps.shape[1]
    state_size = (mixed.shape[1] - inner_width) // 2
    sequence_length = mixed.shape[0]
    head_input = mixed[:, :inner_width].reshape(sequence_length, head_count, inner_width // head_count)
    state_in = mixed[:, inner_width:inner_width + state_size]
    state_out = mixed[:, inner_width + state_size:]
    step_sizes = jax.nn.softplus(raw_steps + offset[None, :])
    log_decay = -step_sizes * rates[None, :]
    cumulated = jnp.cumsum(log_decay, axis=0)
    causal = jnp.arange(sequence_length, dtype=jnp.int32)[:, None] >= jnp.arange(sequence_length, dtype=jnp.int32)[None, :]
    log_gaps = cumulated.T[:, :, None] - cumulated.T[:, None, :]
    weights = jnp.where(causal[None], jnp.exp(jnp.where(causal[None], log_gaps, 0.0)), 0.0)
    intersection = jnp.dot(state_out, state_in.T, precision=highest)
    mixing = weights * intersection[None] * step_sizes.T[:, None, :]
    within = jnp.einsum('hts,shp->thp', mixing, head_input, precision=highest)
    out_zero = within + skip_gain[None, :, None] * head_input
    tail_weight = jnp.exp(cumulated[-1][None, :] - cumulated) * step_sizes
    local_state = jnp.einsum('sh,shp,sn->hpn', tail_weight, head_input, state_in, precision=highest)
    return (out_zero, local_state, jnp.exp(cumulated[-1]), state_out, cumulated)

def finish(out_zero, state_out, cumulated, start_state, gate_z, gain_vec):
    across = jnp.einsum('tn,hpn->thp', state_out, start_state, precision=highest) * jnp.exp(cumulated)[:, :, None]
    whole = out_zero + across
    gated = whole.reshape(whole.shape[0], -1) * jax.nn.silu(gate_z)
    return rms_scale(gated, gain_vec)

def attention_apply(query_rows, key_row_block, value_rows):
    sequence_length = query_rows.shape[0]
    sequence_group = QUERY_HEADS // VALUE_HEADS
    block = min(512, sequence_length)
    grouped_heads = query_rows.reshape(sequence_length, VALUE_HEADS, sequence_group, HEAD_SIZE)
    scale = HEAD_SIZE ** (-0.5)

    def one_block(block_index):
        start = block_index * block
        part = lax.dynamic_slice_in_dim(grouped_heads, start, block, 0)
        scores = lowered_backward(jnp.einsum('qkgd,skd->kgqs', part, key_row_block, precision=highest) * scale)
        query_pos = start + jnp.arange(block, dtype=jnp.int32)
        allowed = jnp.arange(sequence_length, dtype=jnp.int32)[None, :] <= query_pos[:, None]
        masked = jnp.where(allowed[None, None], scores, -1e+30)
        running = lax.optimization_barrier(jnp.max(masked, axis=-1, keepdims=True))
        expanded = jnp.exp(masked - running)
        attn_prob = lowered_forward(expanded / lax.optimization_barrier(jnp.sum(expanded, axis=-1, keepdims=True)))
        return jnp.einsum('kgqs,skd->qkgd', attn_prob, value_rows, precision=highest).reshape(block, QUERY_HEADS * HEAD_SIZE)
    return lax.map(jax.checkpoint(one_block), jnp.arange(sequence_length // block, dtype=jnp.int32)).reshape(sequence_length, QUERY_HEADS * HEAD_SIZE)

def one_sequence(single, params):
    gain_input, w_query, key_weight, value_weight, w_mixin, conv_taps, conv_bias, step_offset, decay_rate, skip_gain, gain_mixer, w_mixout, w_attnout, gain_feed, w_gate, w_up, w_down = params
    sequence_length = single.shape[0]
    token_positions = jnp.arange(sequence_length, dtype=jnp.int32)
    normed = lowered_forward(rms_scale(single, gain_input))
    q_pre = lowered_backward(jnp.dot(normed, w_query, precision=highest))
    key_prerotary = lowered_backward(jnp.dot(normed, key_weight, precision=highest))
    value_lowered = lowered_forward(lowered_backward(jnp.dot(normed, value_weight, precision=highest)))
    query_rows = lowered_forward(rotary_apply(q_pre.reshape(sequence_length, QUERY_HEADS, HEAD_SIZE), token_positions))
    key_row_block = lowered_forward(rotary_apply(key_prerotary.reshape(sequence_length, VALUE_HEADS, HEAD_SIZE), token_positions))
    attended_rows = lowered_forward(lowered_backward(attention_apply(query_rows, key_row_block, value_lowered.reshape(sequence_length, VALUE_HEADS, HEAD_SIZE))))
    attn_out = lowered_backward(jnp.dot(attended_rows, w_attnout, precision=highest))
    mix_pre = lowered_backward(jnp.dot(normed, w_mixin, precision=highest))
    inner_width = MH * MP
    conv_width = inner_width + 2 * NS
    gate_z = mix_pre[:, :inner_width]
    conv_in = lowered_forward(mix_pre[:, inner_width:inner_width + conv_width])
    raw_steps = mix_pre[:, inner_width + conv_width:]
    extended = jnp.concatenate([jnp.zeros((KC - 1, conv_width), jnp.float32), conv_in], axis=0)
    mixed = conv_mix(extended, conv_taps, conv_bias)
    blocks = sequence_length // TOK_DEV

    def block_step(state, pieces):
        mixed_part, step_part, gate_part = pieces
        out_zero, local_state, decay, state_out, cumulated = ssm_part(mixed_part, step_part, step_offset, decay_rate, skip_gain, inner_width)
        normed_part = finish(out_zero, state_out, cumulated, state, gate_part, gain_mixer)
        return (decay[:, None, None] * state + local_state, normed_part)
    start_state = jnp.zeros((MH, MP, NS), jnp.float32)
    final_state, mix_normed = lax.scan(jax.checkpoint(block_step), start_state, (mixed.reshape(blocks, TOK_DEV, conv_width), raw_steps.reshape(blocks, TOK_DEV, MH), gate_z.reshape(blocks, TOK_DEV, inner_width)))
    mix_low = lowered_forward(mix_normed.reshape(sequence_length, inner_width))
    mix_out = lowered_backward(jnp.dot(mix_low, w_mixout, precision=highest))
    residual = single + attn_out + mix_out
    feed_in = lowered_forward(rms_scale(residual, gain_feed))
    gate = lowered_backward(jnp.dot(feed_in, w_gate, precision=highest))
    up_part = lowered_backward(jnp.dot(feed_in, w_up, precision=highest))
    hidden = lowered_forward(jax.nn.silu(gate) * up_part)
    return residual + lowered_backward(jnp.dot(hidden, w_down, precision=highest))

def reference(tokens, cotangent, gain_input, w_query, key_weight, value_weight, w_mixin, conv_taps, conv_bias, step_offset, decay_rate, skip_gain, gain_mixer, w_mixout, w_attnout, gain_feed, w_gate, w_up, w_down):
    params = tuple((item.astype(jnp.float32) for item in (gain_input, w_query, key_weight, value_weight, w_mixin, conv_taps, conv_bias, step_offset, decay_rate, skip_gain, gain_mixer, w_mixout, w_attnout, gain_feed, w_gate, w_up, w_down)))

    def layer(inputs, weights):

        def single_run(single):
            return one_sequence(single, weights)
        return lax.map(jax.checkpoint(single_run), inputs.reshape(SEQS, SEQ_LEN, MODEL_WIDTH)).reshape(TOKENS, MODEL_WIDTH)
    result, pull = jax.vjp(layer, tokens.astype(jnp.float32), params)
    grad_in, grad_w = pull(cotangent.astype(jnp.float32))
    return (result.astype(jnp.bfloat16), grad_in, grad_w[0], grad_w[1], grad_w[2], grad_w[3], grad_w[4], grad_w[5], grad_w[6], grad_w[7], grad_w[8], grad_w[9], grad_w[10], grad_w[11], grad_w[12], grad_w[13], grad_w[14], grad_w[15], grad_w[16])
```

```python
import jax
import jax.numpy as jnp
from jax import lax
from jax.sharding import PartitionSpec as P

QUERY_HEADS = 8
VALUE_HEADS = 2
HEAD_SIZE = 64
MH = 24
MP = 64
NS = 128
KC = 4
GROUP = QUERY_HEADS // VALUE_HEADS
INNER = MH * MP
CONVW = INNER + 2 * NS
QW = QUERY_HEADS * HEAD_SIZE
KW = VALUE_HEADS * HEAD_SIZE

norm_epsilon = 1e-06
rope_base = 100000000000.0
highest = lax.Precision.HIGHEST
f32 = jnp.float32
bf16 = jnp.bfloat16


def dot(a, b):
    return jnp.dot(a, b, preferred_element_type=f32)


def dot_nt(a, b):
    return lax.dot_general(a, b, (((1,), (1,)), ((), ())), preferred_element_type=f32)


def dot_tn(a, b):
    return lax.dot_general(a, b, (((0,), (0,)), ((), ())), preferred_element_type=f32)


def rms_scale(signal, gain_vec):
    return (
        signal
        * lax.rsqrt(jnp.mean(signal * signal, axis=-1, keepdims=True) + norm_epsilon)
        * gain_vec
    )


def rotary_apply(head_rows, cosine, sine):
    half_dim = head_rows.shape[-1] // 2
    lower = head_rows[..., :half_dim]
    upper = head_rows[..., half_dim:]
    return jnp.concatenate(
        [lower * cosine - upper * sine, upper * cosine + lower * sine], axis=-1
    )


def conv_mix(extended, taps, shift):
    rows = extended.shape[0] - KC + 1
    summed = shift[None, :]
    for tap in range(KC):
        summed = summed + taps[tap][None, :] * extended[tap : tap + rows]
    return jax.nn.silu(summed)


def swap_core(value):
    count = lax.axis_size("ctx")
    return lax.ppermute(value, "ctx", [(i, i ^ 1) for i in range(count)])


def chip_shift(value, steps, wrap):
    count = lax.axis_size("ctx")
    pairs = []
    for i in range(count):
        to = i + 2 * steps
        if wrap:
            pairs.append((i, to % count))
        elif 0 <= to < count:
            pairs.append((i, to))
    return lax.ppermute(value, "ctx", pairs)


def seq_swap(value, k):
    count = lax.axis_size("seq")
    return lax.ppermute(value, "seq", [(i, i ^ k) for i in range(count)])


def take_half(value, core):
    rows = value.shape[0] // 2
    return lax.dynamic_slice_in_dim(value, core * rows, rows, 0)


def gather_weight(local, core):
    own = lax.all_gather(take_half(local, core), "seq", axis=0, tiled=True)
    return own, swap_core(own)


def split_cols(x, seqs, core):
    rows, width = x.shape
    part = width // (2 * seqs)
    blocks = x.reshape(rows, seqs, 2, part)
    first, second = blocks[:, :, 0], blocks[:, :, 1]
    own = jnp.where(core == 0, first, second).reshape(rows, width // 2)
    other = jnp.where(core == 0, second, first).reshape(rows, width // 2)
    return own, other


def merge_cols(own, other, seqs, core):
    rows, half = own.shape
    a = own.reshape(rows, seqs, half // seqs)
    b = other.reshape(rows, seqs, half // seqs)
    first = jnp.where(core == 0, a, b)
    second = jnp.where(core == 0, b, a)
    return jnp.stack([first, second], axis=2).reshape(rows, 2 * half)


def times_weight(x, weight, seqs, core):
    own, other = split_cols(x, seqs, core)
    return dot(own, weight[0]) + dot(other, weight[1])


def times_weight_t(y, weight, seqs, core):
    return merge_cols(dot_nt(y, weight[0]), dot_nt(y, weight[1]), seqs, core)


def gather_rows(value, seqs):
    return jnp.concatenate([value] + [seq_swap(value, k) for k in range(1, seqs)], axis=0)


def send_blocks(blocks, place, seqs):
    parts = []
    for k in range(seqs):
        piece = lax.dynamic_index_in_dim(blocks, place ^ k, 1, False)
        parts.append(piece if k == 0 else seq_swap(piece, k))
    return jnp.concatenate(parts, axis=0)


def sum_over_ctx(grad, chips, chip, core):
    rows, cols = grad.shape
    halves = grad.reshape(2, rows // 2, cols)
    mine = lax.dynamic_index_in_dim(halves, core, 0, False)
    others = lax.dynamic_index_in_dim(halves, 1 - core, 0, False).astype(bf16)
    mine = mine + swap_core(others).astype(f32)
    shards = mine.reshape(chips, rows // (2 * chips), cols)
    total = lax.dynamic_index_in_dim(shards, chip, 0, False)
    for k in range(1, chips):
        piece = lax.dynamic_index_in_dim(shards, (chip + k) % chips, 0, False).astype(bf16)
        total = total + chip_shift(piece, k, True).astype(f32)
    total = total.astype(bf16)
    got = [total] + [chip_shift(total, k, True) for k in range(1, chips)]
    got = jnp.stack(got, axis=0)
    both = jnp.stack([got, swap_core(got)], axis=0)
    parts = []
    for half in range(2):
        for q in range(chips):
            parts.append(both[half ^ core, (chip - q) % chips])
    return jnp.concatenate(parts, axis=0)


def ctx_state(value, decays, chips, chip, core, later):
    half = MH // 2
    low = value.astype(bf16)
    mine = lax.dynamic_slice_in_dim(low, core * half, half, 0)
    others = lax.dynamic_slice_in_dim(low, (1 - core) * half, half, 0)
    got = swap_core(others).astype(f32)
    mine = mine.astype(f32)
    even = jnp.where(core == 0, mine, got)
    odd = jnp.where(core == 0, got, mine)
    dec = lax.dynamic_slice_in_dim(decays, core * half, half, 2)[..., None, None]
    if later:
        chip_value = even + dec[0, 0] * odd
    else:
        chip_value = odd + dec[0, 1] * even
    chip_low = chip_value.astype(bf16)
    sign = -1 if later else 1
    total = jnp.zeros_like(chip_value)
    for k in range(chips - 1, 0, -1):
        arrived = chip_shift(chip_low, sign * k, False).astype(f32)
        rel = (sign * k) % chips
        total = arrived + dec[rel, 0] * dec[rel, 1] * total
    if later:
        for_odd = total
        for_even = odd + dec[0, 1] * total
    else:
        for_even = total
        for_odd = even + dec[0, 0] * total
    keep = jnp.where(core == 0, for_even, for_odd).astype(bf16)
    give = jnp.where(core == 0, for_odd, for_even).astype(bf16)
    back = swap_core(give)
    first = jnp.where(core == 0, keep, back)
    second = jnp.where(core == 0, back, keep)
    return jnp.concatenate([first, second], axis=0).astype(f32)


def body(
    tokens,
    cotangent,
    gain_input,
    w_query,
    key_weight,
    value_weight,
    w_mixin,
    conv_taps,
    conv_bias,
    step_offset,
    decay_rate,
    skip_gain,
    gain_mixer,
    w_mixout,
    w_attnout,
    gain_feed,
    w_gate,
    w_up,
    w_down,
):
    rows, width = tokens.shape
    seqs = lax.axis_size("seq")
    ctxs = lax.axis_size("ctx")
    chips = ctxs // 2
    place = lax.axis_index("seq")
    ctx = lax.axis_index("ctx")
    chip, core = ctx // 2, ctx % 2
    ff = w_gate.shape[1]

    sizes = (gain_input.size, gain_feed.size, conv_bias.size, gain_mixer.size, conv_taps.size)
    small = jnp.concatenate(
        [gain_input, gain_feed, conv_bias, gain_mixer, conv_taps.reshape(-1)]
    )
    small = lax.all_gather(small, "seq").astype(f32)
    at = 0
    pieces = []
    for size in sizes:
        pieces.append(small[:, at : at + size])
        at += size
    gin = pieces[0].reshape(-1)
    gfeed = pieces[1].reshape(-1)
    cbias = pieces[2].reshape(-1)
    gmix = pieces[3].reshape(-1)
    taps = pieces[4].reshape(seqs, KC, -1).transpose(1, 0, 2).reshape(KC, -1)

    in_loc = jnp.concatenate([w_query, key_weight, value_weight, w_mixin], axis=1)
    out_loc = jnp.concatenate([w_mixout, w_attnout], axis=0)
    gu_loc = jnp.concatenate([w_gate, w_up], axis=1)
    w_in = gather_weight(in_loc, core)
    w_out = gather_weight(out_loc, core)
    w_gu = gather_weight(gu_loc, core)
    w_dn = gather_weight(w_down, core)

    first_row = ctx * rows
    position = first_row + jnp.arange(rows, dtype=jnp.int32)
    frequency = rope_base ** (
        -(jnp.arange(HEAD_SIZE // 2, dtype=f32) * 2.0 / HEAD_SIZE)
    )
    angles = position.astype(f32)[:, None] * frequency[None, :]
    cosine = jnp.cos(angles)[:, None, :]
    sine = jnp.sin(angles)[:, None, :]

    x = tokens.astype(f32)
    normed = rms_scale(x, gin).astype(bf16)
    pre = times_weight(normed, w_in, seqs, core)
    q_pre = pre[:, :QW].reshape(rows, QUERY_HEADS, HEAD_SIZE)
    k_pre = pre[:, QW : QW + KW].reshape(rows, VALUE_HEADS, HEAD_SIZE)
    v_low = pre[:, QW + KW : QW + 2 * KW].astype(bf16)
    mix0 = QW + 2 * KW
    gate_z = pre[:, mix0 : mix0 + INNER]
    conv_low = pre[:, mix0 + INNER : mix0 + INNER + CONVW].astype(bf16)
    raw_step = pre[:, mix0 + INNER + CONVW :]

    queries = rotary_apply(q_pre, cosine, sine).astype(bf16)
    keys = rotary_apply(k_pre, cosine, sine).astype(bf16).reshape(rows, KW)

    step0 = jax.nn.softplus(raw_step + step_offset[None, :])
    decay = jnp.exp(jnp.sum(-step0 * decay_rate[None, :], axis=0))
    decay_hi = decay.astype(bf16)
    decay_lo = (decay - decay_hi.astype(f32)).astype(bf16)
    extra = jnp.zeros((16, 2 * KW), bf16)
    extra = extra.at[0, :MH].set(decay_hi).at[1, :MH].set(decay_lo)
    message = jnp.concatenate([jnp.concatenate([keys, v_low], axis=1), extra], axis=0)
    got = jnp.stack([message] + [chip_shift(message, k, True) for k in range(1, chips)])
    got_other = swap_core(got)
    kv_all = jnp.stack([got[:, :rows], got_other[:, :rows]])
    dec_own = got[:, rows, :MH].astype(f32) + got[:, rows + 1, :MH].astype(f32)
    dec_oth = got_other[:, rows, :MH].astype(f32) + got_other[:, rows + 1, :MH].astype(f32)
    decays = jnp.stack(
        [jnp.where(core == 0, dec_own, dec_oth), jnp.where(core == 0, dec_oth, dec_own)], axis=1
    )
    count = lax.axis_size("ctx")
    edge = lax.ppermute(
        conv_low[rows - (KC - 1) :], "ctx", [(i, i + 1) for i in range(count - 1)]
    )
    extended = jnp.concatenate([edge, conv_low], axis=0).astype(f32)

    causal = (
        jnp.arange(rows, dtype=jnp.int32)[:, None] >= jnp.arange(rows, dtype=jnp.int32)[None, :]
    )

    def ssm_local(extended_in, steps_in, taps_in, shift_in, offset_in, rates_in, skip_in):
        mixed = conv_mix(extended_in, taps_in, shift_in)
        head_input = mixed[:, :INNER].reshape(rows, MH, MP)
        b_state = mixed[:, INNER : INNER + NS]
        c_state = mixed[:, INNER + NS :]
        step = jax.nn.softplus(steps_in + offset_in[None, :])
        cum = jnp.cumsum(-step * rates_in[None, :], axis=0)
        gaps = cum.T[:, :, None] - cum.T[:, None, :]
        weights = jnp.where(causal[None], jnp.exp(jnp.where(causal[None], gaps, 0.0)), 0.0)
        inter = jnp.dot(c_state, b_state.T, precision=highest)
        mixing = weights * inter[None] * step.T[:, None, :]
        within = jnp.einsum("hts,shp->thp", mixing, head_input, precision=highest)
        out_zero = within + skip_in[None, :, None] * head_input
        tail = jnp.exp(cum[-1][None, :] - cum) * step
        local_state = jnp.einsum(
            "shp,sn->hpn", tail[:, :, None] * head_input, b_state, precision=highest
        )
        return out_zero, local_state, jnp.exp(cum[-1]), c_state, jnp.exp(cum)

    (out_zero, local_state, own_decay, c_state, exp_cum), pull_local = jax.vjp(
        ssm_local, extended, raw_step, taps, cbias, step_offset, decay_rate, skip_gain
    )
    start_state = ctx_state(local_state, decays, chips, chip, core, False)

    qpos = jnp.tile(position, GROUP)
    query_rows = (
        queries.reshape(rows, VALUE_HEADS, GROUP, HEAD_SIZE)
        .transpose(1, 2, 0, 3)
        .reshape(VALUE_HEADS, GROUP * rows, HEAD_SIZE)
    )
    rel = jnp.arange(chips, dtype=jnp.int32)
    key_chip = chip - rel
    side = jnp.stack([core, 1 - core])
    key_pos = (
        (key_chip[None, :, None] * 2 + side[:, None, None]) * rows
        + jnp.arange(rows, dtype=jnp.int32)[None, None, :]
    )
    key_pos = jnp.where(key_chip[None, :, None] >= 0, key_pos, ctxs * rows).reshape(-1)
    total_keys = key_pos.shape[0]
    kv_flat = kv_all.reshape(total_keys, 2, VALUE_HEADS, HEAD_SIZE)
    key_heads = kv_flat[:, 0].transpose(1, 0, 2)
    value_heads = kv_flat[:, 1].transpose(1, 0, 2)
    allowed = key_pos[None, :] <= qpos[:, None]
    scale = HEAD_SIZE ** (-0.5)
    scores = jnp.einsum("hrd,hkd->hrk", query_rows, key_heads, preferred_element_type=f32) * scale
    masked = jnp.where(allowed[None], scores, -1e30)
    top = jnp.max(masked, axis=-1, keepdims=True)
    expanded = jnp.exp(masked - top)
    prob = expanded / jnp.sum(expanded, axis=-1, keepdims=True)
    prob_low = prob.astype(bf16)
    attended = jnp.einsum("hrk,hkd->hrd", prob_low, value_heads, preferred_element_type=f32)
    attn_b = (
        attended.astype(bf16)
        .reshape(VALUE_HEADS, GROUP, rows, HEAD_SIZE)
        .transpose(2, 0, 1, 3)
        .reshape(rows, QW)
    )

    def finish(zero_in, c_in, exp_in, start_in, gate_in, gain_in):
        across = jnp.einsum("tn,hpn->thp", c_in, start_in, precision=highest) * exp_in[:, :, None]
        gated = (zero_in + across).reshape(rows, INNER) * jax.nn.silu(gate_in)
        return rms_scale(gated, gain_in)

    mix_normed, pull_finish = jax.vjp(
        finish, out_zero, c_state, exp_cum, start_state, gate_z, gmix
    )
    mix_b = mix_normed.astype(bf16)

    out_in = jnp.concatenate(
        [
            mix_b.reshape(rows, seqs, INNER // seqs),
            attn_b.reshape(rows, seqs, QW // seqs),
        ],
        axis=2,
    )
    out_flat = out_in.reshape(rows, INNER + QW)
    residual = x + times_weight(out_flat, w_out, seqs, core)
    feed_b, pull_feed = jax.vjp(rms_scale, residual, gfeed)
    feed_b = feed_b.astype(bf16)
    gate_up = times_weight(feed_b, w_gu, seqs, core)
    gate, up = gate_up[:, :ff], gate_up[:, ff:]
    hidden, pull_hidden = jax.vjp(lambda a, b: jax.nn.silu(a) * b, gate, up)
    hidden_b = hidden.astype(bf16)
    layer_out = (residual + times_weight(hidden_b, w_dn, seqs, core)).astype(bf16)

    left = jnp.concatenate(
        [
            normed.reshape(rows, seqs, -1),
            feed_b.reshape(rows, seqs, -1),
            out_in,
            hidden_b.reshape(rows, seqs, -1),
        ],
        axis=2,
    )
    left = send_blocks(left, place, seqs)
    wide = width // seqs
    outw = (INNER + QW) // seqs
    left_normed = left[:, :wide]
    left_feed = left[:, wide : 2 * wide]
    left_out = left[:, 2 * wide : 2 * wide + outw]
    left_hidden = left[:, 2 * wide + outw :]

    d_hidden = times_weight_t(cotangent, w_dn, seqs, core)
    d_gate, d_up = pull_hidden(d_hidden)
    d_gu = jnp.concatenate([d_gate, d_up], axis=1).astype(bf16)
    d_feed = times_weight_t(d_gu, w_gu, seqs, core)
    d_res_norm, d_gfeed = pull_feed(d_feed)
    grad_res = cotangent.astype(f32) + d_res_norm
    res_b = grad_res.astype(bf16)
    d_out = times_weight_t(res_b, w_out, seqs, core).reshape(rows, seqs, outw)
    d_mix = d_out[:, :, : INNER // seqs].reshape(rows, INNER)
    d_att = d_out[:, :, INNER // seqs :].reshape(rows, QW).astype(bf16)

    right = gather_rows(jnp.concatenate([d_gu, cotangent, res_b], axis=1), seqs)
    grad_gu = dot_tn(left_feed, right[:, : 2 * ff])
    grad_dn = dot_tn(left_hidden, right[:, 2 * ff : 2 * ff + width])
    grad_out = dot_tn(left_out, right[:, 2 * ff + width :])
    sum_gu = sum_over_ctx(grad_gu, chips, chip, core)
    sum_do = sum_over_ctx(
        jnp.concatenate([grad_dn, grad_out], axis=1), chips, chip, core
    )

    d_zero, d_c, d_exp, d_start, d_gate_z, d_gmix = pull_finish(d_mix)
    later_grad = ctx_state(d_start, decays, chips, chip, core, True)
    decay_grad = jnp.sum(later_grad * start_state, axis=(1, 2))

    grad_rows = (
        d_att.reshape(rows, VALUE_HEADS, GROUP, HEAD_SIZE)
        .transpose(1, 2, 0, 3)
        .reshape(VALUE_HEADS, GROUP * rows, HEAD_SIZE)
    )
    d_prob = jnp.einsum("hrd,hkd->hrk", grad_rows, value_heads, preferred_element_type=f32)
    delta = jnp.sum(prob * d_prob, axis=-1, keepdims=True)
    d_score = (prob * (d_prob - delta)).astype(bf16)
    d_query_rows = (
        jnp.einsum("hrk,hkd->hrd", d_score, key_heads, preferred_element_type=f32) * scale
    )
    d_keys = jnp.einsum("hrk,hrd->khd", d_score, query_rows, preferred_element_type=f32) * scale
    d_values = jnp.einsum("hrk,hrd->khd", prob_low, grad_rows, preferred_element_type=f32)
    d_kv = jnp.concatenate(
        [d_keys.reshape(total_keys, KW), d_values.reshape(total_keys, KW)], axis=1
    ).reshape(2, chips, rows, 2 * KW)
    d_kv = d_kv[0] + swap_core(d_kv[1].astype(bf16)).astype(f32)
    d_kv_own = d_kv[0]
    for k in range(1, chips):
        d_kv_own = d_kv_own + chip_shift(d_kv[k].astype(bf16), -k, False).astype(f32)
    d_queries = (
        d_query_rows.reshape(VALUE_HEADS, GROUP, rows, HEAD_SIZE)
        .transpose(2, 0, 1, 3)
        .reshape(rows, QUERY_HEADS, HEAD_SIZE)
    )
    d_q = rotary_apply(d_queries, cosine, -sine).reshape(rows, QW).astype(bf16)
    d_k = (
        rotary_apply(d_kv_own[:, :KW].reshape(rows, VALUE_HEADS, HEAD_SIZE), cosine, -sine)
        .reshape(rows, KW)
        .astype(bf16)
    )
    d_v = d_kv_own[:, KW:].astype(bf16)

    d_ext, d_step, d_taps, d_cbias, d_offset, d_rate, d_skip = pull_local(
        (d_zero, later_grad, decay_grad, d_c, d_exp)
    )
    edge_back = lax.ppermute(
        d_ext[: KC - 1], "ctx", [(i + 1, i) for i in range(count - 1)]
    )
    d_conv = d_ext[KC - 1 :]
    d_conv = jnp.concatenate(
        [d_conv[: rows - (KC - 1)], d_conv[rows - (KC - 1) :] + edge_back], axis=0
    )
    d_pre = jnp.concatenate(
        [d_q, d_k, d_v, d_gate_z.astype(bf16), d_conv.astype(bf16), d_step.astype(bf16)], axis=1
    )

    right_in = gather_rows(d_pre, seqs)
    d_normed = times_weight_t(d_pre, w_in, seqs, core)
    unused, pull_input = jax.vjp(rms_scale, x, gin)
    d_x, d_gin = pull_input(d_normed)
    grad_tokens = grad_res + d_x
    parts = (d_gin, d_gfeed, d_cbias, d_gmix, d_taps.reshape(-1), d_offset, d_rate, d_skip)
    sums = lax.psum(jnp.concatenate(parts), ("seq", "ctx"))
    out_small = []
    at = 0
    for part in parts:
        out_small.append(sums[at : at + part.size])
        at += part.size

    def own_share(vec):
        size = vec.shape[-1] // seqs
        return lax.dynamic_slice_in_dim(vec, place * size, size, vec.ndim - 1)

    grad_in = dot_tn(left_normed, right_in)
    sum_in = sum_over_ctx(grad_in, chips, chip, core).astype(f32)
    sum_gu = sum_gu.astype(f32)
    sum_do = sum_do.astype(f32)
    mixo = INNER // seqs
    return (
        layer_out,
        grad_tokens,
        own_share(out_small[0]),
        sum_in[:, :QW],
        sum_in[:, QW : QW + KW],
        sum_in[:, QW + KW : mix0],
        sum_in[:, mix0:],
        own_share(out_small[4].reshape(KC, CONVW)),
        own_share(out_small[2]),
        out_small[5],
        out_small[6],
        out_small[7],
        own_share(out_small[3]),
        sum_do[:mixo, width:],
        sum_do[mixo:, width:],
        own_share(out_small[1]),
        sum_gu[:, :ff],
        sum_gu[:, ff:],
        sum_do[:, :width],
    )


def solution(mesh):
    rows = P(("seq", "ctx"), None)
    vec = P("seq")
    mat = P("seq", None)
    col = P(None, "seq")
    rep = P()
    in_specs = (
        rows, rows, vec, mat, mat, mat, mat, col, vec, rep, rep, rep, vec, mat, mat, vec, mat, mat, mat,
    )
    out_specs = (
        rows, rows, vec, mat, mat, mat, mat, col, vec, rep, rep, rep, vec, mat, mat, vec, mat, mat, mat,
    )
    return jax.shard_map(body, mesh=mesh, in_specs=in_specs, out_specs=out_specs, check_vma=False)
```

```python
import functools

import jax
import jax.numpy as jnp
from jax import lax
from jax.experimental import pallas as pl
from jax.experimental.pallas import tpu as pltpu
from jax.sharding import PartitionSpec as P

QUERY_HEADS = 8
VALUE_HEADS = 2
HEAD_SIZE = 64
MH = 24
MP = 64
NS = 128
KC = 4
GROUP = QUERY_HEADS // VALUE_HEADS
INNER = MH * MP
CONVW = INNER + 2 * NS
QW = QUERY_HEADS * HEAD_SIZE
KW = VALUE_HEADS * HEAD_SIZE

norm_epsilon = 1e-06
rope_base = 100000000000.0
highest = lax.Precision.HIGHEST
f32 = jnp.float32
bf16 = jnp.bfloat16


def dot(a, b):
    return jnp.dot(a, b, preferred_element_type=f32)


def dot_nt(a, b):
    return lax.dot_general(a, b, (((1,), (1,)), ((), ())), preferred_element_type=f32)


def dot_tn(a, b):
    return lax.dot_general(a, b, (((0,), (0,)), ((), ())), preferred_element_type=f32)


def rms_scale(signal, gain_vec):
    return (
        signal
        * lax.rsqrt(jnp.mean(signal * signal, axis=-1, keepdims=True) + norm_epsilon)
        * gain_vec
    )


def rotary_apply(head_rows, cosine, sine):
    half_dim = head_rows.shape[-1] // 2
    lower = head_rows[..., :half_dim]
    upper = head_rows[..., half_dim:]
    return jnp.concatenate(
        [lower * cosine - upper * sine, upper * cosine + lower * sine], axis=-1
    )


def conv_mix(extended, taps, shift):
    rows = extended.shape[0] - KC + 1
    summed = shift[None, :]
    for tap in range(KC):
        summed = summed + taps[tap][None, :] * extended[tap : tap + rows]
    return jax.nn.silu(summed)


def swap_core(value):
    count = lax.axis_size("ctx")
    return lax.ppermute(value, "ctx", [(i, i ^ 1) for i in range(count)])


def chip_shift(value, steps, wrap):
    count = lax.axis_size("ctx")
    pairs = []
    for i in range(count):
        to = i + 2 * steps
        if wrap:
            pairs.append((i, to % count))
        elif 0 <= to < count:
            pairs.append((i, to))
    return lax.ppermute(value, "ctx", pairs)


def seq_swap(value, k):
    count = lax.axis_size("seq")
    return lax.ppermute(value, "seq", [(i, i ^ k) for i in range(count)])


def take_half(value, core):
    rows = value.shape[0] // 2
    return lax.dynamic_slice_in_dim(value, core * rows, rows, 0)


def gather_weight(local, core):
    own = lax.all_gather(take_half(local, core), "seq", axis=0, tiled=True)
    return own, swap_core(own)


def scatter_ctx(mine, others, chips, chip):
    rows, cols = mine.shape
    mine = mine + swap_core(others).astype(f32)
    shards = mine.reshape(chips, rows // chips, cols)
    total = lax.dynamic_index_in_dim(shards, chip, 0, False)
    for k in range(1, chips):
        piece = lax.dynamic_index_in_dim(shards, (chip + k) % chips, 0, False).astype(bf16)
        total = total + chip_shift(piece, k, True).astype(f32)
    return total.astype(bf16)


def spread_ctx(total, chips, chip, core):
    got = [total] + [chip_shift(total, k, True) for k in range(1, chips)]
    got = jnp.stack(got, axis=0)
    both = jnp.stack([got, swap_core(got)], axis=0)
    parts = []
    for half in range(2):
        for q in range(chips):
            parts.append(both[half ^ core, (chip - q) % chips])
    return jnp.concatenate(parts, axis=0)


def ctx_state(value, decays, chips, chip, core, later):
    half = MH // 2
    low = value.astype(bf16)
    mine = lax.dynamic_slice_in_dim(low, core * half, half, 0)
    others = lax.dynamic_slice_in_dim(low, (1 - core) * half, half, 0)
    got = swap_core(others).astype(f32)
    mine = mine.astype(f32)
    even = jnp.where(core == 0, mine, got)
    odd = jnp.where(core == 0, got, mine)
    dec = lax.dynamic_slice_in_dim(decays, core * half, half, 2)[..., None, None]
    if later:
        chip_value = even + dec[0, 0] * odd
    else:
        chip_value = odd + dec[0, 1] * even
    chip_low = chip_value.astype(bf16)
    sign = -1 if later else 1
    total = jnp.zeros_like(chip_value)
    for k in range(chips - 1, 0, -1):
        arrived = chip_shift(chip_low, sign * k, False).astype(f32)
        rel = (sign * k) % chips
        total = arrived + dec[rel, 0] * dec[rel, 1] * total
    if later:
        for_odd = total
        for_even = odd + dec[0, 1] * total
    else:
        for_even = total
        for_odd = even + dec[0, 0] * total
    keep = jnp.where(core == 0, for_even, for_odd).astype(bf16)
    give = jnp.where(core == 0, for_odd, for_even).astype(bf16)
    back = swap_core(give)
    first = jnp.where(core == 0, keep, back)
    second = jnp.where(core == 0, back, keep)
    return jnp.concatenate([first, second], axis=0).astype(f32)


def silu_parts(z):
    sig = 1.0 / (1.0 + jnp.exp(-z))
    return z * sig, sig * (1.0 + z * (1.0 - sig))


def three(a):
    hi = a.astype(bf16)
    rest = a - hi.astype(f32)
    mid = rest.astype(bf16)
    return hi, mid, (rest - mid.astype(f32)).astype(bf16)


def exact_dot(a, b):
    hi, mid, low = three(a)
    return dot(hi, b) + dot(mid, b) + dot(low, b)


def two(a):
    hi = a.astype(bf16)
    return hi, (a - hi.astype(f32)).astype(bf16)


def exact_dot_nt(a, b):
    hi, mid, low = three(a)
    return dot_nt(hi, b) + dot_nt(mid, b) + dot_nt(low, b)


def head_table():
    head = lax.broadcasted_iota(jnp.int32, (MH, INNER), 0)
    column = lax.broadcasted_iota(jnp.int32, (MH, INNER), 1)
    return (column // MP == head).astype(bf16)


def column_halves(ref, seqs, hr, is0):
    first = jnp.concatenate([ref[:, 2 * j * hr : (2 * j + 1) * hr] for j in range(seqs)], axis=1)
    second = jnp.concatenate(
        [ref[:, (2 * j + 1) * hr : (2 * j + 2) * hr] for j in range(seqs)], axis=1
    )
    return jnp.where(is0, first, second), jnp.where(is0, second, first)


def project_kernel(seqs, where_ref, own_ref, sib_ref, tok_ref, gin_ref, nor_ref, pre_ref):
    x = tok_ref[...].astype(f32)
    inv = lax.rsqrt(jnp.mean(x * x, axis=1, keepdims=True) + norm_epsilon)
    nor_ref[...] = (x * inv * gin_ref[...]).astype(bf16)
    hr = x.shape[1] // (2 * seqs)
    own, sib = column_halves(nor_ref, seqs, hr, where_ref[1] == 0)
    wide = own_ref.shape[1]
    part = 512

    def one(i, carry):
        a = pl.ds(pl.multiple_of(i * part, part), part)
        pre_ref[:, a] = dot(own, own_ref[:, a]) + dot(sib, sib_ref[:, a])
        return carry

    whole = wide // part
    lax.fori_loop(0, whole, one, 0)
    if wide % part:
        at = whole * part
        pre_ref[:, at:] = dot(own, own_ref[:, at:]) + dot(sib, sib_ref[:, at:])


def project(where, own, sib, tokens, gin, seqs):
    rows, width = tokens.shape
    wide = own.shape[1]
    vm = pl.BlockSpec(memory_space=pltpu.VMEM)
    return pl.pallas_call(
        functools.partial(project_kernel, seqs),
        out_shape=(
            jax.ShapeDtypeStruct((rows, width), bf16),
            jax.ShapeDtypeStruct((rows, wide), f32),
        ),
        in_specs=[pl.BlockSpec(memory_space=pltpu.SMEM)] + [vm] * 4,
        out_specs=[vm, vm],
        compiler_params=pltpu.CompilerParams(vmem_limit_bytes=48 * 2**20),
        cost_estimate=pl.CostEstimate(
            flops=4 * rows * own.size, bytes_accessed=own.size * 4 + 3 * 2**20, transcendentals=0
        ),
        name="project",
    )(where, own, sib, tokens, gin)


def unproject_kernel(
    seqs, where_ref, own_ref, sib_ref, tok_ref, gin_ref, gres_ref, back_ref, out_ref
):
    x = tok_ref[...].astype(f32)
    rows, width = x.shape
    hr = width // (2 * seqs)
    inv = lax.rsqrt(jnp.mean(x * x, axis=1, keepdims=True) + norm_epsilon)
    unit = x * inv
    is0 = where_ref[1] == 0
    wide = own_ref.shape[1]
    part = 512

    def one(i, carry):
        a = pl.ds(pl.multiple_of(i * part, part), part)
        grad = back_ref[:rows, a]
        return carry[0] + dot_nt(grad, own_ref[:, a]), carry[1] + dot_nt(grad, sib_ref[:, a])

    nothing = jnp.zeros((rows, width // 2), f32)
    whole = wide // part
    own, sib = lax.fori_loop(0, whole, one, (nothing, nothing))
    if wide % part:
        at = whole * part
        grad = back_ref[:rows, at:]
        own = own + dot_nt(grad, own_ref[:, at:])
        sib = sib + dot_nt(grad, sib_ref[:, at:])
    first = jnp.where(is0, own, sib)
    second = jnp.where(is0, sib, own)
    for j in range(seqs):
        out_ref[:, 2 * j * hr : (2 * j + 1) * hr] = first[:, j * hr : (j + 1) * hr]
        out_ref[:, (2 * j + 1) * hr : (2 * j + 2) * hr] = second[:, j * hr : (j + 1) * hr]
    d_norm = out_ref[...] * gin_ref[...]
    d_x = inv * (d_norm - unit * jnp.mean(d_norm * unit, axis=1, keepdims=True))
    out_ref[...] = gres_ref[...] + d_x


def unproject(where, own, sib, tokens, gin, grad_res, back, seqs):
    rows, width = tokens.shape
    vm = pl.BlockSpec(memory_space=pltpu.VMEM)
    return pl.pallas_call(
        functools.partial(unproject_kernel, seqs),
        out_shape=jax.ShapeDtypeStruct((rows, width), f32),
        in_specs=[pl.BlockSpec(memory_space=pltpu.SMEM)] + [vm] * 6,
        out_specs=vm,
        compiler_params=pltpu.CompilerParams(vmem_limit_bytes=48 * 2**20),
        cost_estimate=pl.CostEstimate(
            flops=4 * rows * own.size, bytes_accessed=own.size * 4 + 3 * 2**20, transcendentals=0
        ),
        name="unproject",
    )(where, own, sib, tokens, gin, grad_res, back)


def last_grads_kernel(seqs, where_ref, *refs):
    lefts, rights, keep_ref, give_ref = refs[:seqs], refs[seqs:-2], refs[-2], refs[-1]
    is0 = where_ref[1] == 0
    hr, wide = keep_ref.shape
    rows = lefts[0].shape[0]
    a = jnp.concatenate([m[:, :hr] for m in lefts], axis=0)
    b = jnp.concatenate([m[:, hr : 2 * hr] for m in lefts], axis=0)
    mine, other = jnp.where(is0, a, b), jnp.where(is0, b, a)
    part = 512

    def piece(src):
        right = jnp.concatenate([m[:rows, src] for m in rights], axis=0)
        keep_ref[:, src] = dot_tn(mine, right)
        give_ref[:, src] = dot_tn(other, right).astype(bf16)

    def one(i, carry):
        piece(pl.ds(pl.multiple_of(i * part, part), part))
        return carry

    lax.fori_loop(0, wide // part, one, 0)
    if wide % part:
        piece(slice(wide - wide % part, wide))


def last_grads(where, lefts, rights, hr, seqs):
    wide = rights[0].shape[1]
    vm = pl.BlockSpec(memory_space=pltpu.VMEM)
    part = pl.BlockSpec((lefts[0].shape[0], 2 * hr), lambda i: (0, 0))
    whole = pl.BlockSpec(rights[0].shape, lambda i: (0, 0))
    out = pl.BlockSpec((hr, wide), lambda i: (0, 0))
    return pl.pallas_call(
        functools.partial(last_grads_kernel, seqs),
        grid=(1,),
        out_shape=(jax.ShapeDtypeStruct((hr, wide), f32), jax.ShapeDtypeStruct((hr, wide), bf16)),
        in_specs=[pl.BlockSpec(memory_space=pltpu.SMEM)] + [part] * seqs + [whole] * seqs,
        out_specs=[out, out],
        compiler_params=pltpu.CompilerParams(vmem_limit_bytes=48 * 2**20),
        cost_estimate=pl.CostEstimate(
            flops=4 * seqs * rights[0].size * hr, bytes_accessed=2 * seqs * rights[0].size,
            transcendentals=0,
        ),
        name="last_grads",
    )(where, *lefts, *rights)


def middle_kernel(
    seqs, where_ref, own_ref, sib_ref, tok_ref, cot_ref, nor_ref, zero_ref, gz_ref, c_ref,
    ecum_ref, start_ref, att_ref, gmix_ref, gfeed_ref,
    lay_ref, msg_ref, gres_ref, datt_ref, dssm_ref, dgz_ref, dstart_ref, dc_ref, dcum_ref,
    ssm, outs, feeds, hids, gates, ups, dhid, dout, dgu,
):
    place, core = where_ref[0], where_ref[1]
    rows, width = tok_ref.shape
    ff = hids.shape[1]
    hr = width // (2 * seqs)
    mixw, attw = INNER // seqs, QW // seqs
    outw = mixw + attw
    base_out, base_dn = 2 * ff, 2 * ff + 2 * width
    is0 = core == 0

    def picked(ref, unit, b):
        firsts, seconds = [], []
        for j in range(seqs):
            at = j * 2 * unit * hr + b * hr
            firsts.append(ref[:, at : at + hr])
            seconds.append(ref[:, at + unit * hr : at + unit * hr + hr])
        first = jnp.concatenate(firsts, axis=1)
        second = jnp.concatenate(seconds, axis=1)
        return jnp.where(is0, first, second), jnp.where(is0, second, first)

    def put(ref, unit, b, own, sib):
        first = jnp.where(is0, own, sib)
        second = jnp.where(is0, sib, own)
        for j in range(seqs):
            at = j * 2 * unit * hr + b * hr
            ref[:, at : at + hr] = first[:, j * hr : (j + 1) * hr].astype(ref.dtype)
            at += unit * hr
            ref[:, at : at + hr] = second[:, j * hr : (j + 1) * hr].astype(ref.dtype)

    table = head_table()
    c_hi, c_lo = two(c_ref[...])
    ecum = exact_dot(ecum_ref[...], table)
    across = (dot_nt(c_hi, start_ref[...]) + dot_nt(c_lo, start_ref[...])) * ecum
    whole = zero_ref[...] + across
    silu_z, slope_z = silu_parts(gz_ref[...])
    gated = whole * silu_z
    inv_mix = lax.rsqrt(jnp.mean(gated * gated, axis=1, keepdims=True) + norm_epsilon)
    gmix = gmix_ref[...]
    ssm[...] = gated * inv_mix
    mix_b = (ssm[...] * gmix).astype(bf16)
    for j in range(seqs):
        outs[:, j * outw : j * outw + mixw] = mix_b[:, j * mixw : (j + 1) * mixw]
        outs[:, j * outw + mixw : (j + 1) * outw] = att_ref[:, j * attw : (j + 1) * attw]
    residual = tok_ref[...].astype(f32)
    for b in range(2):
        own, sib = picked(outs, 2, b)
        at = base_out + b * width
        residual = residual + dot(own, own_ref[:, at : at + width])
        residual = residual + dot(sib, sib_ref[:, at : at + width])
    inv_res = lax.rsqrt(jnp.mean(residual * residual, axis=1, keepdims=True) + norm_epsilon)
    unit_res = residual * inv_res
    gfeed = gfeed_ref[...]
    feeds[...] = (unit_res * gfeed).astype(bf16)
    feed_own, feed_sib = picked(feeds, 1, 0)
    part = 512

    def forward(i, carry):
        a = pl.ds(pl.multiple_of(i * part, part), part)
        u = pl.ds(pl.multiple_of(ff + i * part, part), part)
        gate = dot(feed_own, own_ref[:, a]) + dot(feed_sib, sib_ref[:, a])
        up = dot(feed_own, own_ref[:, u]) + dot(feed_sib, sib_ref[:, u])
        gates[:, a] = gate
        ups[:, a] = up
        hids[:, a] = (gate / (1.0 + jnp.exp(-gate)) * up).astype(bf16)
        return carry

    lax.fori_loop(0, ff // part, forward, 0)
    layer = residual
    cot = cot_ref[...]
    for b in range(2):
        own, sib = picked(hids, 2, b)
        at = base_dn + b * width
        layer = layer + dot(own, own_ref[:, at : at + width])
        layer = layer + dot(sib, sib_ref[:, at : at + width])
        put(
            dhid, 2, b,
            dot_nt(cot, own_ref[:, at : at + width]),
            dot_nt(cot, sib_ref[:, at : at + width]),
        )
    lay_ref[...] = layer.astype(bf16)

    def backward(i, carry):
        a = pl.ds(pl.multiple_of(i * part, part), part)
        u = pl.ds(pl.multiple_of(ff + i * part, part), part)
        silu_g, slope_g = silu_parts(gates[:, a])
        grad = dhid[:, a]
        d_gate = (grad * ups[:, a] * slope_g).astype(bf16)
        d_up = (grad * silu_g).astype(bf16)
        dgu[:, a] = d_gate
        dgu[:, u] = d_up
        own = dot_nt(d_gate, own_ref[:, a]) + dot_nt(d_up, own_ref[:, u])
        sib = dot_nt(d_gate, sib_ref[:, a]) + dot_nt(d_up, sib_ref[:, u])
        return carry[0] + own, carry[1] + sib

    nothing = jnp.zeros((rows, width // 2), f32)
    own, sib = lax.fori_loop(0, ff // part, backward, (nothing, nothing))
    put(gres_ref, 1, 0, own, sib)
    d_feed = gres_ref[...] * gfeed
    d_res = inv_res * (d_feed - unit_res * jnp.mean(d_feed * unit_res, axis=1, keepdims=True))
    grad_res = cot.astype(f32) + d_res
    gres_ref[...] = grad_res
    res_b = grad_res.astype(bf16)
    for b in range(2):
        at = base_out + b * width
        put(
            dout, 2, b,
            dot_nt(res_b, own_ref[:, at : at + width]),
            dot_nt(res_b, sib_ref[:, at : at + width]),
        )
    for j in range(seqs):
        datt_ref[:, j * attw : (j + 1) * attw] = dout[
            :, j * outw + mixw : (j + 1) * outw
        ].astype(bf16)
        dssm_ref[:, j * mixw : (j + 1) * mixw] = dout[:, j * outw : j * outw + mixw]
    for k in range(seqs):
        to = place ^ k
        at = 0
        for ref, size in ((nor_ref, 2 * hr), (feeds, 2 * hr), (outs, outw), (hids, ff // seqs)):
            msg_ref[k, :, at : at + size] = ref[:, pl.ds(pl.multiple_of(to * size, 128), size)]
            at += size
        msg_ref[k, :, at : at + 2 * ff] = dgu[...]
        msg_ref[k, :, at + 2 * ff : at + 2 * ff + width] = cot
        msg_ref[k, :, at + 2 * ff + width :] = res_b
    unit_mix = ssm[...]
    d_norm = dssm_ref[...] * gmix
    d_gated = inv_mix * (d_norm - unit_mix * jnp.mean(d_norm * unit_mix, axis=1, keepdims=True))
    dgz_ref[...] = (d_gated * whole * slope_z).astype(bf16)
    d_ssm = d_gated * silu_z
    dssm_ref[...] = d_ssm
    dcum_ref[...] = exact_dot_nt(d_ssm * across, table)
    da_hi, da_lo = two(d_ssm * ecum)
    dc_ref[...] = dot(da_hi, start_ref[...]) + dot(da_lo, start_ref[...])
    dstart_ref[...] = (dot_tn(da_hi, c_hi) + dot_tn(da_hi, c_lo) + dot_tn(da_lo, c_hi)).astype(
        bf16
    )


def middle(where, own, sib, tokens, cotangent, normed, out_zero, gate_z, c_state, ecum, start,
           attn_b, gmix, gfeed, seqs):
    rows, width = tokens.shape
    ff = own.shape[1] // 2 - 2 * width
    message = (2 * width + INNER + QW + ff) // seqs + 2 * ff + 2 * width
    out_shape = (
        jax.ShapeDtypeStruct((rows, width), bf16),
        jax.ShapeDtypeStruct((seqs, rows, message), bf16),
        jax.ShapeDtypeStruct((rows, width), f32),
        jax.ShapeDtypeStruct((rows, QW), bf16),
        jax.ShapeDtypeStruct((rows, INNER), f32),
        jax.ShapeDtypeStruct((rows, INNER), bf16),
        jax.ShapeDtypeStruct((INNER, NS), bf16),
        jax.ShapeDtypeStruct((rows, NS), f32),
        jax.ShapeDtypeStruct((rows, MH), f32),
    )
    vm = pl.BlockSpec(memory_space=pltpu.VMEM)
    scratch = [
        pltpu.VMEM((rows, INNER), f32),
        pltpu.VMEM((rows, INNER + QW), bf16),
        pltpu.VMEM((rows, width), bf16),
        pltpu.VMEM((rows, ff), bf16),
        pltpu.VMEM((rows, ff), f32),
        pltpu.VMEM((rows, ff), f32),
        pltpu.VMEM((rows, ff), f32),
        pltpu.VMEM((rows, INNER + QW), f32),
        pltpu.VMEM((rows, 2 * ff), bf16),
    ]
    return pl.pallas_call(
        functools.partial(middle_kernel, seqs),
        out_shape=out_shape,
        in_specs=[pl.BlockSpec(memory_space=pltpu.SMEM)] + [vm] * 13,
        out_specs=[vm] * len(out_shape),
        scratch_shapes=scratch,
        compiler_params=pltpu.CompilerParams(vmem_limit_bytes=56 * 2**20),
        cost_estimate=pl.CostEstimate(
            flops=4 * rows * own.size * 2, bytes_accessed=own.size * 4 + 16 * 2**20,
            transcendentals=rows * 8192,
        ),
        name="middle",
    )(where, own, sib, tokens, cotangent, normed, out_zero, gate_z, c_state, ecum, start,
      attn_b, gmix, gfeed)


def grads_kernel(seqs, ff, where_ref, *refs):
    msgs, keep_ref, give_ref = refs[:-2], refs[-2], refs[-1]
    is0 = where_ref[1] == 0
    hr = keep_ref.shape[0]
    width = 2 * hr * seqs
    outw = 4 * hr
    right = 2 * (2 * hr) + 2 * outw
    part = 512

    def left(at):
        return jnp.concatenate([m[:, at : at + hr] for m in msgs], axis=0)

    def segment(first, second, source, target, size):
        a, b = left(first), left(second)
        mine, other = jnp.where(is0, a, b), jnp.where(is0, b, a)

        def one(i, carry):
            src = pl.ds(pl.multiple_of(source + i * part, 128), part)
            dst = pl.ds(pl.multiple_of(target + i * part, 128), part)
            rows = jnp.concatenate([m[:, src] for m in msgs], axis=0)
            keep_ref[:, dst] = dot_tn(mine, rows)
            give_ref[:, dst] = dot_tn(other, rows).astype(bf16)
            return carry

        lax.fori_loop(0, size // part, one, 0)

    at_feed, at_out, at_hid = 2 * hr, 4 * hr, 4 * hr + outw
    segment(at_feed, at_feed + hr, right, 0, 2 * ff)
    for b in range(2):
        segment(
            at_out + b * hr, at_out + (b + 2) * hr, right + 2 * ff + width,
            2 * ff + b * width, width,
        )
        segment(
            at_hid + b * hr, at_hid + (b + 2) * hr, right + 2 * ff,
            2 * ff + (2 + b) * width, width,
        )


def grads(where, msgs, ff, seqs):
    hr = (msgs[0].shape[1] - 2 * ff) // (12 + 4 * seqs)
    columns = 2 * ff + 8 * hr * seqs
    vm = pl.BlockSpec(memory_space=pltpu.VMEM)
    return pl.pallas_call(
        functools.partial(grads_kernel, seqs, ff),
        out_shape=(
            jax.ShapeDtypeStruct((hr, columns), f32),
            jax.ShapeDtypeStruct((hr, columns), bf16),
        ),
        in_specs=[pl.BlockSpec(memory_space=pltpu.SMEM)] + [vm] * len(msgs),
        out_specs=[vm, vm],
        compiler_params=pltpu.CompilerParams(vmem_limit_bytes=56 * 2**20),
        cost_estimate=pl.CostEstimate(
            flops=4 * msgs[0].shape[0] * seqs * hr * columns,
            bytes_accessed=2 * seqs * msgs[0].size + 6 * hr * columns,
            transcendentals=0,
        ),
        name="grads",
    )(where, *msgs)


def body(
    tokens,
    cotangent,
    gain_input,
    w_query,
    key_weight,
    value_weight,
    w_mixin,
    conv_taps,
    conv_bias,
    step_offset,
    decay_rate,
    skip_gain,
    gain_mixer,
    w_mixout,
    w_attnout,
    gain_feed,
    w_gate,
    w_up,
    w_down,
):
    rows, width = tokens.shape
    seqs = lax.axis_size("seq")
    ctxs = lax.axis_size("ctx")
    chips = ctxs // 2
    place = lax.axis_index("seq")
    ctx = lax.axis_index("ctx")
    chip, core = ctx // 2, ctx % 2
    ff = w_gate.shape[1]

    sizes = (gain_input.size, gain_feed.size, conv_bias.size, gain_mixer.size, conv_taps.size)
    small = jnp.concatenate(
        [gain_input, gain_feed, conv_bias, gain_mixer, conv_taps.reshape(-1)]
    )
    small = lax.all_gather(small, "seq").astype(f32)
    at = 0
    pieces = []
    for size in sizes:
        pieces.append(small[:, at : at + size])
        at += size
    gin = pieces[0].reshape(-1)
    gfeed = pieces[1].reshape(-1)
    cbias = pieces[2].reshape(-1)
    gmix = pieces[3].reshape(-1)
    taps = pieces[4].reshape(seqs, KC, -1).transpose(1, 0, 2).reshape(KC, -1)

    used = QW + 2 * KW + w_mixin.shape[1]
    wide = -(-used // 128) * 128
    blank = jnp.zeros((w_mixin.shape[0], wide - used), bf16)
    in_loc = jnp.concatenate([w_query, key_weight, value_weight, w_mixin, blank], axis=1)
    w_in = gather_weight(in_loc, core)
    out_loc = jnp.concatenate([w_mixout, w_attnout], axis=0)
    half_out = take_half(out_loc, core)
    half_dn = take_half(w_down, core)
    hr = half_out.shape[0] // 2
    rest = jnp.concatenate(
        [
            take_half(w_gate, core),
            take_half(w_up, core),
            half_out[:hr],
            half_out[hr:],
            half_dn[:hr],
            half_dn[hr:],
        ],
        axis=1,
    )
    where = jnp.stack([place, core]).astype(jnp.int32)

    first_row = ctx * rows
    position = first_row + jnp.arange(rows, dtype=jnp.int32)
    frequency = rope_base ** (
        -(jnp.arange(HEAD_SIZE // 2, dtype=f32) * 2.0 / HEAD_SIZE)
    )
    angles = position.astype(f32)[:, None] * frequency[None, :]
    cosine = jnp.cos(angles)[:, None, :]
    sine = jnp.sin(angles)[:, None, :]

    x = tokens.astype(f32)
    rest, kept_in = lax.optimization_barrier((rest, w_in[0]))
    w_in = (kept_in, w_in[1])
    rest_own = lax.all_gather(rest, "seq", axis=0, tiled=True)
    normed, pre = project(where, w_in[0], w_in[1], tokens, gin[None, :], seqs)
    q_pre = pre[:, :QW].reshape(rows, QUERY_HEADS, HEAD_SIZE)
    k_pre = pre[:, QW : QW + KW].reshape(rows, VALUE_HEADS, HEAD_SIZE)
    v_low = pre[:, QW + KW : QW + 2 * KW].astype(bf16)
    mix0 = QW + 2 * KW
    gate_z = pre[:, mix0 : mix0 + INNER]
    conv_low = pre[:, mix0 + INNER : mix0 + INNER + CONVW].astype(bf16)
    raw_step = pre[:, mix0 + INNER + CONVW : used]

    queries = rotary_apply(q_pre, cosine, sine).astype(bf16)
    keys = rotary_apply(k_pre, cosine, sine).astype(bf16).reshape(rows, KW)

    step0 = jax.nn.softplus(raw_step + step_offset[None, :])
    decay = jnp.exp(jnp.sum(-step0 * decay_rate[None, :], axis=0))
    decay_hi = decay.astype(bf16)
    decay_lo = (decay - decay_hi.astype(f32)).astype(bf16)
    extra = jnp.zeros((16, 2 * KW), bf16)
    extra = extra.at[0, :MH].set(decay_hi).at[1, :MH].set(decay_lo)
    message = jnp.concatenate([jnp.concatenate([keys, v_low], axis=1), extra], axis=0)
    got = jnp.stack([message] + [chip_shift(message, k, True) for k in range(1, chips)])
    got_other = swap_core(got)
    kv_all = jnp.stack([got[:, :rows], got_other[:, :rows]])
    dec_own = got[:, rows, :MH].astype(f32) + got[:, rows + 1, :MH].astype(f32)
    dec_oth = got_other[:, rows, :MH].astype(f32) + got_other[:, rows + 1, :MH].astype(f32)
    decays = jnp.stack(
        [jnp.where(core == 0, dec_own, dec_oth), jnp.where(core == 0, dec_oth, dec_own)], axis=1
    )
    count = lax.axis_size("ctx")
    edge = lax.ppermute(
        conv_low[rows - (KC - 1) :], "ctx", [(i, i + 1) for i in range(count - 1)]
    )
    extended = jnp.concatenate([edge, conv_low], axis=0).astype(f32)

    causal = (
        jnp.arange(rows, dtype=jnp.int32)[:, None] >= jnp.arange(rows, dtype=jnp.int32)[None, :]
    )

    def ssm_local(extended_in, steps_in, taps_in, shift_in, offset_in, rates_in, skip_in):
        mixed = conv_mix(extended_in, taps_in, shift_in)
        head_input = mixed[:, :INNER].reshape(rows, MH, MP)
        b_state = mixed[:, INNER : INNER + NS]
        c_state = mixed[:, INNER + NS :]
        step = jax.nn.softplus(steps_in + offset_in[None, :])
        cum = jnp.cumsum(-step * rates_in[None, :], axis=0)
        gaps = cum.T[:, :, None] - cum.T[:, None, :]
        weights = jnp.where(causal[None], jnp.exp(jnp.where(causal[None], gaps, 0.0)), 0.0)
        inter = jnp.dot(c_state, b_state.T, precision=highest)
        mixing = weights * inter[None] * step.T[:, None, :]
        within = jnp.einsum("hts,shp->thp", mixing, head_input, precision=highest)
        out_zero = within + skip_in[None, :, None] * head_input
        tail = jnp.exp(cum[-1][None, :] - cum) * step
        local_state = jnp.einsum(
            "shp,sn->hpn", tail[:, :, None] * head_input, b_state, precision=highest
        )
        return out_zero, local_state, jnp.exp(cum[-1]), c_state, cum

    (out_zero, local_state, own_decay, c_state, cum), pull_local = jax.vjp(
        ssm_local, extended, raw_step, taps, cbias, step_offset, decay_rate, skip_gain
    )
    exp_cum = jnp.exp(cum)
    start_state = ctx_state(local_state, decays, chips, chip, core, False)

    qpos = jnp.tile(position, GROUP)
    query_rows = (
        queries.reshape(rows, VALUE_HEADS, GROUP, HEAD_SIZE)
        .transpose(1, 2, 0, 3)
        .reshape(VALUE_HEADS, GROUP * rows, HEAD_SIZE)
    )
    rel = jnp.arange(chips, dtype=jnp.int32)
    key_chip = chip - rel
    side = jnp.stack([core, 1 - core])
    key_pos = (
        (key_chip[None, :, None] * 2 + side[:, None, None]) * rows
        + jnp.arange(rows, dtype=jnp.int32)[None, None, :]
    )
    key_pos = jnp.where(key_chip[None, :, None] >= 0, key_pos, ctxs * rows).reshape(-1)
    total_keys = key_pos.shape[0]
    kv_flat = kv_all.reshape(total_keys, 2, VALUE_HEADS, HEAD_SIZE)
    key_heads = kv_flat[:, 0].transpose(1, 0, 2)
    value_heads = kv_flat[:, 1].transpose(1, 0, 2)
    allowed = key_pos[None, :] <= qpos[:, None]
    scale = HEAD_SIZE ** (-0.5)
    scores = jnp.einsum("hrd,hkd->hrk", query_rows, key_heads, preferred_element_type=f32) * scale
    masked = jnp.where(allowed[None], scores, -1e30)
    top = jnp.max(masked, axis=-1, keepdims=True)
    top, rest_own = lax.optimization_barrier((top, rest_own))
    rest_sib = swap_core(rest_own)
    expanded = jnp.exp(masked - top)
    prob = expanded / jnp.sum(expanded, axis=-1, keepdims=True)
    prob_low = prob.astype(bf16)
    attended = jnp.einsum("hrk,hkd->hrd", prob_low, value_heads, preferred_element_type=f32)
    attn_b = (
        attended.astype(bf16)
        .reshape(VALUE_HEADS, GROUP, rows, HEAD_SIZE)
        .transpose(2, 0, 1, 3)
        .reshape(rows, QW)
    )

    layer_out, msg, grad_res, d_att, d_ssm, d_gate_z, d_start, d_c, d_cum = middle(
        where, rest_own, rest_sib, tokens, cotangent, normed,
        out_zero.reshape(rows, INNER), gate_z, c_state, exp_cum,
        start_state.reshape(INNER, NS).astype(bf16), attn_b, gmix[None, :], gfeed[None, :], seqs,
    )
    msgs = [msg[0]] + [seq_swap(msg[k], k) for k in range(1, seqs)]
    keep, give = grads(where, msgs, ff, seqs)

    later_grad = ctx_state(d_start.reshape(MH, MP, NS), decays, chips, chip, core, True)
    decay_grad = jnp.sum(later_grad * start_state, axis=(1, 2))

    grad_rows = (
        d_att.reshape(rows, VALUE_HEADS, GROUP, HEAD_SIZE)
        .transpose(1, 2, 0, 3)
        .reshape(VALUE_HEADS, GROUP * rows, HEAD_SIZE)
    )
    d_prob = jnp.einsum("hrd,hkd->hrk", grad_rows, value_heads, preferred_element_type=f32)
    delta = jnp.sum(prob * d_prob, axis=-1, keepdims=True)
    d_score = (prob * (d_prob - delta)).astype(bf16)
    d_query_rows = (
        jnp.einsum("hrk,hkd->hrd", d_score, key_heads, preferred_element_type=f32) * scale
    )
    d_keys = jnp.einsum("hrk,hrd->khd", d_score, query_rows, preferred_element_type=f32) * scale
    d_values = jnp.einsum("hrk,hrd->khd", prob_low, grad_rows, preferred_element_type=f32)
    d_kv = jnp.concatenate(
        [d_keys.reshape(total_keys, KW), d_values.reshape(total_keys, KW)], axis=1
    ).reshape(2, chips, rows, 2 * KW)
    d_kv = d_kv[0] + swap_core(d_kv[1].astype(bf16)).astype(f32)
    d_kv_own = d_kv[0]
    for k in range(1, chips):
        d_kv_own = d_kv_own + chip_shift(d_kv[k].astype(bf16), -k, False).astype(f32)
    d_queries = (
        d_query_rows.reshape(VALUE_HEADS, GROUP, rows, HEAD_SIZE)
        .transpose(2, 0, 1, 3)
        .reshape(rows, QUERY_HEADS, HEAD_SIZE)
    )
    d_q = rotary_apply(d_queries, cosine, -sine).reshape(rows, QW).astype(bf16)
    d_k = (
        rotary_apply(d_kv_own[:, :KW].reshape(rows, VALUE_HEADS, HEAD_SIZE), cosine, -sine)
        .reshape(rows, KW)
        .astype(bf16)
    )
    d_v = d_kv_own[:, KW:].astype(bf16)

    d_ext, d_step, d_taps, d_cbias, d_offset, d_rate, d_skip = pull_local(
        (d_ssm.reshape(rows, MH, MP), later_grad, decay_grad, d_c, d_cum)
    )
    edge_back = lax.ppermute(
        d_ext[: KC - 1], "ctx", [(i + 1, i) for i in range(count - 1)]
    )
    d_conv = d_ext[KC - 1 :]
    d_conv = jnp.concatenate(
        [d_conv[: rows - (KC - 1)], d_conv[rows - (KC - 1) :] + edge_back], axis=0
    )
    d_pre = jnp.concatenate(
        [d_q, d_k, d_v, d_gate_z, d_conv.astype(bf16), d_step.astype(bf16), jnp.zeros((rows, wide - used), bf16)], axis=1
    )

    last = jnp.concatenate([d_cbias, d_offset, d_rate, d_skip])
    extra = jnp.stack(
        [
            jnp.pad(d_taps[:2].reshape(-1), (0, wide - 2 * CONVW)),
            jnp.pad(d_taps[2:].reshape(-1), (0, wide - 2 * CONVW)),
            jnp.pad(last, (0, wide - last.size)),
        ]
    )
    extra_hi = extra.astype(bf16)
    extra_lo = (extra - extra_hi.astype(f32)).astype(bf16)
    back_msg = jnp.concatenate([d_pre, extra_hi, extra_lo, jnp.zeros((10, wide), bf16)], axis=0)
    back_msg, keep, give = lax.optimization_barrier((back_msg, keep, give))
    total_rest = scatter_ctx(keep, give, chips, chip)
    backs = [back_msg] + [seq_swap(back_msg, k) for k in range(1, seqs)]

    grad_tokens = unproject(
        where, w_in[0], w_in[1], tokens, gin[None, :], grad_res, back_msg, seqs
    )

    smalls = [
        (m[rows : rows + 3].astype(f32) + m[rows + 3 : rows + 6].astype(f32)) for m in backs
    ]
    while len(smalls) > 1:
        smalls = [smalls[i] + smalls[i + 1] for i in range(0, len(smalls), 2)]
    small_sum = smalls[0]
    small_taps = small_sum[:2, : 2 * CONVW].reshape(KC, CONVW)

    def own_share(vec):
        size = vec.shape[-1] // seqs
        return lax.dynamic_slice_in_dim(vec, place * size, size, vec.ndim - 1)

    flat = jnp.concatenate(
        [
            own_share(small_taps).reshape(-1),
            own_share(small_sum[2, :CONVW]),
            small_sum[2, CONVW : CONVW + 3 * MH],
        ]
    )
    step = 1
    while step < ctxs:
        flat = flat + lax.ppermute(flat, "ctx", [(i, i ^ step) for i in range(ctxs)])
        step *= 2
    own_conv = CONVW // seqs
    out_taps = flat[: KC * own_conv].reshape(KC, own_conv)
    out_cbias = flat[KC * own_conv : (KC + 1) * own_conv]
    heads = flat[(KC + 1) * own_conv :]

    backs[0], total_rest = lax.optimization_barrier((backs[0], total_rest))
    keep_in, give_in = last_grads(where, msgs, backs, hr, seqs)
    total_in = scatter_ctx(keep_in, give_in, chips, chip)
    sum_rest = spread_ctx(total_rest, chips, chip, core)
    sum_in = spread_ctx(total_in, chips, chip, core).astype(f32)
    sum_rest = sum_rest.astype(f32)
    sum_gate, sum_up = sum_rest[:, :ff], sum_rest[:, ff : 2 * ff]

    def unfold(first, second):
        first = first.reshape(2, hr, width)
        second = second.reshape(2, hr, width)
        return jnp.stack([first, second], axis=1).reshape(4 * hr, width)

    at = 2 * ff
    sum_out = unfold(sum_rest[:, at : at + width], sum_rest[:, at + width : at + 2 * width])
    at += 2 * width
    sum_dn = unfold(sum_rest[:, at : at + width], sum_rest[:, at + width : at + 2 * width])
    mixo = INNER // seqs
    grad_gin = jnp.sum(sum_in * in_loc.astype(f32), axis=1) / gain_input.astype(f32)
    grad_gfeed = (
        jnp.sum(sum_gate * w_gate.astype(f32), axis=1)
        + jnp.sum(sum_up * w_up.astype(f32), axis=1)
    ) / gain_feed.astype(f32)
    grad_gmix = jnp.sum(sum_out[:mixo] * w_mixout.astype(f32), axis=1) / gain_mixer.astype(f32)
    return (
        layer_out,
        grad_tokens,
        grad_gin,
        sum_in[:, :QW],
        sum_in[:, QW : QW + KW],
        sum_in[:, QW + KW : mix0],
        sum_in[:, mix0:used],
        out_taps,
        out_cbias,
        heads[:MH],
        heads[MH : 2 * MH],
        heads[2 * MH :],
        grad_gmix,
        sum_out[:mixo],
        sum_out[mixo:],
        grad_gfeed,
        sum_gate,
        sum_up,
        sum_dn,
    )


def solution(mesh):
    rows = P(("seq", "ctx"), None)
    vec = P("seq")
    mat = P("seq", None)
    col = P(None, "seq")
    rep = P()
    in_specs = (
        rows, rows, vec, mat, mat, mat, mat, col, vec, rep, rep, rep, vec, mat, mat, vec, mat, mat, mat,
    )
    out_specs = (
        rows, rows, vec, mat, mat, mat, mat, col, vec, rep, rep, rep, vec, mat, mat, vec, mat, mat, mat,
    )
    return jax.shard_map(body, mesh=mesh, in_specs=in_specs, out_specs=out_specs, check_vma=False)
```

```python
import functools

import jax
import jax.numpy as jnp
from jax import lax
from jax.experimental import pallas as pl
from jax.experimental.pallas import tpu as pltpu
from jax.sharding import PartitionSpec as P

QUERY_HEADS = 8
VALUE_HEADS = 2
HEAD_SIZE = 64
MH = 24
MP = 64
NS = 128
KC = 4
GROUP = QUERY_HEADS // VALUE_HEADS
INNER = MH * MP
CONVW = INNER + 2 * NS
QW = QUERY_HEADS * HEAD_SIZE
KW = VALUE_HEADS * HEAD_SIZE

norm_epsilon = 1e-06
rope_base = 100000000000.0
f32 = jnp.float32
bf16 = jnp.bfloat16


def dot(a, b):
    return jnp.dot(a, b, preferred_element_type=f32)


def dot_nt(a, b):
    return lax.dot_general(a, b, (((1,), (1,)), ((), ())), preferred_element_type=f32)


def dot_tn(a, b):
    return lax.dot_general(a, b, (((0,), (0,)), ((), ())), preferred_element_type=f32)


def swap_core(value):
    count = lax.axis_size("ctx")
    return lax.ppermute(value, "ctx", [(i, i ^ 1) for i in range(count)])


def chip_shift(value, steps, wrap):
    count = lax.axis_size("ctx")
    pairs = []
    for i in range(count):
        to = i + 2 * steps
        if wrap:
            pairs.append((i, to % count))
        elif 0 <= to < count:
            pairs.append((i, to))
    return lax.ppermute(value, "ctx", pairs)


def seq_swap(value, k):
    count = lax.axis_size("seq")
    return lax.ppermute(value, "seq", [(i, i ^ k) for i in range(count)])


def take_half(value, core):
    rows = value.shape[0] // 2
    return lax.dynamic_slice_in_dim(value, core * rows, rows, 0)


def first_phase(value):
    seqs = lax.axis_size("seq")
    return [seq_swap(value, k) for k in (range(1, seqs) if seqs != 4 else (1, 2))]


def second_phase(near, cut):
    if len(near) != 2:
        return [(k + 1, 0, piece) for k, piece in enumerate(near)]
    far_a = seq_swap(near[0][:cut], 2)
    far_b = seq_swap(near[1][cut:], 1)
    return [(1, 0, near[0]), (2, 0, near[1]), (3, 0, far_a), (3, cut, far_b)]


def gather_pieces(value, cut):
    return second_phase(first_phase(value), cut)


def both_cores(pieces):
    out = []
    for k, row, array in pieces:
        out.append((k, 0, row, array))
        out.append((k, 1, row, swap_core(array)))
    return out


def chip_swap(value, bit):
    count = lax.axis_size("ctx")
    return lax.ppermute(value, "ctx", [(i, i ^ (2 * bit)) for i in range(count)])


def sum_halves(mine, arrived, chips, chip, small):
    rows = mine.shape[0]

    def widened(message, rows):
        return message[rows : rows + 8].astype(f32) + message[rows + 8 : rows + 16].astype(f32)

    def narrowed(values):
        hi, low = two(values)
        return jnp.concatenate([hi, low], axis=0)

    if small is not None:
        tail = narrowed(small)
        small = widened(tail, 0) + widened(arrived, rows)
        arrived = arrived[:rows]
    total = mine + arrived.astype(f32)
    bit = 1
    while bit < chips:
        rows //= 2
        side = jnp.where((chip & bit) != 0, 1, 0)
        give = lax.dynamic_slice_in_dim(total, (1 - side) * rows, rows, 0).astype(bf16)
        if small is not None:
            tail = narrowed(small)
            give = jnp.concatenate([give, tail], axis=0)
        arrived = chip_swap(give, bit)
        if small is not None:
            small = widened(tail, 0) + widened(arrived, rows)
            arrived = arrived[:rows]
        total = lax.dynamic_slice_in_dim(total, side * rows, rows, 0) + arrived.astype(f32)
        bit *= 2
    return total.astype(bf16), small


def spread_halves(total, chips, chip):
    bit = chips // 2
    while bit >= 1:
        other = chip_swap(total, bit)
        upper = (chip & bit) != 0
        total = jnp.concatenate(
            [jnp.where(upper, other, total), jnp.where(upper, total, other)], axis=0
        )
        bit //= 2
    return total


def ctx_state(low, decays, chips, core, later):
    half = INNER // 2
    mine = lax.dynamic_slice_in_dim(low, core * half, half, 0).astype(f32)
    others = lax.dynamic_slice_in_dim(low, (1 - core) * half, half, 0)
    got = swap_core(others).astype(f32)
    even = jnp.where(core == 0, mine, got)
    odd = jnp.where(core == 0, got, mine)
    dec = lax.dynamic_slice_in_dim(decays, core * (MH // 2), MH // 2, 2)
    dec = jnp.repeat(dec, MP, axis=2)[..., None]
    if later:
        chip_value = even + dec[0, 0] * odd
    else:
        chip_value = odd + dec[0, 1] * even
    chip_low = chip_value.astype(bf16)
    sign = -1 if later else 1
    total = jnp.zeros_like(chip_value)
    for k in range(chips - 1, 0, -1):
        arrived = chip_shift(chip_low, sign * k, False).astype(f32)
        rel = (sign * k) % chips
        total = arrived + dec[rel, 0] * dec[rel, 1] * total
    if later:
        for_odd = total
        for_even = odd + dec[0, 1] * total
    else:
        for_even = total
        for_odd = even + dec[0, 0] * total
    keep = jnp.where(core == 0, for_even, for_odd).astype(bf16)
    give = jnp.where(core == 0, for_odd, for_even).astype(bf16)
    back = swap_core(give)
    first = jnp.where(core == 0, keep, back)
    second = jnp.where(core == 0, back, keep)
    return jnp.concatenate([first, second], axis=0)


def silu_parts(z):
    sig = 1.0 / (1.0 + jnp.exp(-z))
    return z * sig, sig * (1.0 + z * (1.0 - sig))


def three(a):
    hi = a.astype(bf16)
    rest = a - hi.astype(f32)
    mid = rest.astype(bf16)
    return hi, mid, (rest - mid.astype(f32)).astype(bf16)


def exact_dot(a, b):
    hi, mid, low = three(a)
    return dot(hi, b) + dot(mid, b) + dot(low, b)


def two(a):
    hi = a.astype(bf16)
    return hi, (a - hi.astype(f32)).astype(bf16)


def exact_dot_nt(a, b):
    hi, mid, low = three(a)
    return dot_nt(hi, b) + dot_nt(mid, b) + dot_nt(low, b)


def head_table():
    head = lax.broadcasted_iota(jnp.int32, (128, INNER), 0)
    column = lax.broadcasted_iota(jnp.int32, (128, INNER), 1)
    return (column // MP == head).astype(bf16)


def placed(place, core, pieces, hr):
    return [
        ((place ^ k) * 2 * hr + jnp.where(core == side, 0, hr) + row) for k, side, row in pieces
    ]


def run_copies(copies):
    for copy in copies:
        copy.start()


def wait_copies(copies):
    for copy in copies:
        copy.wait()


def in_copies(pieces, where_ref, local_ref, refs, weight, sems):
    place, core = where_ref[0], where_ref[1]
    hr = local_ref.shape[0] // 2
    copies = [
        pltpu.make_async_copy(
            local_ref,
            weight.at[pl.ds(pl.multiple_of(place * 2 * hr, 16), 2 * hr), :],
            sems.at[0],
        )
    ]
    for i, (at, ref) in enumerate(zip(placed(place, core, pieces, hr), refs)):
        copies.append(
            pltpu.make_async_copy(
                ref,
                weight.at[pl.ds(pl.multiple_of(at, 16), ref.shape[0]), :],
                sems.at[i + 1],
            )
        )
    return copies


def project_kernel(pieces, where_ref, tok_ref, gin_ref, cos_ref, sin_ref, off_ref, rate_ref,
                   local_ref, *refs):
    count = len(pieces)
    parts, outs = refs[:count], refs[count:]
    nor_ref, q_ref, kv_ref, gz_ref, conv_ref, raw_ref, pre, weight, sems = outs
    copies = in_copies(pieces, where_ref, local_ref, parts, weight, sems)
    run_copies(copies)
    x = tok_ref[...].astype(f32)
    rows = x.shape[0]
    inv = lax.rsqrt(jnp.mean(x * x, axis=1, keepdims=True) + norm_epsilon)
    nor_ref[...] = (x * inv * gin_ref[...]).astype(bf16)
    wide = weight.shape[1]
    part = 384
    wait_copies(copies)

    def one(i, carry):
        a = pl.ds(pl.multiple_of(i * part, 128), part)
        pre[:, a] = dot(nor_ref[...], weight[:, a])
        return carry

    lax.fori_loop(0, wide // part, one, 0)
    for at in range(0, QW, 128):
        u = pre[:, at : at + 128]
        q_ref[:, at : at + 128] = (u * cos_ref[...] + half_turned(u) * sin_ref[...]).astype(bf16)
    u = pre[:, QW : QW + KW]
    kv_ref[:rows, :KW] = (u * cos_ref[...] + half_turned(u) * sin_ref[...]).astype(bf16)
    kv_ref[:rows, KW:] = pre[:, QW + KW : QW + 2 * KW].astype(bf16)
    at = QW + 2 * KW
    gz_ref[...] = pre[:, at : at + INNER]
    at += INNER
    conv_ref[...] = pre[:, at : at + CONVW].astype(bf16)
    at += CONVW
    raw = pre[:, at:]
    raw_ref[...] = raw
    unused, unused, cum, unused = heads_of(raw, off_ref[...], rate_ref[...])
    decay = jnp.exp(cum[rows - 1 : rows, :])
    hi, low = two(decay)
    row = lax.broadcasted_iota(jnp.int32, (16, 128), 0)
    both = jnp.where(row == 0, hi.astype(f32), jnp.where(row == 1, low.astype(f32), 0.0))
    kv_ref[rows:, :KW] = both.astype(bf16)
    kv_ref[rows:, KW:] = jnp.zeros((16, KW), bf16)


def project(where, tokens, gin, cosine, sine, offset, rates, local, pieces):
    rows, width = tokens.shape
    wide = local.shape[1]
    vm = pl.BlockSpec(memory_space=pltpu.VMEM)
    hbm = pl.BlockSpec(memory_space=pl.ANY)
    return pl.pallas_call(
        functools.partial(project_kernel, [p[:3] for p in pieces]),
        out_shape=(
            jax.ShapeDtypeStruct((rows, width), bf16),
            jax.ShapeDtypeStruct((rows, QW), bf16),
            jax.ShapeDtypeStruct((rows + 16, 2 * KW), bf16),
            jax.ShapeDtypeStruct((rows, INNER), f32),
            jax.ShapeDtypeStruct((rows, CONVW), bf16),
            jax.ShapeDtypeStruct((rows, 128), f32),
        ),
        in_specs=[pl.BlockSpec(memory_space=pltpu.SMEM)] + [vm] * 6 + [hbm] * (1 + len(pieces)),
        out_specs=[vm] * 6,
        scratch_shapes=[
            pltpu.VMEM((rows, wide), f32),
            pltpu.VMEM((width, wide), bf16),
            pltpu.SemaphoreType.DMA((1 + len(pieces),)),
        ],
        compiler_params=pltpu.CompilerParams(vmem_limit_bytes=40 * 2**20),
        cost_estimate=pl.CostEstimate(
            flops=2 * rows * width * wide, bytes_accessed=2 * width * wide + 3 * 2**20,
            transcendentals=0,
        ),
        name="project",
    )(where, tokens, gin, cosine, sine, offset, rates, local, *[p[3] for p in pieces])


def unproject_kernel(pieces, where_ref, tok_ref, gin_ref, gres_ref, back_ref, local_ref, *refs):
    parts, (out_ref, weight, sems) = refs[:-3], refs[-3:]
    copies = in_copies(pieces, where_ref, local_ref, parts, weight, sems)
    run_copies(copies)
    x = tok_ref[...].astype(f32)
    rows, width = x.shape
    inv = lax.rsqrt(jnp.mean(x * x, axis=1, keepdims=True) + norm_epsilon)
    unit = x * inv
    wide = weight.shape[1]
    part = 384
    out_ref[...] = jnp.zeros_like(out_ref)
    wait_copies(copies)

    def one(i, carry):
        a = pl.ds(pl.multiple_of(i * part, 128), part)
        out_ref[...] += dot_nt(back_ref[:rows, a], weight[:, a])
        return carry

    lax.fori_loop(0, wide // part, one, 0)
    d_norm = out_ref[...] * gin_ref[...]
    d_x = inv * (d_norm - unit * jnp.mean(d_norm * unit, axis=1, keepdims=True))
    out_ref[...] = gres_ref[...] + d_x


def unproject(where, tokens, gin, grad_res, back, local, pieces):
    rows, width = tokens.shape
    wide = local.shape[1]
    vm = pl.BlockSpec(memory_space=pltpu.VMEM)
    hbm = pl.BlockSpec(memory_space=pl.ANY)
    return pl.pallas_call(
        functools.partial(unproject_kernel, [p[:3] for p in pieces]),
        out_shape=jax.ShapeDtypeStruct((rows, width), f32),
        in_specs=[pl.BlockSpec(memory_space=pltpu.SMEM)] + [vm] * 4 + [hbm] * (1 + len(pieces)),
        out_specs=vm,
        scratch_shapes=[
            pltpu.VMEM((width, wide), bf16),
            pltpu.SemaphoreType.DMA((1 + len(pieces),)),
        ],
        compiler_params=pltpu.CompilerParams(vmem_limit_bytes=40 * 2**20),
        cost_estimate=pl.CostEstimate(
            flops=2 * rows * width * wide, bytes_accessed=2 * width * wide + 3 * 2**20,
            transcendentals=0,
        ),
        name="unproject",
    )(where, tokens, gin, grad_res, back, local, *[p[3] for p in pieces])


def last_grads_kernel(seqs, cut, where_ref, *refs):
    lefts, rights = refs[:seqs], refs[seqs:-3]
    keep_ref, give_ref, small_ref = refs[-3:]
    is0 = where_ref[1] == 0
    hr, wide = keep_ref.shape
    rows = lefts[0].shape[0]
    a = jnp.concatenate([m[:, :hr] for m in lefts], axis=0)
    b = jnp.concatenate([m[:, hr : 2 * hr] for m in lefts], axis=0)
    mine, other = jnp.where(is0, a, b), jnp.where(is0, b, a)
    part = 384
    if cut:
        spans = [rows] * (seqs - 1) + [cut, rows - cut]
        ends = list(range(seqs - 1)) + [seqs]
        starts = [rows] * (seqs - 1) + [rows - cut]
    else:
        spans, ends, starts = [rows] * seqs, list(range(seqs)), [rows] * seqs
    extras = [
        rights[i][at : at + 8, :].astype(f32) + rights[i][at + 8 : at + 16, :].astype(f32)
        for i, at in zip(ends, starts)
    ]
    while len(extras) > 1:
        extras = [extras[i] + extras[i + 1] for i in range(0, len(extras), 2)]
    small_ref[...] = extras[0]
    hi, low = two(extras[0])
    give_ref[hr:, :] = jnp.concatenate([hi.astype(f32), low.astype(f32)], axis=0).astype(bf16)

    def one(i, carry):
        src = pl.ds(pl.multiple_of(i * part, 128), part)
        right = jnp.concatenate([m[:n, src] for m, n in zip(rights, spans)], axis=0)
        keep_ref[:, src] = dot_tn(mine, right)
        give_ref[:hr, src] = dot_tn(other, right).astype(bf16)
        return carry

    lax.fori_loop(0, wide // part, one, 0)


def last_grads(where, lefts, rights, hr, cut):
    wide = rights[0].shape[1]
    seqs = len(lefts)
    vm = pl.BlockSpec(memory_space=pltpu.VMEM)
    return pl.pallas_call(
        functools.partial(last_grads_kernel, seqs, cut if len(rights) > seqs else 0),
        out_shape=(
            jax.ShapeDtypeStruct((hr, wide), f32),
            jax.ShapeDtypeStruct((hr + 16, wide), bf16),
            jax.ShapeDtypeStruct((8, wide), f32),
        ),
        in_specs=[pl.BlockSpec(memory_space=pltpu.SMEM)] + [vm] * (len(lefts) + len(rights)),
        out_specs=[vm, vm, vm],
        compiler_params=pltpu.CompilerParams(vmem_limit_bytes=40 * 2**20),
        cost_estimate=pl.CostEstimate(
            flops=4 * seqs * rights[0].size * hr, bytes_accessed=2 * seqs * rights[0].size,
            transcendentals=0,
        ),
        name="last_grads",
    )(where, *lefts, *rights)


def middle_kernel(
    seqs, pieces, where_ref, tok_ref, cot_ref, nor_ref, zero_ref, gz_ref, c_ref,
    ecum_ref, start_ref, att_ref, gmix_ref, gfeed_ref,
    gate_ref, up_ref, mix_ref, attw_ref, down_ref, *refs,
):
    count = len(pieces)
    parts = refs[:count]
    (
        lay_ref, msg1_ref, msg2_ref, dgu_ref, gres_ref, datt_ref, dssm_ref, dgz_ref, dstart_ref,
        dc_ref, dcum_ref,
        ssm, outs, feeds, hids, gates, ups, dhid, dout, w_gu, w_out, w_dn, sems,
    ) = refs[count:]
    place, core = where_ref[0], where_ref[1]
    rows, width = tok_ref.shape
    ff = hids.shape[1]
    hr = width // (2 * seqs)
    mixw, attw = INNER // seqs, QW // seqs
    outw = mixw + attw
    base_out, base_dn = 2 * ff, 2 * ff + 2 * width

    def at_rows(ref, row, size):
        return ref.at[pl.ds(pl.multiple_of(row, 16), size), :]

    starts = placed(place, core, pieces, hr)
    copies = {"out": [], "gu": [], "dn": []}

    def add(group, source, target):
        number = sum(len(c) for c in copies.values())
        copies[group].append(pltpu.make_async_copy(source, target, sems.at[number]))

    add("out", mix_ref, at_rows(w_out, place * 4 * hr, mixw))
    add("out", attw_ref, at_rows(w_out, place * 4 * hr + mixw, attw))

    def blocks(group, base, target):
        for (k, side, row), ref in zip(pieces, parts):
            for b in range(2):
                at = (place ^ k) * 4 * hr + jnp.where(core == side, 0, 2 * hr) + b * hr + row
                add(
                    group, ref.at[:, base + b * width : base + (b + 1) * width],
                    at_rows(target, at, ref.shape[0]),
                )

    blocks("out", base_out, w_out)
    own_rows = pl.ds(pl.multiple_of(place * 2 * hr, 16), 2 * hr)
    add("gu", gate_ref, w_gu.at[own_rows, :ff])
    add("gu", up_ref, w_gu.at[own_rows, ff:])
    for at, ref in zip(starts, parts):
        add("gu", ref.at[:, : 2 * ff], at_rows(w_gu, at, ref.shape[0]))
    add("dn", down_ref, at_rows(w_dn, place * 4 * hr, 4 * hr))
    blocks("dn", base_dn, w_dn)
    for group in ("out", "gu", "dn"):
        run_copies(copies[group])

    table = head_table()
    c_hi, c_lo = two(c_ref[...])
    ecum = exact_dot(ecum_ref[...], table)
    across = (dot_nt(c_hi, start_ref[...]) + dot_nt(c_lo, start_ref[...])) * ecum
    whole = zero_ref[...] + across
    silu_z, slope_z = silu_parts(gz_ref[...])
    gated = whole * silu_z
    inv_mix = lax.rsqrt(jnp.mean(gated * gated, axis=1, keepdims=True) + norm_epsilon)
    gmix = gmix_ref[...]
    ssm[...] = gated * inv_mix
    mix_b = (ssm[...] * gmix).astype(bf16)
    for j in range(seqs):
        outs[:, j * outw : j * outw + mixw] = mix_b[:, j * mixw : (j + 1) * mixw]
        outs[:, j * outw + mixw : (j + 1) * outw] = att_ref[:, j * attw : (j + 1) * attw]
    part = 512
    wait_copies(copies["out"])

    def attach(i, carry):
        a = pl.ds(pl.multiple_of(i * part, part), part)
        gres_ref[:, a] = tok_ref[:, a].astype(f32) + dot(outs[...], w_out[:, a])
        return carry

    lax.fori_loop(0, width // part, attach, 0)
    residual = gres_ref[...]
    inv_res = lax.rsqrt(jnp.mean(residual * residual, axis=1, keepdims=True) + norm_epsilon)
    gfeed = gfeed_ref[...]
    feeds[...] = (residual * inv_res * gfeed).astype(bf16)
    wait_copies(copies["gu"])

    def forward(i, carry):
        a = pl.ds(pl.multiple_of(i * part, part), part)
        u = pl.ds(pl.multiple_of(ff + i * part, part), part)
        gate = dot(feeds[...], w_gu[:, a])
        up = dot(feeds[...], w_gu[:, u])
        gates[:, a] = gate
        ups[:, a] = up
        hids[:, a] = (gate / (1.0 + jnp.exp(-gate)) * up).astype(bf16)
        return carry

    lax.fori_loop(0, ff // part, forward, 0)
    cot = cot_ref[...]
    wait_copies(copies["dn"])

    def finish(i, carry):
        a = pl.ds(pl.multiple_of(i * part, part), part)
        lay_ref[:, a] = (gres_ref[:, a] + dot(hids[...], w_dn[:, a])).astype(bf16)
        return carry

    lax.fori_loop(0, width // part, finish, 0)

    def through(i, carry):
        a = pl.ds(pl.multiple_of(i * part, part), part)
        dhid[:, a] = dot_nt(cot, w_dn[a, :])
        return carry

    lax.fori_loop(0, ff // part, through, 0)
    dout[:, :width] = jnp.zeros((rows, width), f32)

    def backward(i, carry):
        a = pl.ds(pl.multiple_of(i * part, part), part)
        u = pl.ds(pl.multiple_of(ff + i * part, part), part)
        silu_g, slope_g = silu_parts(gates[:, a])
        grad = dhid[:, a]
        d_gate = (grad * ups[:, a] * slope_g).astype(bf16)
        d_up = (grad * silu_g).astype(bf16)
        dgu_ref[:, a] = d_gate
        dgu_ref[:, u] = d_up
        dout[:, :width] += dot_nt(d_gate, w_gu[:, a]) + dot_nt(d_up, w_gu[:, u])
        return carry

    lax.fori_loop(0, ff // part, backward, 0)
    unit_res = gres_ref[...] * inv_res
    d_feed = dout[:, :width] * gfeed
    d_res = inv_res * (d_feed - unit_res * jnp.mean(d_feed * unit_res, axis=1, keepdims=True))
    grad_res = cot.astype(f32) + d_res
    gres_ref[...] = grad_res
    res_b = grad_res.astype(bf16)

    def leave(i, carry):
        a = pl.ds(pl.multiple_of(i * part, part), part)
        dout[:, a] = dot_nt(res_b, w_out[a, :])
        return carry

    lax.fori_loop(0, (INNER + QW) // part, leave, 0)
    for j in range(seqs):
        datt_ref[:, j * attw : (j + 1) * attw] = dout[
            :, j * outw + mixw : (j + 1) * outw
        ].astype(bf16)
        dssm_ref[:, j * mixw : (j + 1) * mixw] = dout[:, j * outw : j * outw + mixw]
    for k in range(seqs):
        to = place ^ k
        for ref, sources in (
            (msg1_ref, ((outs, outw), (hids, ff // seqs))),
            (msg2_ref, ((nor_ref, 2 * hr), (feeds, 2 * hr))),
        ):
            at = 0
            for source, size in sources:
                ref[k, :, at : at + size] = source[:, pl.ds(pl.multiple_of(to * size, 128), size)]
                at += size
        msg1_ref[k, :, outw + ff // seqs :] = res_b
    unit_mix = ssm[...]
    d_norm = dssm_ref[...] * gmix
    d_gated = inv_mix * (d_norm - unit_mix * jnp.mean(d_norm * unit_mix, axis=1, keepdims=True))
    dgz_ref[...] = (d_gated * whole * slope_z).astype(bf16)
    d_ssm = d_gated * silu_z
    dssm_ref[...] = d_ssm
    dcum_ref[...] = exact_dot_nt(d_ssm * across, table)
    da_hi, da_lo = two(d_ssm * ecum)
    dc_ref[...] = dot(da_hi, start_ref[...]) + dot(da_lo, start_ref[...])
    dstart_ref[...] = (dot_tn(da_hi, c_hi) + dot_tn(da_hi, c_lo) + dot_tn(da_lo, c_hi)).astype(
        bf16
    )


def middle(where, tokens, cotangent, normed, out_zero, gate_z, c_state, ecum, start,
           attn_b, gmix, gfeed, locals_, pieces, seqs):
    rows, width = tokens.shape
    ff = locals_[0].shape[1]
    outw = INNER + QW
    out_shape = (
        jax.ShapeDtypeStruct((rows, width), bf16),
        jax.ShapeDtypeStruct((seqs, rows, (outw + ff) // seqs + width), bf16),
        jax.ShapeDtypeStruct((seqs, rows, 2 * width // seqs), bf16),
        jax.ShapeDtypeStruct((rows, 2 * ff), bf16),
        jax.ShapeDtypeStruct((rows, width), f32),
        jax.ShapeDtypeStruct((rows, QW), bf16),
        jax.ShapeDtypeStruct((rows, INNER), f32),
        jax.ShapeDtypeStruct((rows, INNER), bf16),
        jax.ShapeDtypeStruct((INNER, NS), bf16),
        jax.ShapeDtypeStruct((rows, NS), f32),
        jax.ShapeDtypeStruct((rows, 128), f32),
    )
    vm = pl.BlockSpec(memory_space=pltpu.VMEM)
    hbm = pl.BlockSpec(memory_space=pl.ANY)
    scratch = [
        pltpu.VMEM((rows, INNER), f32),
        pltpu.VMEM((rows, outw), bf16),
        pltpu.VMEM((rows, width), bf16),
        pltpu.VMEM((rows, ff), bf16),
        pltpu.VMEM((rows, ff), f32),
        pltpu.VMEM((rows, ff), f32),
        pltpu.VMEM((rows, ff), f32),
        pltpu.VMEM((rows, outw), f32),
        pltpu.VMEM((width, 2 * ff), bf16),
        pltpu.VMEM((outw, width), bf16),
        pltpu.VMEM((ff, width), bf16),
        pltpu.SemaphoreType.DMA((5 + 5 * len(pieces),)),
    ]
    weights = width * 2 * ff + (outw + ff) * width
    return pl.pallas_call(
        functools.partial(middle_kernel, seqs, [p[:3] for p in pieces]),
        out_shape=out_shape,
        in_specs=[pl.BlockSpec(memory_space=pltpu.SMEM)] + [vm] * 11
        + [hbm] * (5 + len(pieces)),
        out_specs=[vm] * len(out_shape),
        scratch_shapes=scratch,
        compiler_params=pltpu.CompilerParams(vmem_limit_bytes=52 * 2**20),
        cost_estimate=pl.CostEstimate(
            flops=4 * rows * weights, bytes_accessed=2 * weights + 8 * 2**20,
            transcendentals=rows * 8192,
        ),
        name="middle",
    )(where, tokens, cotangent, normed, out_zero, gate_z, c_state, ecum, start,
      attn_b, gmix, gfeed, *locals_, *[p[3] for p in pieces])


def segment(is0, a, b, rights, span, target, keep_ref, give_ref):
    mine, other = jnp.where(is0, a, b), jnp.where(is0, b, a)
    part = 512

    def one(i, carry):
        src = pl.ds(pl.multiple_of(span[0] + i * part, 128), part)
        dst = pl.ds(pl.multiple_of(target + i * part, 128), part)
        rows = jnp.concatenate([m[:, src] for m in rights], axis=0)
        keep_ref[:, dst] = dot_tn(mine, rows)
        give_ref[:, dst] = dot_tn(other, rows).astype(bf16)
        return carry

    lax.fori_loop(0, span[1] // part, one, 0)


def grads_kernel(seqs, where_ref, *refs):
    msgs, cots, keep_ref, give_ref = refs[:seqs], refs[seqs:-2], refs[-2], refs[-1]
    is0 = where_ref[1] == 0
    hr = keep_ref.shape[0]
    width = 2 * hr * seqs
    at_res = msgs[0].shape[1] - width

    def left(at):
        return jnp.concatenate([m[:, at : at + hr] for m in msgs], axis=0)

    for b in range(2):
        segment(
            is0, left(b * hr), left((b + 2) * hr), msgs, (at_res, width), b * width,
            keep_ref, give_ref,
        )
        at = 4 * hr + b * hr
        segment(
            is0, left(at), left(at + 2 * hr), cots, (0, width), (2 + b) * width,
            keep_ref, give_ref,
        )


def feed_grads_kernel(seqs, where_ref, *refs):
    msgs, rights, keep_ref, give_ref = refs[:seqs], refs[seqs:-2], refs[-2], refs[-1]
    is0 = where_ref[1] == 0
    hr, columns = keep_ref.shape

    def left(at):
        return jnp.concatenate([m[:, at : at + hr] for m in msgs], axis=0)

    segment(is0, left(2 * hr), left(3 * hr), rights, (0, columns), 0, keep_ref, give_ref)


def grads(kernel, name, where, lefts, rights, hr, columns):
    vm = pl.BlockSpec(memory_space=pltpu.VMEM)
    seqs = len(lefts)
    return pl.pallas_call(
        functools.partial(kernel, seqs),
        out_shape=(
            jax.ShapeDtypeStruct((hr, columns), f32),
            jax.ShapeDtypeStruct((hr, columns), bf16),
        ),
        in_specs=[pl.BlockSpec(memory_space=pltpu.SMEM)] + [vm] * (len(lefts) + len(rights)),
        out_specs=[vm, vm],
        compiler_params=pltpu.CompilerParams(vmem_limit_bytes=40 * 2**20),
        cost_estimate=pl.CostEstimate(
            flops=4 * lefts[0].shape[0] * seqs * hr * columns,
            bytes_accessed=2 * seqs * (lefts[0].size + rights[0].size) + 6 * hr * columns,
            transcendentals=0,
        ),
        name=name,
    )(where, *lefts, *rights)


def halves_in_order(is0, mine_ref, other_ref, cols):
    mine, other = mine_ref[:, cols].astype(f32), other_ref[:, cols].astype(f32)
    return jnp.where(is0, mine, other), jnp.where(is0, other, mine)


def last_in_kernel(where_ref, mine_ref, other_ref, weight_ref, gain_ref,
                   q_ref, k_ref, v_ref, mix_ref, gin_ref):
    is0 = where_ref[1] == 0
    hr = mine_ref.shape[0]
    total = [jnp.zeros((hr, 1), f32), jnp.zeros((hr, 1), f32)]
    at = 0
    for ref in (q_ref, k_ref, v_ref, mix_ref):
        size = ref.shape[1]
        for start in range(0, size, 512):
            step = min(512, size - start)
            cols = slice(at + start, at + start + step)
            for i, grad in enumerate(halves_in_order(is0, mine_ref, other_ref, cols)):
                here = slice(i * hr, (i + 1) * hr)
                ref[here, start : start + step] = grad
                total[i] = total[i] + jnp.sum(
                    grad * weight_ref[here, cols].astype(f32), axis=1, keepdims=True
                )
        at += size
    for i in range(2):
        here = slice(i * hr, (i + 1) * hr)
        gin_ref[here, :] = total[i] / gain_ref[here, :].astype(f32)


def last_in(where, mine, other, weight, gain, mixed):
    vm = pl.BlockSpec(memory_space=pltpu.VMEM)
    rows = 2 * mine.shape[0]
    sizes = (QW, KW, KW, mixed, 1)
    return pl.pallas_call(
        last_in_kernel,
        out_shape=tuple(jax.ShapeDtypeStruct((rows, size), f32) for size in sizes),
        in_specs=[pl.BlockSpec(memory_space=pltpu.SMEM)] + [vm] * 4,
        out_specs=[vm] * 5,
        compiler_params=pltpu.CompilerParams(vmem_limit_bytes=40 * 2**20),
        name="last_in",
    )(where, mine, other, weight, gain)


def last_feed_kernel(where_ref, mine_ref, other_ref, gate_ref, up_ref, gain_ref,
                     out_gate_ref, out_up_ref, gfeed_ref):
    is0 = where_ref[1] == 0
    hr = mine_ref.shape[0]
    ff = gate_ref.shape[1]
    total = [jnp.zeros((hr, 1), f32), jnp.zeros((hr, 1), f32)]
    for base, weight_ref, out_ref in ((0, gate_ref, out_gate_ref), (ff, up_ref, out_up_ref)):
        for start in range(0, ff, 512):
            cols = slice(base + start, base + start + 512)
            to = slice(start, start + 512)
            for i, grad in enumerate(halves_in_order(is0, mine_ref, other_ref, cols)):
                here = slice(i * hr, (i + 1) * hr)
                out_ref[here, to] = grad
                total[i] = total[i] + jnp.sum(
                    grad * weight_ref[here, to].astype(f32), axis=1, keepdims=True
                )
    for i in range(2):
        here = slice(i * hr, (i + 1) * hr)
        gfeed_ref[here, :] = total[i] / gain_ref[here, :].astype(f32)


def last_feed(where, mine, other, gate, up, gain):
    vm = pl.BlockSpec(memory_space=pltpu.VMEM)
    rows, ff = gate.shape
    return pl.pallas_call(
        last_feed_kernel,
        out_shape=tuple(jax.ShapeDtypeStruct((rows, size), f32) for size in (ff, ff, 1)),
        in_specs=[pl.BlockSpec(memory_space=pltpu.SMEM)] + [vm] * 5,
        out_specs=[vm] * 3,
        compiler_params=pltpu.CompilerParams(vmem_limit_bytes=40 * 2**20),
        name="last_feed",
    )(where, mine, other, gate, up, gain)


def last_out_kernel(where_ref, mine_ref, other_ref, weight_ref, gain_ref,
                    mix_ref, att_ref, down_ref, gmix_ref):
    is0 = where_ref[1] == 0
    hr = mine_ref.shape[0]
    width = mix_ref.shape[1]
    mixw = mix_ref.shape[0]
    for b in range(2):
        cols = slice(b * width, (b + 1) * width)
        for i, grad in enumerate(halves_in_order(is0, mine_ref, other_ref, cols)):
            at = i * 2 * hr + b * hr
            end = at + hr
            inside = min(end, mixw) - at
            if inside > 0:
                here = slice(at, at + inside)
                own = grad[:inside]
                mix_ref[here, :] = own
                total = jnp.sum(own * weight_ref[here, :].astype(f32), axis=1, keepdims=True)
                gmix_ref[here, :] = total / gain_ref[here, :].astype(f32)
            if inside < hr:
                begin = max(inside, 0)
                att_ref[at + begin - mixw : end - mixw, :] = grad[begin:]
        cols = slice((2 + b) * width, (3 + b) * width)
        for i, grad in enumerate(halves_in_order(is0, mine_ref, other_ref, cols)):
            at = i * 2 * hr + b * hr
            down_ref[at : at + hr, :] = grad


def last_out(where, mine, other, weight, gain, attw):
    vm = pl.BlockSpec(memory_space=pltpu.VMEM)
    mixw, width = weight.shape
    shapes = ((mixw, width), (attw, width), (mixw + attw, width), (mixw, 1))
    return pl.pallas_call(
        last_out_kernel,
        out_shape=tuple(jax.ShapeDtypeStruct(shape, f32) for shape in shapes),
        in_specs=[pl.BlockSpec(memory_space=pltpu.SMEM)] + [vm] * 4,
        out_specs=[vm] * 4,
        compiler_params=pltpu.CompilerParams(vmem_limit_bytes=40 * 2**20),
        name="last_out",
    )(where, mine, other, weight, gain)


def heads_of(raw, offset, rates):
    z = raw + offset
    step = jnp.maximum(z, 0.0) + jnp.log(1.0 + jnp.exp(-jnp.abs(z)))
    hi, mid, low = three(-step * rates)
    shape = (raw.shape[0], raw.shape[0])
    causal = lax.broadcasted_iota(jnp.int32, shape, 0) >= lax.broadcasted_iota(
        jnp.int32, shape, 1
    )
    tril = causal.astype(bf16)
    cum = dot(tril, hi) + dot(tril, mid) + dot(tril, low)
    return z, step, cum, causal


def dot3(kind, a, b):
    a_hi, a_lo = two(a)
    b_hi, b_lo = two(b)
    return kind(a_hi, b_hi) + kind(a_hi, b_lo) + kind(a_lo, b_hi)


def lane_halves(shape):
    return lax.broadcasted_iota(jnp.int32, shape, 1) < MP


def conv_sums(ext, taps_ref, bias_ref, act_ref, rows):
    part = 256
    for at in range(0, CONVW, part):
        cols = slice(at, at + part)
        total = bias_ref[:, cols]
        for tap in range(KC):
            start = 16 - (KC - 1) + tap
            total = total + taps_ref[tap : tap + 1, cols] * ext[start : start + rows, cols]
        act_ref[:, cols] = total


def ssm_kernel(
    conv_ref, edge_ref, raw_ref, taps_ref, bias_ref, off_ref, rate_ref, skip_ref,
    act_ref, zero_ref, state_ref, c_ref, ecum_ref, ext,
):
    rows = conv_ref.shape[0]
    ext[0:16, :] = edge_ref[...].astype(f32)
    ext[16:, :] = conv_ref[...].astype(f32)
    conv_sums(ext, taps_ref, bias_ref, act_ref, rows)
    unused, step, cum, causal = heads_of(raw_ref[...], off_ref[...], rate_ref[...])
    cum_t, step_t = jnp.transpose(cum), jnp.transpose(step)
    table = head_table()
    b_state = silu_parts(act_ref[:, INNER : INNER + NS])[0]
    c_state = silu_parts(act_ref[:, INNER + NS :])[0]
    c_ref[...] = c_state
    ecum_ref[...] = jnp.exp(cum)
    inter = dot3(dot_nt, c_state, b_state)
    last = cum[rows - 1 : rows, :]
    tail = exact_dot(jnp.exp(last - cum) * step, table)
    low_lane = lane_halves((rows, 2 * MP))
    b_hi, b_lo = two(b_state)
    for pair in range(MH // 2):
        cols = slice(pair * 2 * MP, (pair + 1) * 2 * MP)
        x = silu_parts(act_ref[:, cols])[0]
        mixes = []
        for h in (2 * pair, 2 * pair + 1):
            gaps = jnp.where(causal, cum[:, h : h + 1] - cum_t[h : h + 1, :], -1e30)
            mixes.append((jnp.exp(gaps) * inter * step_t[h : h + 1, :]).astype(bf16))
        low = x.astype(bf16)
        none = jnp.zeros_like(low)
        stacked = jnp.concatenate(
            [jnp.where(low_lane, low, none), jnp.where(low_lane, none, low)], axis=0
        )
        within = dot(jnp.concatenate(mixes, axis=1), stacked)
        zero_ref[:, cols] = within + skip_ref[:, cols] * x
        t_hi, t_lo = two(tail[:, cols] * x)
        state = dot_tn(t_hi, b_hi) + dot_tn(t_hi, b_lo) + dot_tn(t_lo, b_hi)
        state_ref[cols, :] = state.astype(bf16)


def ssm_forward(conv_low, edge, raw, taps, bias, offset, rates, skip_wide):
    rows = conv_low.shape[0]
    vm = pl.BlockSpec(memory_space=pltpu.VMEM)
    return pl.pallas_call(
        ssm_kernel,
        out_shape=(
            jax.ShapeDtypeStruct((rows, CONVW), f32),
            jax.ShapeDtypeStruct((rows, INNER), f32),
            jax.ShapeDtypeStruct((INNER, NS), bf16),
            jax.ShapeDtypeStruct((rows, NS), f32),
            jax.ShapeDtypeStruct((rows, 128), f32),
        ),
        in_specs=[vm] * 8,
        out_specs=[vm] * 5,
        scratch_shapes=[pltpu.VMEM((rows + 16, CONVW), f32)],
        compiler_params=pltpu.CompilerParams(vmem_limit_bytes=32 * 2**20),
        cost_estimate=pl.CostEstimate(
            flops=2 * MH * rows * rows * 512, bytes_accessed=6 * 2**20, transcendentals=10**6
        ),
        name="ssm_forward",
    )(conv_low, edge, raw, taps, bias, offset, rates, skip_wide)


def ssm_back_kernel(
    conv_ref, edge_ref, raw_ref, taps_ref, off_ref, rate_ref, skip_ref, act_ref,
    dssm_ref, dc_in_ref, dcum_ref, later_ref, start_ref,
    dconv_ref, dedge_ref, draw_ref, extra_ref, ext, dact, rowg, colq, rows_out,
):
    rows = conv_ref.shape[0]
    ext[0:16, :] = edge_ref[...].astype(f32)
    ext[16:, :] = conv_ref[...].astype(f32)
    z, step, cum, causal = heads_of(raw_ref[...], off_ref[...], rate_ref[...])
    cum_t, step_t = jnp.transpose(cum), jnp.transpose(step)
    table = head_table()
    b_state, b_slope = silu_parts(act_ref[:, INNER : INNER + NS])
    c_state, c_slope = silu_parts(act_ref[:, INNER + NS :])
    inter = dot3(dot_nt, c_state, b_state)
    last = cum[rows - 1 : rows, :]
    reach = jnp.exp(last - cum)
    tail = exact_dot(reach * step, table)
    low_lane = lane_halves((rows, 2 * MP))
    b_hi, b_lo = two(b_state)
    dact[0:8, :] = jnp.zeros((8, CONVW), f32)
    dact[rows + 8 :, :] = jnp.zeros((8, CONVW), f32)
    rowg[...] = jnp.zeros_like(rowg)
    colq[...] = jnp.zeros_like(colq)
    d_inter = jnp.zeros((rows, rows), f32)
    d_b = jnp.zeros((rows, NS), f32)
    d_tail = jnp.zeros((rows, 128), f32)
    d_decay = jnp.zeros((8, 128), f32)
    d_skip = jnp.zeros((8, 128), f32)
    ones = jnp.ones((8, NS), bf16)
    for pair in range(MH // 2):
        cols = slice(pair * 2 * MP, (pair + 1) * 2 * MP)
        x, slope = silu_parts(act_ref[:, cols])
        dy = dssm_ref[:, cols]
        x_low, dy_low = x.astype(bf16), dy.astype(bf16)
        none = jnp.zeros_like(dy_low)
        stacked = jnp.concatenate(
            [jnp.where(low_lane, dy_low, none), jnp.where(low_lane, none, dy_low)], axis=0
        )
        d_mix = dot_nt(stacked, x_low)
        mixes = []
        for i, h in enumerate((2 * pair, 2 * pair + 1)):
            gaps = jnp.where(causal, cum[:, h : h + 1] - cum_t[h : h + 1, :], -1e30)
            weight = jnp.exp(gaps)
            step_row = step_t[h : h + 1, :]
            dm_w = d_mix[i * rows : (i + 1) * rows, :] * weight
            q = dm_w * inter
            d_inter = d_inter + dm_w * step_row
            colq[h : h + 1, :] = jnp.sum(q, axis=0, keepdims=True)
            rowg[:, h : h + 1] = jnp.sum(q * step_row, axis=1, keepdims=True)
            mixes.append((weight * inter * step_row).astype(bf16))
        dx = dot_tn(jnp.concatenate(mixes, axis=0), stacked)
        later = later_ref[cols, :]
        from_state = dot_nt(b_hi, later) + dot_nt(b_lo, later)
        tail_part = tail[:, cols]
        dx = dx + skip_ref[:, cols] * dy + tail_part * from_state
        dact[8 : rows + 8, cols] = dx * slope
        part_table = table[:, cols]
        d_tail = d_tail + exact_dot_nt(x * from_state, part_table)
        t_hi, t_lo = two(tail_part * x)
        d_b = d_b + dot(t_hi, later) + dot(t_lo, later)
        held = later.astype(f32) * start_ref[cols, :].astype(f32)
        hi, mid, low = three(held)
        sums = dot_nt(ones, hi) + dot_nt(ones, mid) + dot_nt(ones, low)
        d_decay = d_decay + exact_dot_nt(sums, part_table)
        skips = jnp.broadcast_to(jnp.sum(dy * x, axis=0, keepdims=True), (8, 2 * MP))
        d_skip = d_skip + exact_dot_nt(skips, part_table)
    d_b = d_b + dot3(dot_tn, d_inter, c_state)
    d_c = dc_in_ref[...] + dot3(dot, d_inter, b_state)
    dact[8 : rows + 8, INNER : INNER + NS] = d_b * b_slope
    dact[8 : rows + 8, INNER + NS :] = d_c * c_slope
    col = jnp.transpose(colq[...])
    moved = d_tail * reach
    fade = moved * step
    d_cum = dcum_ref[...] + rowg[...] - col * step - fade
    at_last = jnp.sum(fade, axis=0, keepdims=True) + d_decay[0:1, :] * jnp.exp(last)
    is_last = lax.broadcasted_iota(jnp.int32, (rows, 128), 0) == rows - 1
    d_cum = d_cum + jnp.where(is_last, at_last, 0.0)
    shape = (rows, rows)
    triu = (
        lax.broadcasted_iota(jnp.int32, shape, 0) <= lax.broadcasted_iota(jnp.int32, shape, 1)
    ).astype(bf16)
    hi, mid, low = three(d_cum)
    d_log = dot(triu, hi) + dot(triu, mid) + dot(triu, low)
    d_step = col + moved - rate_ref[...] * d_log
    d_raw = d_step / (1.0 + jnp.exp(-z))
    draw_ref[...] = d_raw
    rows_out[...] = jnp.zeros_like(rows_out)
    rows_out[2:3, CONVW : CONVW + 128] = jnp.sum(d_raw, axis=0, keepdims=True)
    rows_out[2:3, CONVW + 128 : CONVW + 256] = jnp.sum(-step * d_log, axis=0, keepdims=True)
    rows_out[2:3, CONVW + 256 : CONVW + 384] = d_skip[0:1, :]
    part = 256
    for at in range(0, CONVW, part):
        cols = slice(at, at + part)
        own = dact[8 : rows + 8, cols]
        total = jnp.zeros((rows, part), f32)
        edge = jnp.zeros((8, part), f32)
        for tap in range(KC):
            weight = taps_ref[tap : tap + 1, cols]
            start = 8 + KC - 1 - tap
            total = total + weight * dact[start : start + rows, cols]
            edge = edge + weight * dact[8 - tap : 16 - tap, cols]
            seen = ext[16 - (KC - 1) + tap : 16 - (KC - 1) + tap + rows, cols]
            to = (tap % 2) * CONVW + at
            rows_out[tap // 2 : tap // 2 + 1, to : to + part] = jnp.sum(
                own * seen, axis=0, keepdims=True
            )
        rows_out[2:3, cols] = jnp.sum(own, axis=0, keepdims=True)
        dconv_ref[:, cols] = total
        dedge_ref[:, cols] = edge
    hi, low = two(rows_out[...])
    extra_ref[...] = jnp.concatenate([hi.astype(f32), low.astype(f32)], axis=0).astype(bf16)


def ssm_backward(conv_low, edge, raw, taps, offset, rates, skip_wide, act,
                 d_ssm, d_c, d_cum, later, start, wide):
    rows = conv_low.shape[0]
    vm = pl.BlockSpec(memory_space=pltpu.VMEM)
    return pl.pallas_call(
        ssm_back_kernel,
        out_shape=(
            jax.ShapeDtypeStruct((rows, CONVW), f32),
            jax.ShapeDtypeStruct((8, CONVW), f32),
            jax.ShapeDtypeStruct((rows, 128), f32),
            jax.ShapeDtypeStruct((16, wide), bf16),
        ),
        in_specs=[vm] * 13,
        out_specs=[vm] * 4,
        scratch_shapes=[
            pltpu.VMEM((rows + 16, CONVW), f32),
            pltpu.VMEM((rows + 16, CONVW), f32),
            pltpu.VMEM((rows, 128), f32),
            pltpu.VMEM((128, rows), f32),
            pltpu.VMEM((8, wide), f32),
        ],
        compiler_params=pltpu.CompilerParams(vmem_limit_bytes=32 * 2**20),
        cost_estimate=pl.CostEstimate(
            flops=2 * MH * rows * rows * 1024, bytes_accessed=8 * 2**20, transcendentals=10**6
        ),
        name="ssm_backward",
    )(conv_low, edge, raw, taps, offset, rates, skip_wide, act,
      d_ssm, d_c, d_cum, later, start)


def allowed_keys(place_ref, rows, chips):
    core, chip = place_ref[1], place_ref[2]
    total = 2 * chips * rows
    key = lax.broadcasted_iota(jnp.int32, (rows, total), 1)
    query = (chip * 2 + core) * rows + lax.broadcasted_iota(jnp.int32, (rows, total), 0)
    block = key // rows
    side = block // chips
    key_chip = chip - block % chips
    parity = jnp.where(side == 0, core, 1 - core)
    position = (key_chip * 2 + parity) * rows + key % rows
    return (key_chip >= 0) & (position <= query)


def key_block(own_ref, sib_ref, rows, at):
    chips = own_ref.shape[0]
    parts = [own_ref[k, :rows, at : at + HEAD_SIZE] for k in range(chips)]
    parts += [sib_ref[k, :rows, at : at + HEAD_SIZE] for k in range(chips)]
    return jnp.concatenate(parts, axis=0)


def attend_kernel(place_ref, q_ref, own_ref, sib_ref, out_ref, top_ref, sum_ref):
    rows = q_ref.shape[0]
    allowed = allowed_keys(place_ref, rows, own_ref.shape[0])
    scale = HEAD_SIZE ** (-0.5)
    top_ref[...] = jnp.zeros_like(top_ref)
    sum_ref[...] = jnp.zeros_like(sum_ref)
    for g in range(VALUE_HEADS):
        keys = key_block(own_ref, sib_ref, rows, g * HEAD_SIZE)
        values = key_block(own_ref, sib_ref, rows, KW + g * HEAD_SIZE)
        for i in range(GROUP):
            h = g * GROUP + i
            cols = slice(h * HEAD_SIZE, (h + 1) * HEAD_SIZE)
            scores = dot_nt(q_ref[:, cols], keys) * scale
            scores = jnp.where(allowed, scores, -1e30)
            top = jnp.max(scores, axis=1, keepdims=True)
            raised = jnp.exp(scores - top)
            total = jnp.sum(raised, axis=1, keepdims=True)
            prob = (raised * (1.0 / total)).astype(bf16)
            out_ref[:, cols] = dot(prob, values).astype(bf16)
            top_ref[:, h : h + 1] = top
            sum_ref[:, h : h + 1] = 1.0 / total


def attend(where, queries, kv_own, kv_sib):
    rows = queries.shape[0]
    vm = pl.BlockSpec(memory_space=pltpu.VMEM)
    keys = 2 * kv_own.shape[0] * rows
    return pl.pallas_call(
        attend_kernel,
        out_shape=(
            jax.ShapeDtypeStruct((rows, QW), bf16),
            jax.ShapeDtypeStruct((rows, 128), f32),
            jax.ShapeDtypeStruct((rows, 128), f32),
        ),
        in_specs=[pl.BlockSpec(memory_space=pltpu.SMEM)] + [vm] * 3,
        out_specs=[vm] * 3,
        compiler_params=pltpu.CompilerParams(vmem_limit_bytes=48 * 2**20),
        cost_estimate=pl.CostEstimate(
            flops=4 * rows * keys * QW, bytes_accessed=4 * kv_own.size,
            transcendentals=rows * keys * QUERY_HEADS,
        ),
        name="attend",
    )(where, queries, kv_own, kv_sib)


def half_turned(x):
    lane = lax.broadcasted_iota(jnp.int32, x.shape, 1)
    first = lane % HEAD_SIZE < HEAD_SIZE // 2
    return jnp.where(
        first, pltpu.roll(x, 128 - HEAD_SIZE // 2, 1), pltpu.roll(x, HEAD_SIZE // 2, 1)
    )


def attend_back_kernel(
    place_ref, q_ref, own_ref, sib_ref, top_ref, sum_ref, dout_ref, cos_ref, sin_ref,
    dq_ref, down_ref, dsib_ref, dq_s,
):
    rows = q_ref.shape[0]
    chips = own_ref.shape[0]
    allowed = allowed_keys(place_ref, rows, chips)
    scale = HEAD_SIZE ** (-0.5)
    for g in range(VALUE_HEADS):
        keys = key_block(own_ref, sib_ref, rows, g * HEAD_SIZE)
        values = key_block(own_ref, sib_ref, rows, KW + g * HEAD_SIZE)
        d_keys = jnp.zeros(keys.shape, f32)
        d_values = jnp.zeros(keys.shape, f32)
        for i in range(GROUP):
            h = g * GROUP + i
            cols = slice(h * HEAD_SIZE, (h + 1) * HEAD_SIZE)
            q = q_ref[:, cols]
            d_out = dout_ref[:, cols]
            scores = dot_nt(q, keys) * scale
            scores = jnp.where(allowed, scores, -1e30)
            prob = jnp.exp(scores - top_ref[:, h : h + 1]) * sum_ref[:, h : h + 1]
            d_prob = dot_nt(d_out, values)
            delta = jnp.sum(prob * d_prob, axis=1, keepdims=True)
            d_score = (prob * (d_prob - delta)).astype(bf16)
            dq_s[:, cols] = dot(d_score, keys) * scale
            d_keys = d_keys + dot_tn(d_score, q)
            d_values = d_values + dot_tn(prob.astype(bf16), d_out)
        d_keys = d_keys * scale
        for k in range(chips):
            at = k * rows
            cols = slice(g * HEAD_SIZE, (g + 1) * HEAD_SIZE)
            more = slice(KW + g * HEAD_SIZE, KW + (g + 1) * HEAD_SIZE)
            down_ref[k, :, cols] = d_keys[at : at + rows]
            down_ref[k, :, more] = d_values[at : at + rows]
            at += chips * rows
            dsib_ref[k, :, cols] = d_keys[at : at + rows].astype(bf16)
            dsib_ref[k, :, more] = d_values[at : at + rows].astype(bf16)
    for at in range(0, QW, 128):
        x = dq_s[:, at : at + 128]
        turned = x * cos_ref[...] - half_turned(x) * sin_ref[...]
        dq_ref[:, at : at + 128] = turned.astype(bf16)


def attend_back(where, queries, kv_own, kv_sib, top, total, d_att, cosine, sine):
    rows = queries.shape[0]
    chips = kv_own.shape[0]
    vm = pl.BlockSpec(memory_space=pltpu.VMEM)
    keys = 2 * chips * rows
    return pl.pallas_call(
        attend_back_kernel,
        out_shape=(
            jax.ShapeDtypeStruct((rows, QW), bf16),
            jax.ShapeDtypeStruct((chips, rows, 2 * KW), f32),
            jax.ShapeDtypeStruct((chips, rows, 2 * KW), bf16),
        ),
        in_specs=[pl.BlockSpec(memory_space=pltpu.SMEM)] + [vm] * 8,
        out_specs=[vm] * 3,
        scratch_shapes=[pltpu.VMEM((rows, QW), f32)],
        compiler_params=pltpu.CompilerParams(vmem_limit_bytes=48 * 2**20),
        cost_estimate=pl.CostEstimate(
            flops=10 * rows * keys * QW, bytes_accessed=8 * kv_own.size,
            transcendentals=rows * keys * QUERY_HEADS,
        ),
        name="attend_back",
    )(where, queries, kv_own, kv_sib, top, total, d_att, cosine, sine)


def pack_kernel(
    dq_ref, dkv_ref, cos_ref, sin_ref, dgz_ref, dconv_ref, edge_ref, draw_ref, extra_ref, *refs
):
    arrived, out_ref, conv = refs[:-2], refs[-2], refs[-1]
    rows = dq_ref.shape[0]
    d_kv = dkv_ref[...]
    for ref in arrived:
        d_kv = d_kv + ref[...].astype(f32)
    d_k = d_kv[:, :KW]
    d_k = d_k * cos_ref[...] - half_turned(d_k) * sin_ref[...]
    out_ref[:rows, :QW] = dq_ref[...]
    out_ref[:rows, QW : QW + KW] = d_k.astype(bf16)
    out_ref[:rows, QW + KW : QW + 2 * KW] = d_kv[:, KW:].astype(bf16)
    at = QW + 2 * KW
    out_ref[:rows, at : at + INNER] = dgz_ref[...]
    at += INNER
    conv[...] = dconv_ref[...]
    more = edge_ref[0 : KC - 1, :]
    conv[rows - (KC - 1) :, :] = conv[rows - (KC - 1) :, :] + more
    out_ref[:rows, at : at + CONVW] = conv[...].astype(bf16)
    at += CONVW
    out_ref[:rows, at:] = draw_ref[...].astype(bf16)
    out_ref[rows:, :] = extra_ref[...]


def pack(d_q, d_kv, cosine, sine, d_gate_z, d_conv, edge, d_raw, extra, arrived):
    rows = d_q.shape[0]
    vm = pl.BlockSpec(memory_space=pltpu.VMEM)
    return pl.pallas_call(
        pack_kernel,
        out_shape=jax.ShapeDtypeStruct((rows + 16, extra.shape[1]), bf16),
        in_specs=[vm] * (9 + len(arrived)),
        out_specs=vm,
        scratch_shapes=[pltpu.VMEM((rows, CONVW), f32)],
        compiler_params=pltpu.CompilerParams(vmem_limit_bytes=32 * 2**20),
        cost_estimate=pl.CostEstimate(flops=10**6, bytes_accessed=4 * 2**20, transcendentals=0),
        name="pack",
    )(d_q, d_kv, cosine, sine, d_gate_z, d_conv, edge, d_raw, extra, *arrived)


def body(
    tokens,
    cotangent,
    gain_input,
    w_query,
    key_weight,
    value_weight,
    w_mixin,
    conv_taps,
    conv_bias,
    step_offset,
    decay_rate,
    skip_gain,
    gain_mixer,
    w_mixout,
    w_attnout,
    gain_feed,
    w_gate,
    w_up,
    w_down,
):
    rows, width = tokens.shape
    seqs = lax.axis_size("seq")
    ctxs = lax.axis_size("ctx")
    chips = ctxs // 2
    place = lax.axis_index("seq")
    ctx = lax.axis_index("ctx")
    chip, core = ctx // 2, ctx % 2
    ff = w_gate.shape[1]

    sizes = (gain_input.size, gain_feed.size, conv_bias.size, gain_mixer.size, conv_taps.size)
    small = jnp.concatenate(
        [gain_input, gain_feed, conv_bias, gain_mixer, conv_taps.reshape(-1)]
    )
    small = [small] + [seq_swap(small, k) for k in range(1, seqs)]
    bit = 1
    while bit < seqs:
        flip = (place & bit) != 0
        small = [jnp.where(flip, small[j ^ bit], small[j]) for j in range(seqs)]
        bit *= 2
    small = jnp.stack(small).astype(f32)
    at = 0
    pieces = []
    for size in sizes:
        pieces.append(small[:, at : at + size])
        at += size
    gin = pieces[0].reshape(-1)
    gfeed = pieces[1].reshape(-1)
    cbias = pieces[2].reshape(-1)
    gmix = pieces[3].reshape(-1)
    taps = pieces[4].reshape(seqs, KC, -1).transpose(1, 0, 2).reshape(KC, -1)

    used = QW + 2 * KW + w_mixin.shape[1]
    wide = -(-used // 128) * 128
    blank = jnp.zeros((w_mixin.shape[0], wide - used), bf16)
    in_loc = jnp.concatenate([w_query, key_weight, value_weight, w_mixin, blank], axis=1)
    cut = width // (4 * seqs)
    cut = cut if cut % 16 == 0 else 0
    w_in = gather_pieces(take_half(in_loc, core), cut)
    out_loc = jnp.concatenate([w_mixout, w_attnout], axis=0)
    half_out = take_half(out_loc, core)
    half_dn = take_half(w_down, core)
    hr = half_out.shape[0] // 2
    rest = jnp.concatenate(
        [
            take_half(w_gate, core),
            take_half(w_up, core),
            half_out[:hr],
            half_out[hr:],
            half_dn[:hr],
            half_dn[hr:],
        ],
        axis=1,
    )
    where = jnp.stack([place, core, chip]).astype(jnp.int32)

    position = ctx * rows + jnp.arange(rows, dtype=jnp.int32)
    frequency = rope_base ** (
        -(jnp.arange(HEAD_SIZE // 2, dtype=f32) * 2.0 / HEAD_SIZE)
    )
    angles = position.astype(f32)[:, None] * jnp.tile(frequency, 4)[None, :]
    sign = jnp.tile(jnp.repeat(jnp.array([-1.0, 1.0], f32), HEAD_SIZE // 2), 2)
    cosine = jnp.cos(angles)
    sine = jnp.sin(angles) * sign[None, :]
    offset = jnp.pad(step_offset, (0, 128 - MH))[None, :]
    rates = jnp.pad(decay_rate, (0, 128 - MH))[None, :]
    skip_wide = jnp.repeat(skip_gain, MP)[None, :]

    rest, far_in = lax.optimization_barrier((rest, w_in[-1][2]))
    w_in[-1] = (*w_in[-1][:2], far_in)
    w_in = both_cores(w_in)
    near = first_phase(rest)
    normed, queries, message, gate_z, conv_low, raw_step = project(
        where, tokens, gin[None, :], cosine, sine, offset, rates, in_loc, w_in
    )
    mix0 = QW + 2 * KW

    edge = lax.ppermute(
        conv_low[rows - 16 :], "ctx", [(i, i + 1) for i in range(ctxs - 1)]
    )
    kv_own = jnp.stack([message] + [chip_shift(message, k, True) for k in range(1, chips)])
    kv_sib = swap_core(kv_own)
    dec_own = kv_own[:, rows, :MH].astype(f32) + kv_own[:, rows + 1, :MH].astype(f32)
    dec_sib = kv_sib[:, rows, :MH].astype(f32) + kv_sib[:, rows + 1, :MH].astype(f32)
    decays = jnp.stack(
        [jnp.where(core == 0, dec_own, dec_sib), jnp.where(core == 0, dec_sib, dec_own)], axis=1
    )

    act, out_zero, local_state, c_state, exp_cum = ssm_forward(
        conv_low, edge, raw_step, taps, cbias[None, :], offset, rates, skip_wide
    )
    start_state = ctx_state(local_state, decays, chips, core, False)
    cots = [cotangent] + [p[2] for p in gather_pieces(cotangent, rows // 2)]
    queries, near = lax.optimization_barrier((queries, near))
    rest_far = second_phase(near, cut)
    w_rest = both_cores(rest_far)
    attn_b, top, total = attend(where, queries, kv_own, kv_sib)

    layer_out, msg1, msg2, d_gu, grad_res, d_att, d_ssm, d_gate_z, d_start, d_c, d_cum = middle(
        where, tokens, cotangent, normed, out_zero, gate_z, c_state, exp_cum, start_state, attn_b,
        gmix[None, :], gfeed[None, :], (w_gate, w_up, w_mixout, w_attnout, w_down), w_rest, seqs,
    )
    msgs1 = [msg1[0]] + [seq_swap(msg1[k], k) for k in range(1, seqs)]
    msgs2 = [msg2[0]] + [seq_swap(msg2[k], k) for k in range(1, seqs)]

    later_grad = ctx_state(d_start, decays, chips, core, True)
    d_q, d_kv, d_kv_sib = attend_back(
        where, queries, kv_own, kv_sib, top, total, d_att, cosine, sine
    )
    d_kv = d_kv + swap_core(d_kv_sib).astype(f32)
    arrived = [chip_shift(d_kv[k].astype(bf16), -k, False) for k in range(1, chips)]
    d_conv, d_edge, d_raw, extra = ssm_backward(
        conv_low, edge, raw_step, taps, offset, rates, skip_wide, act,
        d_ssm, d_c, d_cum, later_grad, start_state, wide,
    )
    edge_back = lax.ppermute(d_edge, "ctx", [(i + 1, i) for i in range(ctxs - 1)])
    back_msg = pack(
        d_q, d_kv[0], cosine, sine, d_gate_z, d_conv, edge_back, d_raw, extra, arrived
    )
    keep1, give1 = grads(grads_kernel, "out_grads", where, msgs1, cots, hr, 4 * width)
    back_msg, keep1, give1 = lax.optimization_barrier((back_msg, keep1, give1))
    total1, unused = sum_halves(keep1, swap_core(give1), chips, chip, None)
    rights2 = [d_gu] + [p[2] for p in gather_pieces(d_gu, rows // 2)]
    keep2, give2 = grads(feed_grads_kernel, "feed_grads", where, msgs2, rights2, hr, 2 * ff)
    total2, unused = sum_halves(keep2, swap_core(give2), chips, chip, None)
    backs = [back_msg] + [p[2] for p in gather_pieces(back_msg, rows // 2)]
    backs[0], total2 = lax.optimization_barrier((backs[0], total2))
    keep3, give3, small = last_grads(where, msgs2, backs, hr, rows // 2)
    mine1 = spread_halves(total1, chips, chip)
    mine2 = spread_halves(total2, chips, chip)
    total3, small_sum = sum_halves(keep3, swap_core(give3), chips, chip, small)
    grad_tokens = unproject(where, tokens, gin[None, :], grad_res, back_msg, in_loc, w_in)
    mine3 = spread_halves(total3, chips, chip)

    sum_mix, sum_att, sum_dn, grad_gmix = last_out(
        where, mine1, swap_core(mine1), w_mixout, gain_mixer[:, None], QW // seqs
    )
    sum_gate, sum_up, grad_gfeed = last_feed(
        where, mine2, swap_core(mine2), w_gate, w_up, gain_feed[:, None]
    )
    sum_q, sum_k, sum_v, sum_mixin, grad_gin = last_in(
        where, mine3, swap_core(mine3), in_loc, gain_input[:, None], used - mix0
    )
    small_taps = small_sum[:2, : 2 * CONVW].reshape(KC, CONVW)

    def own_share(vec):
        size = vec.shape[-1] // seqs
        return lax.dynamic_slice_in_dim(vec, place * size, size, vec.ndim - 1)

    heads = small_sum[2, CONVW:]
    return (
        layer_out,
        grad_tokens,
        grad_gin[:, 0],
        sum_q,
        sum_k,
        sum_v,
        sum_mixin,
        own_share(small_taps),
        own_share(small_sum[2, :CONVW]),
        heads[:MH],
        heads[128 : 128 + MH],
        heads[256 : 256 + MH],
        grad_gmix[:, 0],
        sum_mix,
        sum_att,
        grad_gfeed[:, 0],
        sum_gate,
        sum_up,
        sum_dn,
    )


def solution(mesh):
    rows = P(("seq", "ctx"), None)
    vec = P("seq")
    mat = P("seq", None)
    col = P(None, "seq")
    rep = P()
    in_specs = (
        rows, rows, vec, mat, mat, mat, mat, col, vec, rep, rep, rep, vec, mat, mat, vec, mat, mat, mat,
    )
    out_specs = (
        rows, rows, vec, mat, mat, mat, mat, col, vec, rep, rep, rep, vec, mat, mat, vec, mat, mat, mat,
    )
    return jax.shard_map(body, mesh=mesh, in_specs=in_specs, out_specs=out_specs, check_vma=False)
```

```python
import functools

import jax
import jax.numpy as jnp
from jax import lax
from jax.experimental import pallas as pl
from jax.experimental.pallas import tpu as pltpu
from jax.sharding import PartitionSpec as P

QUERY_HEADS = 8
VALUE_HEADS = 2
HEAD_SIZE = 64
MH = 24
MP = 64
NS = 128
KC = 4
GROUP = QUERY_HEADS // VALUE_HEADS
INNER = MH * MP
CONVW = INNER + 2 * NS
QW = QUERY_HEADS * HEAD_SIZE
KW = VALUE_HEADS * HEAD_SIZE

norm_epsilon = 1e-06
rope_base = 100000000000.0
f32 = jnp.float32
bf16 = jnp.bfloat16


def dot(a, b):
    return jnp.dot(a, b, preferred_element_type=f32)


def dot_nt(a, b):
    return lax.dot_general(a, b, (((1,), (1,)), ((), ())), preferred_element_type=f32)


def dot_tn(a, b):
    return lax.dot_general(a, b, (((0,), (0,)), ((), ())), preferred_element_type=f32)


def swap_core(value):
    count = lax.axis_size("ctx")
    return lax.ppermute(value, "ctx", [(i, i ^ 1) for i in range(count)])


def chip_shift(value, steps, wrap):
    count = lax.axis_size("ctx")
    pairs = []
    for i in range(count):
        to = i + 2 * steps
        if wrap:
            pairs.append((i, to % count))
        elif 0 <= to < count:
            pairs.append((i, to))
    return lax.ppermute(value, "ctx", pairs)


def seq_swap(value, k):
    count = lax.axis_size("seq")
    return lax.ppermute(value, "seq", [(i, i ^ k) for i in range(count)])


def take_half(value, core):
    rows = value.shape[0] // 2
    return lax.dynamic_slice_in_dim(value, core * rows, rows, 0)


def first_phase(value):
    seqs = lax.axis_size("seq")
    return [seq_swap(value, k) for k in (range(1, seqs) if seqs != 4 else (1, 2))]


def second_phase(near, cut):
    if len(near) != 2:
        return [(k + 1, 0, piece) for k, piece in enumerate(near)]
    far_a = seq_swap(near[0][:cut], 2)
    far_b = seq_swap(near[1][cut:], 1)
    return [(1, 0, near[0]), (2, 0, near[1]), (3, 0, far_a), (3, cut, far_b)]


def gather_pieces(value, cut):
    return second_phase(first_phase(value), cut)


def both_cores(pieces):
    out = []
    for k, row, array in pieces:
        out.append((k, 0, row, array))
        out.append((k, 1, row, swap_core(array)))
    return out


def chip_swap(value, bit):
    count = lax.axis_size("ctx")
    return lax.ppermute(value, "ctx", [(i, i ^ (2 * bit)) for i in range(count)])


def sum_halves(mine, arrived, chips, chip, small):
    rows = mine.shape[0]

    def widened(message, rows):
        return message[rows : rows + 8].astype(f32) + message[rows + 8 : rows + 16].astype(f32)

    def narrowed(values):
        hi, low = two(values)
        return jnp.concatenate([hi, low], axis=0)

    if small is not None:
        tail = narrowed(small)
        small = widened(tail, 0) + widened(arrived, rows)
        arrived = arrived[:rows]
    total = mine + arrived.astype(f32)
    bit = 1
    while bit < chips:
        rows //= 2
        side = jnp.where((chip & bit) != 0, 1, 0)
        give = lax.dynamic_slice_in_dim(total, (1 - side) * rows, rows, 0).astype(bf16)
        if small is not None:
            tail = narrowed(small)
            give = jnp.concatenate([give, tail], axis=0)
        arrived = chip_swap(give, bit)
        if small is not None:
            small = widened(tail, 0) + widened(arrived, rows)
            arrived = arrived[:rows]
        total = lax.dynamic_slice_in_dim(total, side * rows, rows, 0) + arrived.astype(f32)
        bit *= 2
    return total.astype(bf16), small


def spread_halves(total, chips, chip):
    bit = chips // 2
    while bit >= 1:
        other = chip_swap(total, bit)
        upper = (chip & bit) != 0
        total = jnp.concatenate(
            [jnp.where(upper, other, total), jnp.where(upper, total, other)], axis=0
        )
        bit //= 2
    return total


def ctx_state(low, decays, chips, chip, core, later):
    half = INNER // 2
    mine = lax.dynamic_slice_in_dim(low, core * half, half, 0).astype(f32)
    others = lax.dynamic_slice_in_dim(low, (1 - core) * half, half, 0)
    got = swap_core(others).astype(f32)
    even = jnp.where(core == 0, mine, got)
    odd = jnp.where(core == 0, got, mine)
    dec = lax.dynamic_slice_in_dim(decays, core * (MH // 2), MH // 2, 2)
    here = lax.dynamic_index_in_dim(dec, chip, 0, False)
    here = jnp.repeat(here, MP, axis=1)[..., None]
    block_decay = [dec[c, 0] * dec[c, 1] for c in range(chips)]
    if later:
        total = even + here[0] * odd
    else:
        total = odd + here[1] * even
    before = jnp.zeros_like(total)
    reach = jnp.ones((MH // 2,), f32)
    bit = 1

    def wide(vec):
        return jnp.repeat(vec, MP)[:, None]

    while bit < chips:
        if later or bit == 1:
            arrived = chip_swap(total.astype(bf16), bit).astype(f32)
        else:
            arrived = chip_swap(jnp.concatenate(two(total), axis=0), bit).astype(f32)
            arrived = arrived[:half] + arrived[half:]
        upper = (chip & bit) != 0
        takes = jnp.logical_not(upper) if later else upper
        mine_at, other_at = chip // bit, (chip // bit) ^ 1
        table = jnp.stack(block_decay)
        mine_decay = lax.dynamic_index_in_dim(table, mine_at, 0, False)
        other_decay = lax.dynamic_index_in_dim(table, other_at, 0, False)
        before = before + jnp.where(takes, wide(reach) * arrived, 0.0)
        reach = jnp.where(takes, reach * other_decay, reach)
        if 2 * bit < chips:
            total = jnp.where(
                takes, wide(mine_decay) * arrived + total, wide(other_decay) * total + arrived
            )
            block_decay = [
                block_decay[2 * i] * block_decay[2 * i + 1] for i in range(len(block_decay) // 2)
            ]
        bit *= 2
    if later:
        for_odd = before
        for_even = odd + here[1] * before
    else:
        for_even = before
        for_odd = even + here[0] * before
    keep = jnp.where(core == 0, for_even, for_odd).astype(bf16)
    give = jnp.where(core == 0, for_odd, for_even).astype(bf16)
    back = swap_core(give)
    first = jnp.where(core == 0, keep, back)
    second = jnp.where(core == 0, back, keep)
    return jnp.concatenate([first, second], axis=0)


def silu_parts(z):
    sig = 1.0 / (1.0 + jnp.exp(-z))
    return z * sig, sig * (1.0 + z * (1.0 - sig))


def three(a):
    hi = a.astype(bf16)
    rest = a - hi.astype(f32)
    mid = rest.astype(bf16)
    return hi, mid, (rest - mid.astype(f32)).astype(bf16)


def exact_dot(a, b):
    hi, mid, low = three(a)
    return dot(hi, b) + dot(mid, b) + dot(low, b)


def two(a):
    hi = a.astype(bf16)
    return hi, (a - hi.astype(f32)).astype(bf16)


def exact_dot_nt(a, b):
    hi, mid, low = three(a)
    return dot_nt(hi, b) + dot_nt(mid, b) + dot_nt(low, b)


def head_table():
    head = lax.broadcasted_iota(jnp.int32, (128, INNER), 0)
    column = lax.broadcasted_iota(jnp.int32, (128, INNER), 1)
    return (column // MP == head).astype(bf16)


def placed(place, core, pieces, hr):
    return [
        ((place ^ k) * 2 * hr + jnp.where(core == side, 0, hr) + row) for k, side, row in pieces
    ]


def run_copies(copies):
    for copy in copies:
        copy.start()


def wait_copies(copies):
    for copy in copies:
        copy.wait()


def in_copies(pieces, where_ref, local_ref, refs, weight, sems):
    place, core = where_ref[0], where_ref[1]
    hr = local_ref.shape[0] // 2
    copies = [
        pltpu.make_async_copy(
            local_ref,
            weight.at[pl.ds(pl.multiple_of(place * 2 * hr, 16), 2 * hr), :],
            sems.at[0],
        )
    ]
    for i, (at, ref) in enumerate(zip(placed(place, core, pieces, hr), refs)):
        copies.append(
            pltpu.make_async_copy(
                ref,
                weight.at[pl.ds(pl.multiple_of(at, 16), ref.shape[0]), :],
                sems.at[i + 1],
            )
        )
    return copies


def project_kernel(pieces, where_ref, tok_ref, gin_ref, cos_ref, sin_ref, off_ref, rate_ref,
                   local_ref, *refs):
    count = len(pieces)
    parts, outs = refs[:count], refs[count:]
    nor_ref, q_ref, kv_ref, gz_ref, conv_ref, raw_ref, pre, weight, sems = outs
    copies = in_copies(pieces, where_ref, local_ref, parts, weight, sems)
    run_copies(copies)
    x = tok_ref[...].astype(f32)
    rows = x.shape[0]
    inv = lax.rsqrt(jnp.mean(x * x, axis=1, keepdims=True) + norm_epsilon)
    nor_ref[...] = (x * inv * gin_ref[...]).astype(bf16)
    wide = weight.shape[1]
    part = 384
    wait_copies(copies)

    def one(i, carry):
        a = pl.ds(pl.multiple_of(i * part, 128), part)
        pre[:, a] = dot(nor_ref[...], weight[:, a])
        return carry

    lax.fori_loop(0, wide // part, one, 0)
    for at in range(0, QW, 128):
        u = pre[:, at : at + 128]
        q_ref[:, at : at + 128] = (u * cos_ref[...] + half_turned(u) * sin_ref[...]).astype(bf16)
    u = pre[:, QW : QW + KW]
    kv_ref[:rows, :KW] = (u * cos_ref[...] + half_turned(u) * sin_ref[...]).astype(bf16)
    kv_ref[:rows, KW:] = pre[:, QW + KW : QW + 2 * KW].astype(bf16)
    at = QW + 2 * KW
    gz_ref[...] = pre[:, at : at + INNER]
    at += INNER
    conv_ref[...] = pre[:, at : at + CONVW].astype(bf16)
    at += CONVW
    raw = pre[:, at:]
    raw_ref[...] = raw
    unused, unused, cum, unused = heads_of(raw, off_ref[...], rate_ref[...])
    decay = jnp.exp(cum[rows - 1 : rows, :])
    hi, low = two(decay)
    row = lax.broadcasted_iota(jnp.int32, (16, 128), 0)
    both = jnp.where(row == 0, hi.astype(f32), jnp.where(row == 1, low.astype(f32), 0.0))
    kv_ref[rows:, :KW] = both.astype(bf16)
    kv_ref[rows:, KW:] = jnp.zeros((16, KW), bf16)


def project(where, tokens, gin, cosine, sine, offset, rates, local, pieces):
    rows, width = tokens.shape
    wide = local.shape[1]
    vm = pl.BlockSpec(memory_space=pltpu.VMEM)
    hbm = pl.BlockSpec(memory_space=pl.ANY)
    return pl.pallas_call(
        functools.partial(project_kernel, [p[:3] for p in pieces]),
        out_shape=(
            jax.ShapeDtypeStruct((rows, width), bf16),
            jax.ShapeDtypeStruct((rows, QW), bf16),
            jax.ShapeDtypeStruct((rows + 16, 2 * KW), bf16),
            jax.ShapeDtypeStruct((rows, INNER), f32),
            jax.ShapeDtypeStruct((rows, CONVW), bf16),
            jax.ShapeDtypeStruct((rows, 128), f32),
        ),
        in_specs=[pl.BlockSpec(memory_space=pltpu.SMEM)] + [vm] * 6 + [hbm] * (1 + len(pieces)),
        out_specs=[vm] * 6,
        scratch_shapes=[
            pltpu.VMEM((rows, wide), f32),
            pltpu.VMEM((width, wide), bf16),
            pltpu.SemaphoreType.DMA((1 + len(pieces),)),
        ],
        compiler_params=pltpu.CompilerParams(vmem_limit_bytes=40 * 2**20),
        cost_estimate=pl.CostEstimate(
            flops=2 * rows * width * wide, bytes_accessed=2 * width * wide + 3 * 2**20,
            transcendentals=0,
        ),
        name="project",
    )(where, tokens, gin, cosine, sine, offset, rates, local, *[p[3] for p in pieces])


def unproject_kernel(pieces, where_ref, tok_ref, gin_ref, gres_ref, back_ref, local_ref, *refs):
    parts, (out_ref, weight, sems) = refs[:-3], refs[-3:]
    copies = in_copies(pieces, where_ref, local_ref, parts, weight, sems)
    run_copies(copies)
    x = tok_ref[...].astype(f32)
    rows, width = x.shape
    inv = lax.rsqrt(jnp.mean(x * x, axis=1, keepdims=True) + norm_epsilon)
    unit = x * inv
    wide = weight.shape[1]
    part = 384
    out_ref[...] = jnp.zeros_like(out_ref)
    wait_copies(copies)

    def one(i, carry):
        a = pl.ds(pl.multiple_of(i * part, 128), part)
        out_ref[...] += dot_nt(back_ref[:rows, a], weight[:, a])
        return carry

    lax.fori_loop(0, wide // part, one, 0)
    d_norm = out_ref[...] * gin_ref[...]
    d_x = inv * (d_norm - unit * jnp.mean(d_norm * unit, axis=1, keepdims=True))
    out_ref[...] = gres_ref[...] + d_x


def unproject(where, tokens, gin, grad_res, back, local, pieces):
    rows, width = tokens.shape
    wide = local.shape[1]
    vm = pl.BlockSpec(memory_space=pltpu.VMEM)
    hbm = pl.BlockSpec(memory_space=pl.ANY)
    return pl.pallas_call(
        functools.partial(unproject_kernel, [p[:3] for p in pieces]),
        out_shape=jax.ShapeDtypeStruct((rows, width), f32),
        in_specs=[pl.BlockSpec(memory_space=pltpu.SMEM)] + [vm] * 4 + [hbm] * (1 + len(pieces)),
        out_specs=vm,
        scratch_shapes=[
            pltpu.VMEM((width, wide), bf16),
            pltpu.SemaphoreType.DMA((1 + len(pieces),)),
        ],
        compiler_params=pltpu.CompilerParams(vmem_limit_bytes=40 * 2**20),
        cost_estimate=pl.CostEstimate(
            flops=2 * rows * width * wide, bytes_accessed=2 * width * wide + 3 * 2**20,
            transcendentals=0,
        ),
        name="unproject",
    )(where, tokens, gin, grad_res, back, local, *[p[3] for p in pieces])


def last_grads_kernel(seqs, cut, where_ref, *refs):
    lefts, rights = refs[:seqs], refs[seqs:-3]
    keep_ref, give_ref, small_ref = refs[-3:]
    is0 = where_ref[1] == 0
    hr, wide = keep_ref.shape
    rows = lefts[0].shape[0]
    a = jnp.concatenate([m[:, :hr] for m in lefts], axis=0)
    b = jnp.concatenate([m[:, hr : 2 * hr] for m in lefts], axis=0)
    mine, other = jnp.where(is0, a, b), jnp.where(is0, b, a)
    part = 384
    if cut:
        spans = [rows] * (seqs - 1) + [cut, rows - cut]
        ends = list(range(seqs - 1)) + [seqs]
        starts = [rows] * (seqs - 1) + [rows - cut]
    else:
        spans, ends, starts = [rows] * seqs, list(range(seqs)), [rows] * seqs
    extras = [
        rights[i][at : at + 8, :].astype(f32) + rights[i][at + 8 : at + 16, :].astype(f32)
        for i, at in zip(ends, starts)
    ]
    while len(extras) > 1:
        extras = [extras[i] + extras[i + 1] for i in range(0, len(extras), 2)]
    small_ref[...] = extras[0]
    hi, low = two(extras[0])
    give_ref[hr:, :] = jnp.concatenate([hi.astype(f32), low.astype(f32)], axis=0).astype(bf16)

    def one(i, carry):
        src = pl.ds(pl.multiple_of(i * part, 128), part)
        right = jnp.concatenate([m[:n, src] for m, n in zip(rights, spans)], axis=0)
        keep_ref[:, src] = dot_tn(mine, right)
        give_ref[:hr, src] = dot_tn(other, right).astype(bf16)
        return carry

    lax.fori_loop(0, wide // part, one, 0)


def last_grads(where, lefts, rights, hr, cut):
    wide = rights[0].shape[1]
    seqs = len(lefts)
    vm = pl.BlockSpec(memory_space=pltpu.VMEM)
    return pl.pallas_call(
        functools.partial(last_grads_kernel, seqs, cut if len(rights) > seqs else 0),
        out_shape=(
            jax.ShapeDtypeStruct((hr, wide), f32),
            jax.ShapeDtypeStruct((hr + 16, wide), bf16),
            jax.ShapeDtypeStruct((8, wide), f32),
        ),
        in_specs=[pl.BlockSpec(memory_space=pltpu.SMEM)] + [vm] * (len(lefts) + len(rights)),
        out_specs=[vm, vm, vm],
        compiler_params=pltpu.CompilerParams(vmem_limit_bytes=40 * 2**20),
        cost_estimate=pl.CostEstimate(
            flops=4 * seqs * rights[0].size * hr, bytes_accessed=2 * seqs * rights[0].size,
            transcendentals=0,
        ),
        name="last_grads",
    )(where, *lefts, *rights)


def middle_kernel(
    seqs, pieces, where_ref, tok_ref, cot_ref, nor_ref, zero_ref, gz_ref, c_ref,
    ecum_ref, start_ref, att_ref, gmix_ref, gfeed_ref,
    gate_ref, up_ref, mix_ref, attw_ref, down_ref, *refs,
):
    count = len(pieces)
    parts = refs[:count]
    (
        lay_ref, msg1_ref, msg2_ref, dgu_ref, gres_ref, datt_ref, dssm_ref, dgz_ref, dstart_ref,
        dc_ref, dcum_ref,
        ssm, outs, feeds, hids, gates, ups, dhid, dout, w_gu, w_out, w_dn, sems,
    ) = refs[count:]
    place, core = where_ref[0], where_ref[1]
    rows, width = tok_ref.shape
    ff = hids.shape[1]
    hr = width // (2 * seqs)
    mixw, attw = INNER // seqs, QW // seqs
    outw = mixw + attw
    base_out, base_dn = 2 * ff, 2 * ff + 2 * width

    def at_rows(ref, row, size):
        return ref.at[pl.ds(pl.multiple_of(row, 16), size), :]

    starts = placed(place, core, pieces, hr)
    copies = {"out": [], "gu": [], "dn": []}

    def add(group, source, target):
        number = sum(len(c) for c in copies.values())
        copies[group].append(pltpu.make_async_copy(source, target, sems.at[number]))

    add("out", mix_ref, at_rows(w_out, place * 4 * hr, mixw))
    add("out", attw_ref, at_rows(w_out, place * 4 * hr + mixw, attw))

    def blocks(group, base, target):
        for (k, side, row), ref in zip(pieces, parts):
            for b in range(2):
                at = (place ^ k) * 4 * hr + jnp.where(core == side, 0, 2 * hr) + b * hr + row
                add(
                    group, ref.at[:, base + b * width : base + (b + 1) * width],
                    at_rows(target, at, ref.shape[0]),
                )

    blocks("out", base_out, w_out)
    own_rows = pl.ds(pl.multiple_of(place * 2 * hr, 16), 2 * hr)
    add("gu", gate_ref, w_gu.at[own_rows, :ff])
    add("gu", up_ref, w_gu.at[own_rows, ff:])
    for at, ref in zip(starts, parts):
        add("gu", ref.at[:, : 2 * ff], at_rows(w_gu, at, ref.shape[0]))
    add("dn", down_ref, at_rows(w_dn, place * 4 * hr, 4 * hr))
    blocks("dn", base_dn, w_dn)
    for group in ("out", "gu", "dn"):
        run_copies(copies[group])

    table = head_table()
    c_hi, c_lo = two(c_ref[...])
    ecum = exact_dot(ecum_ref[...], table)
    across = (dot_nt(c_hi, start_ref[...]) + dot_nt(c_lo, start_ref[...])) * ecum
    whole = zero_ref[...] + across
    silu_z, slope_z = silu_parts(gz_ref[...])
    gated = whole * silu_z
    inv_mix = lax.rsqrt(jnp.mean(gated * gated, axis=1, keepdims=True) + norm_epsilon)
    gmix = gmix_ref[...]
    ssm[...] = gated * inv_mix
    mix_b = (ssm[...] * gmix).astype(bf16)
    for j in range(seqs):
        outs[:, j * outw : j * outw + mixw] = mix_b[:, j * mixw : (j + 1) * mixw]
        outs[:, j * outw + mixw : (j + 1) * outw] = att_ref[:, j * attw : (j + 1) * attw]
    part = 512
    wait_copies(copies["out"])

    def attach(i, carry):
        a = pl.ds(pl.multiple_of(i * part, part), part)
        gres_ref[:, a] = tok_ref[:, a].astype(f32) + dot(outs[...], w_out[:, a])
        return carry

    lax.fori_loop(0, width // part, attach, 0)
    residual = gres_ref[...]
    inv_res = lax.rsqrt(jnp.mean(residual * residual, axis=1, keepdims=True) + norm_epsilon)
    gfeed = gfeed_ref[...]
    feeds[...] = (residual * inv_res * gfeed).astype(bf16)
    wait_copies(copies["gu"])

    def forward(i, carry):
        a = pl.ds(pl.multiple_of(i * part, part), part)
        u = pl.ds(pl.multiple_of(ff + i * part, part), part)
        gate = dot(feeds[...], w_gu[:, a])
        up = dot(feeds[...], w_gu[:, u])
        gates[:, a] = gate
        ups[:, a] = up
        hids[:, a] = (gate / (1.0 + jnp.exp(-gate)) * up).astype(bf16)
        return carry

    lax.fori_loop(0, ff // part, forward, 0)
    cot = cot_ref[...]
    wait_copies(copies["dn"])

    def finish(i, carry):
        a = pl.ds(pl.multiple_of(i * part, part), part)
        lay_ref[:, a] = (gres_ref[:, a] + dot(hids[...], w_dn[:, a])).astype(bf16)
        return carry

    lax.fori_loop(0, width // part, finish, 0)

    def through(i, carry):
        a = pl.ds(pl.multiple_of(i * part, part), part)
        dhid[:, a] = dot_nt(cot, w_dn[a, :])
        return carry

    lax.fori_loop(0, ff // part, through, 0)
    dout[:, :width] = jnp.zeros((rows, width), f32)

    def backward(i, carry):
        a = pl.ds(pl.multiple_of(i * part, part), part)
        u = pl.ds(pl.multiple_of(ff + i * part, part), part)
        silu_g, slope_g = silu_parts(gates[:, a])
        grad = dhid[:, a]
        d_gate = (grad * ups[:, a] * slope_g).astype(bf16)
        d_up = (grad * silu_g).astype(bf16)
        dgu_ref[:, a] = d_gate
        dgu_ref[:, u] = d_up
        dout[:, :width] += dot_nt(d_gate, w_gu[:, a]) + dot_nt(d_up, w_gu[:, u])
        return carry

    lax.fori_loop(0, ff // part, backward, 0)
    unit_res = gres_ref[...] * inv_res
    d_feed = dout[:, :width] * gfeed
    d_res = inv_res * (d_feed - unit_res * jnp.mean(d_feed * unit_res, axis=1, keepdims=True))
    grad_res = cot.astype(f32) + d_res
    gres_ref[...] = grad_res
    res_b = grad_res.astype(bf16)

    def leave(i, carry):
        a = pl.ds(pl.multiple_of(i * part, part), part)
        dout[:, a] = dot_nt(res_b, w_out[a, :])
        return carry

    lax.fori_loop(0, (INNER + QW) // part, leave, 0)
    for j in range(seqs):
        datt_ref[:, j * attw : (j + 1) * attw] = dout[
            :, j * outw + mixw : (j + 1) * outw
        ].astype(bf16)
        dssm_ref[:, j * mixw : (j + 1) * mixw] = dout[:, j * outw : j * outw + mixw]
    for k in range(seqs):
        to = place ^ k
        for ref, sources in (
            (msg1_ref, ((outs, outw), (hids, ff // seqs))),
            (msg2_ref, ((nor_ref, 2 * hr), (feeds, 2 * hr))),
        ):
            at = 0
            for source, size in sources:
                ref[k, :, at : at + size] = source[:, pl.ds(pl.multiple_of(to * size, 128), size)]
                at += size
        msg1_ref[k, :, outw + ff // seqs :] = res_b
    unit_mix = ssm[...]
    d_norm = dssm_ref[...] * gmix
    d_gated = inv_mix * (d_norm - unit_mix * jnp.mean(d_norm * unit_mix, axis=1, keepdims=True))
    dgz_ref[...] = (d_gated * whole * slope_z).astype(bf16)
    d_ssm = d_gated * silu_z
    dssm_ref[...] = d_ssm
    dcum_ref[...] = exact_dot_nt(d_ssm * across, table)
    da_hi, da_lo = two(d_ssm * ecum)
    dc_ref[...] = dot(da_hi, start_ref[...]) + dot(da_lo, start_ref[...])
    dstart_ref[...] = (dot_tn(da_hi, c_hi) + dot_tn(da_hi, c_lo) + dot_tn(da_lo, c_hi)).astype(
        bf16
    )


def middle(where, tokens, cotangent, normed, out_zero, gate_z, c_state, ecum, start,
           attn_b, gmix, gfeed, locals_, pieces, seqs):
    rows, width = tokens.shape
    ff = locals_[0].shape[1]
    outw = INNER + QW
    out_shape = (
        jax.ShapeDtypeStruct((rows, width), bf16),
        jax.ShapeDtypeStruct((seqs, rows, (outw + ff) // seqs + width), bf16),
        jax.ShapeDtypeStruct((seqs, rows, 2 * width // seqs), bf16),
        jax.ShapeDtypeStruct((rows, 2 * ff), bf16),
        jax.ShapeDtypeStruct((rows, width), f32),
        jax.ShapeDtypeStruct((rows, QW), bf16),
        jax.ShapeDtypeStruct((rows, INNER), f32),
        jax.ShapeDtypeStruct((rows, INNER), bf16),
        jax.ShapeDtypeStruct((INNER, NS), bf16),
        jax.ShapeDtypeStruct((rows, NS), f32),
        jax.ShapeDtypeStruct((rows, 128), f32),
    )
    vm = pl.BlockSpec(memory_space=pltpu.VMEM)
    hbm = pl.BlockSpec(memory_space=pl.ANY)
    scratch = [
        pltpu.VMEM((rows, INNER), f32),
        pltpu.VMEM((rows, outw), bf16),
        pltpu.VMEM((rows, width), bf16),
        pltpu.VMEM((rows, ff), bf16),
        pltpu.VMEM((rows, ff), f32),
        pltpu.VMEM((rows, ff), f32),
        pltpu.VMEM((rows, ff), f32),
        pltpu.VMEM((rows, outw), f32),
        pltpu.VMEM((width, 2 * ff), bf16),
        pltpu.VMEM((outw, width), bf16),
        pltpu.VMEM((ff, width), bf16),
        pltpu.SemaphoreType.DMA((5 + 5 * len(pieces),)),
    ]
    weights = width * 2 * ff + (outw + ff) * width
    return pl.pallas_call(
        functools.partial(middle_kernel, seqs, [p[:3] for p in pieces]),
        out_shape=out_shape,
        in_specs=[pl.BlockSpec(memory_space=pltpu.SMEM)] + [vm] * 11
        + [hbm] * (5 + len(pieces)),
        out_specs=[vm] * len(out_shape),
        scratch_shapes=scratch,
        compiler_params=pltpu.CompilerParams(vmem_limit_bytes=52 * 2**20),
        cost_estimate=pl.CostEstimate(
            flops=4 * rows * weights, bytes_accessed=2 * weights + 8 * 2**20,
            transcendentals=rows * 8192,
        ),
        name="middle",
    )(where, tokens, cotangent, normed, out_zero, gate_z, c_state, ecum, start,
      attn_b, gmix, gfeed, *locals_, *[p[3] for p in pieces])


def segment(is0, a, b, rights, span, target, keep_ref, give_ref):
    mine, other = jnp.where(is0, a, b), jnp.where(is0, b, a)
    part = 512

    def one(i, carry):
        src = pl.ds(pl.multiple_of(span[0] + i * part, 128), part)
        dst = pl.ds(pl.multiple_of(target + i * part, 128), part)
        rows = jnp.concatenate([m[:, src] for m in rights], axis=0)
        keep_ref[:, dst] = dot_tn(mine, rows)
        give_ref[:, dst] = dot_tn(other, rows).astype(bf16)
        return carry

    lax.fori_loop(0, span[1] // part, one, 0)


def grads_kernel(seqs, where_ref, *refs):
    msgs, cots, keep_ref, give_ref = refs[:seqs], refs[seqs:-2], refs[-2], refs[-1]
    is0 = where_ref[1] == 0
    hr = keep_ref.shape[0]
    width = 2 * hr * seqs
    at_res = msgs[0].shape[1] - width

    def left(at):
        return jnp.concatenate([m[:, at : at + hr] for m in msgs], axis=0)

    for b in range(2):
        segment(
            is0, left(b * hr), left((b + 2) * hr), msgs, (at_res, width), b * width,
            keep_ref, give_ref,
        )
        at = 4 * hr + b * hr
        segment(
            is0, left(at), left(at + 2 * hr), cots, (0, width), (2 + b) * width,
            keep_ref, give_ref,
        )


def feed_grads_kernel(seqs, where_ref, *refs):
    msgs, rights, keep_ref, give_ref = refs[:seqs], refs[seqs:-2], refs[-2], refs[-1]
    is0 = where_ref[1] == 0
    hr, columns = keep_ref.shape

    def left(at):
        return jnp.concatenate([m[:, at : at + hr] for m in msgs], axis=0)

    segment(is0, left(2 * hr), left(3 * hr), rights, (0, columns), 0, keep_ref, give_ref)


def grads(kernel, name, where, lefts, rights, hr, columns):
    vm = pl.BlockSpec(memory_space=pltpu.VMEM)
    seqs = len(lefts)
    return pl.pallas_call(
        functools.partial(kernel, seqs),
        out_shape=(
            jax.ShapeDtypeStruct((hr, columns), f32),
            jax.ShapeDtypeStruct((hr, columns), bf16),
        ),
        in_specs=[pl.BlockSpec(memory_space=pltpu.SMEM)] + [vm] * (len(lefts) + len(rights)),
        out_specs=[vm, vm],
        compiler_params=pltpu.CompilerParams(vmem_limit_bytes=40 * 2**20),
        cost_estimate=pl.CostEstimate(
            flops=4 * lefts[0].shape[0] * seqs * hr * columns,
            bytes_accessed=2 * seqs * (lefts[0].size + rights[0].size) + 6 * hr * columns,
            transcendentals=0,
        ),
        name=name,
    )(where, *lefts, *rights)


def halves_in_order(is0, mine_ref, other_ref, cols):
    mine, other = mine_ref[:, cols].astype(f32), other_ref[:, cols].astype(f32)
    return jnp.where(is0, mine, other), jnp.where(is0, other, mine)


def last_in_kernel(where_ref, mine_ref, other_ref, weight_ref, gain_ref,
                   q_ref, k_ref, v_ref, mix_ref, gin_ref):
    is0 = where_ref[1] == 0
    hr = mine_ref.shape[0]
    total = [jnp.zeros((hr, 1), f32), jnp.zeros((hr, 1), f32)]

    def added(i, grad, here, cols):
        total[i] = total[i] + jnp.sum(
            grad * weight_ref[here, cols].astype(f32), axis=1, keepdims=True
        )

    at = 0
    for ref in (q_ref, k_ref, v_ref):
        cols = slice(at, at + ref.shape[1])
        for i, grad in enumerate(halves_in_order(is0, mine_ref, other_ref, cols)):
            here = slice(i * hr, (i + 1) * hr)
            ref[here, :] = grad
            added(i, grad, here, cols)
        at += ref.shape[1]
    mixed, part = mix_ref.shape[0], 128
    for start in range(0, mixed, part):
        size = min(part, mixed - start)
        cols = slice(at + start, at + start + part)
        turned = []
        for i, grad in enumerate(halves_in_order(is0, mine_ref, other_ref, cols)):
            added(i, grad, slice(i * hr, (i + 1) * hr), cols)
            turned.append(jnp.transpose(grad)[:size])
        mix_ref[start : start + size, :] = jnp.concatenate(turned, axis=1)
    for i in range(2):
        here = slice(i * hr, (i + 1) * hr)
        gin_ref[here, :] = total[i] / gain_ref[here, :].astype(f32)


def last_in(where, mine, other, weight, gain, mixed):
    vm = pl.BlockSpec(memory_space=pltpu.VMEM)
    rows = 2 * mine.shape[0]
    shapes = ((rows, QW), (rows, KW), (rows, KW), (mixed, rows), (rows, 1))
    return pl.pallas_call(
        last_in_kernel,
        out_shape=tuple(jax.ShapeDtypeStruct(shape, f32) for shape in shapes),
        in_specs=[pl.BlockSpec(memory_space=pltpu.SMEM)] + [vm] * 4,
        out_specs=[vm] * 5,
        compiler_params=pltpu.CompilerParams(vmem_limit_bytes=40 * 2**20),
        name="last_in",
    )(where, mine, other, weight, gain)


def last_feed_kernel(where_ref, mine_ref, other_ref, gate_ref, up_ref, gain_ref,
                     out_gate_ref, out_up_ref, gfeed_ref):
    is0 = where_ref[1] == 0
    hr = mine_ref.shape[0]
    ff = gate_ref.shape[1]
    total = [jnp.zeros((hr, 1), f32), jnp.zeros((hr, 1), f32)]
    for base, weight_ref, out_ref in ((0, gate_ref, out_gate_ref), (ff, up_ref, out_up_ref)):
        for start in range(0, ff, 512):
            cols = slice(base + start, base + start + 512)
            to = slice(start, start + 512)
            for i, grad in enumerate(halves_in_order(is0, mine_ref, other_ref, cols)):
                here = slice(i * hr, (i + 1) * hr)
                out_ref[here, to] = grad
                total[i] = total[i] + jnp.sum(
                    grad * weight_ref[here, to].astype(f32), axis=1, keepdims=True
                )
    for i in range(2):
        here = slice(i * hr, (i + 1) * hr)
        gfeed_ref[here, :] = total[i] / gain_ref[here, :].astype(f32)


def last_feed(where, mine, other, gate, up, gain):
    vm = pl.BlockSpec(memory_space=pltpu.VMEM)
    rows, ff = gate.shape
    return pl.pallas_call(
        last_feed_kernel,
        out_shape=tuple(jax.ShapeDtypeStruct((rows, size), f32) for size in (ff, ff, 1)),
        in_specs=[pl.BlockSpec(memory_space=pltpu.SMEM)] + [vm] * 5,
        out_specs=[vm] * 3,
        compiler_params=pltpu.CompilerParams(vmem_limit_bytes=40 * 2**20),
        name="last_feed",
    )(where, mine, other, gate, up, gain)


def last_out_kernel(where_ref, mine_ref, other_ref, weight_ref, gain_ref,
                    mix_ref, att_ref, down_ref, gmix_ref):
    is0 = where_ref[1] == 0
    hr = mine_ref.shape[0]
    width = mix_ref.shape[1]
    mixw = mix_ref.shape[0]
    for b in range(2):
        cols = slice(b * width, (b + 1) * width)
        for i, grad in enumerate(halves_in_order(is0, mine_ref, other_ref, cols)):
            at = i * 2 * hr + b * hr
            end = at + hr
            inside = min(end, mixw) - at
            if inside > 0:
                here = slice(at, at + inside)
                own = grad[:inside]
                mix_ref[here, :] = own
                total = jnp.sum(own * weight_ref[here, :].astype(f32), axis=1, keepdims=True)
                gmix_ref[here, :] = total / gain_ref[here, :].astype(f32)
            if inside < hr:
                begin = max(inside, 0)
                att_ref[at + begin - mixw : end - mixw, :] = grad[begin:]
        cols = slice((2 + b) * width, (3 + b) * width)
        for i, grad in enumerate(halves_in_order(is0, mine_ref, other_ref, cols)):
            at = i * 2 * hr + b * hr
            down_ref[at : at + hr, :] = grad


def last_out(where, mine, other, weight, gain, attw):
    vm = pl.BlockSpec(memory_space=pltpu.VMEM)
    mixw, width = weight.shape
    shapes = ((mixw, width), (attw, width), (mixw + attw, width), (mixw, 1))
    return pl.pallas_call(
        last_out_kernel,
        out_shape=tuple(jax.ShapeDtypeStruct(shape, f32) for shape in shapes),
        in_specs=[pl.BlockSpec(memory_space=pltpu.SMEM)] + [vm] * 4,
        out_specs=[vm] * 4,
        compiler_params=pltpu.CompilerParams(vmem_limit_bytes=40 * 2**20),
        name="last_out",
    )(where, mine, other, weight, gain)


def heads_of(raw, offset, rates):
    z = raw + offset
    step = jnp.maximum(z, 0.0) + jnp.log(1.0 + jnp.exp(-jnp.abs(z)))
    hi, mid, low = three(-step * rates)
    shape = (raw.shape[0], raw.shape[0])
    causal = lax.broadcasted_iota(jnp.int32, shape, 0) >= lax.broadcasted_iota(
        jnp.int32, shape, 1
    )
    tril = causal.astype(bf16)
    cum = dot(tril, hi) + dot(tril, mid) + dot(tril, low)
    return z, step, cum, causal


def dot3(kind, a, b):
    a_hi, a_lo = two(a)
    b_hi, b_lo = two(b)
    return kind(a_hi, b_hi) + kind(a_hi, b_lo) + kind(a_lo, b_hi)


def lane_halves(shape):
    return lax.broadcasted_iota(jnp.int32, shape, 1) < MP


def conv_sums(ext, taps_ref, bias_ref, act_ref, rows):
    part = 256
    for at in range(0, CONVW, part):
        cols = slice(at, at + part)
        total = bias_ref[:, cols]
        for tap in range(KC):
            start = 16 - (KC - 1) + tap
            total = total + taps_ref[tap : tap + 1, cols] * ext[start : start + rows, cols]
        act_ref[:, cols] = total


def ssm_kernel(
    conv_ref, edge_ref, raw_ref, taps_ref, bias_ref, off_ref, rate_ref, skip_ref,
    act_ref, zero_ref, state_ref, c_ref, ecum_ref, ext,
):
    rows = conv_ref.shape[0]
    ext[0:16, :] = edge_ref[...].astype(f32)
    ext[16:, :] = conv_ref[...].astype(f32)
    conv_sums(ext, taps_ref, bias_ref, act_ref, rows)
    unused, step, cum, causal = heads_of(raw_ref[...], off_ref[...], rate_ref[...])
    cum_t, step_t = jnp.transpose(cum), jnp.transpose(step)
    table = head_table()
    b_state = silu_parts(act_ref[:, INNER : INNER + NS])[0]
    c_state = silu_parts(act_ref[:, INNER + NS :])[0]
    c_ref[...] = c_state
    ecum_ref[...] = jnp.exp(cum)
    inter = dot3(dot_nt, c_state, b_state)
    last = cum[rows - 1 : rows, :]
    tail = exact_dot(jnp.exp(last - cum) * step, table)
    low_lane = lane_halves((rows, 2 * MP))
    b_hi, b_lo = two(b_state)
    for pair in range(MH // 2):
        cols = slice(pair * 2 * MP, (pair + 1) * 2 * MP)
        x = silu_parts(act_ref[:, cols])[0]
        mixes = []
        for h in (2 * pair, 2 * pair + 1):
            gaps = jnp.where(causal, cum[:, h : h + 1] - cum_t[h : h + 1, :], -1e30)
            mixes.append((jnp.exp(gaps) * inter * step_t[h : h + 1, :]).astype(bf16))
        low = x.astype(bf16)
        none = jnp.zeros_like(low)
        stacked = jnp.concatenate(
            [jnp.where(low_lane, low, none), jnp.where(low_lane, none, low)], axis=0
        )
        within = dot(jnp.concatenate(mixes, axis=1), stacked)
        zero_ref[:, cols] = within + skip_ref[:, cols] * x
        t_hi, t_lo = two(tail[:, cols] * x)
        state = dot_tn(t_hi, b_hi) + dot_tn(t_hi, b_lo) + dot_tn(t_lo, b_hi)
        state_ref[cols, :] = state.astype(bf16)


def ssm_forward(conv_low, edge, raw, taps, bias, offset, rates, skip_wide):
    rows = conv_low.shape[0]
    vm = pl.BlockSpec(memory_space=pltpu.VMEM)
    return pl.pallas_call(
        ssm_kernel,
        out_shape=(
            jax.ShapeDtypeStruct((rows, CONVW), f32),
            jax.ShapeDtypeStruct((rows, INNER), f32),
            jax.ShapeDtypeStruct((INNER, NS), bf16),
            jax.ShapeDtypeStruct((rows, NS), f32),
            jax.ShapeDtypeStruct((rows, 128), f32),
        ),
        in_specs=[vm] * 8,
        out_specs=[vm] * 5,
        scratch_shapes=[pltpu.VMEM((rows + 16, CONVW), f32)],
        compiler_params=pltpu.CompilerParams(vmem_limit_bytes=32 * 2**20),
        cost_estimate=pl.CostEstimate(
            flops=2 * MH * rows * rows * 512, bytes_accessed=6 * 2**20, transcendentals=10**6
        ),
        name="ssm_forward",
    )(conv_low, edge, raw, taps, bias, offset, rates, skip_wide)


def ssm_back_kernel(
    conv_ref, edge_ref, raw_ref, taps_ref, off_ref, rate_ref, skip_ref, act_ref,
    dssm_ref, dc_in_ref, dcum_ref, later_ref, start_ref,
    dconv_ref, dedge_ref, draw_ref, extra_ref, ext, dact, rowg, colq, rows_out,
):
    rows = conv_ref.shape[0]
    ext[0:16, :] = edge_ref[...].astype(f32)
    ext[16:, :] = conv_ref[...].astype(f32)
    z, step, cum, causal = heads_of(raw_ref[...], off_ref[...], rate_ref[...])
    cum_t, step_t = jnp.transpose(cum), jnp.transpose(step)
    table = head_table()
    b_state, b_slope = silu_parts(act_ref[:, INNER : INNER + NS])
    c_state, c_slope = silu_parts(act_ref[:, INNER + NS :])
    inter = dot3(dot_nt, c_state, b_state)
    last = cum[rows - 1 : rows, :]
    reach = jnp.exp(last - cum)
    tail = exact_dot(reach * step, table)
    low_lane = lane_halves((rows, 2 * MP))
    b_hi, b_lo = two(b_state)
    dact[0:8, :] = jnp.zeros((8, CONVW), f32)
    dact[rows + 8 :, :] = jnp.zeros((8, CONVW), f32)
    rowg[...] = jnp.zeros_like(rowg)
    colq[...] = jnp.zeros_like(colq)
    d_inter = jnp.zeros((rows, rows), f32)
    d_b = jnp.zeros((rows, NS), f32)
    d_tail = jnp.zeros((rows, 128), f32)
    d_decay = jnp.zeros((8, 128), f32)
    d_skip = jnp.zeros((8, 128), f32)
    ones = jnp.ones((8, NS), bf16)
    for pair in range(MH // 2):
        cols = slice(pair * 2 * MP, (pair + 1) * 2 * MP)
        x, slope = silu_parts(act_ref[:, cols])
        dy = dssm_ref[:, cols]
        x_low, dy_low = x.astype(bf16), dy.astype(bf16)
        none = jnp.zeros_like(dy_low)
        stacked = jnp.concatenate(
            [jnp.where(low_lane, dy_low, none), jnp.where(low_lane, none, dy_low)], axis=0
        )
        d_mix = dot_nt(stacked, x_low)
        mixes = []
        for i, h in enumerate((2 * pair, 2 * pair + 1)):
            gaps = jnp.where(causal, cum[:, h : h + 1] - cum_t[h : h + 1, :], -1e30)
            weight = jnp.exp(gaps)
            step_row = step_t[h : h + 1, :]
            dm_w = d_mix[i * rows : (i + 1) * rows, :] * weight
            q = dm_w * inter
            d_inter = d_inter + dm_w * step_row
            colq[h : h + 1, :] = jnp.sum(q, axis=0, keepdims=True)
            rowg[:, h : h + 1] = jnp.sum(q * step_row, axis=1, keepdims=True)
            mixes.append((weight * inter * step_row).astype(bf16))
        dx = dot_tn(jnp.concatenate(mixes, axis=0), stacked)
        later = later_ref[cols, :]
        from_state = dot_nt(b_hi, later) + dot_nt(b_lo, later)
        tail_part = tail[:, cols]
        dx = dx + skip_ref[:, cols] * dy + tail_part * from_state
        dact[8 : rows + 8, cols] = dx * slope
        part_table = table[:, cols]
        d_tail = d_tail + exact_dot_nt(x * from_state, part_table)
        t_hi, t_lo = two(tail_part * x)
        d_b = d_b + dot(t_hi, later) + dot(t_lo, later)
        held = later.astype(f32) * start_ref[cols, :].astype(f32)
        hi, mid, low = three(held)
        sums = dot_nt(ones, hi) + dot_nt(ones, mid) + dot_nt(ones, low)
        d_decay = d_decay + exact_dot_nt(sums, part_table)
        skips = jnp.broadcast_to(jnp.sum(dy * x, axis=0, keepdims=True), (8, 2 * MP))
        d_skip = d_skip + exact_dot_nt(skips, part_table)
    d_b = d_b + dot3(dot_tn, d_inter, c_state)
    d_c = dc_in_ref[...] + dot3(dot, d_inter, b_state)
    dact[8 : rows + 8, INNER : INNER + NS] = d_b * b_slope
    dact[8 : rows + 8, INNER + NS :] = d_c * c_slope
    col = jnp.transpose(colq[...])
    moved = d_tail * reach
    fade = moved * step
    d_cum = dcum_ref[...] + rowg[...] - col * step - fade
    at_last = jnp.sum(fade, axis=0, keepdims=True) + d_decay[0:1, :] * jnp.exp(last)
    is_last = lax.broadcasted_iota(jnp.int32, (rows, 128), 0) == rows - 1
    d_cum = d_cum + jnp.where(is_last, at_last, 0.0)
    shape = (rows, rows)
    triu = (
        lax.broadcasted_iota(jnp.int32, shape, 0) <= lax.broadcasted_iota(jnp.int32, shape, 1)
    ).astype(bf16)
    hi, mid, low = three(d_cum)
    d_log = dot(triu, hi) + dot(triu, mid) + dot(triu, low)
    d_step = col + moved - rate_ref[...] * d_log
    d_raw = d_step / (1.0 + jnp.exp(-z))
    draw_ref[...] = d_raw
    rows_out[...] = jnp.zeros_like(rows_out)
    rows_out[2:3, CONVW : CONVW + 128] = jnp.sum(d_raw, axis=0, keepdims=True)
    rows_out[2:3, CONVW + 128 : CONVW + 256] = jnp.sum(-step * d_log, axis=0, keepdims=True)
    rows_out[2:3, CONVW + 256 : CONVW + 384] = d_skip[0:1, :]
    part = 256
    for at in range(0, CONVW, part):
        cols = slice(at, at + part)
        own = dact[8 : rows + 8, cols]
        total = jnp.zeros((rows, part), f32)
        edge = jnp.zeros((8, part), f32)
        for tap in range(KC):
            weight = taps_ref[tap : tap + 1, cols]
            start = 8 + KC - 1 - tap
            total = total + weight * dact[start : start + rows, cols]
            edge = edge + weight * dact[8 - tap : 16 - tap, cols]
            seen = ext[16 - (KC - 1) + tap : 16 - (KC - 1) + tap + rows, cols]
            to = (tap % 2) * CONVW + at
            rows_out[tap // 2 : tap // 2 + 1, to : to + part] = jnp.sum(
                own * seen, axis=0, keepdims=True
            )
        rows_out[2:3, cols] = jnp.sum(own, axis=0, keepdims=True)
        dconv_ref[:, cols] = total
        dedge_ref[:, cols] = edge
    hi, low = two(rows_out[...])
    extra_ref[...] = jnp.concatenate([hi.astype(f32), low.astype(f32)], axis=0).astype(bf16)


def ssm_backward(conv_low, edge, raw, taps, offset, rates, skip_wide, act,
                 d_ssm, d_c, d_cum, later, start, wide):
    rows = conv_low.shape[0]
    vm = pl.BlockSpec(memory_space=pltpu.VMEM)
    return pl.pallas_call(
        ssm_back_kernel,
        out_shape=(
            jax.ShapeDtypeStruct((rows, CONVW), f32),
            jax.ShapeDtypeStruct((8, CONVW), f32),
            jax.ShapeDtypeStruct((rows, 128), f32),
            jax.ShapeDtypeStruct((16, wide), bf16),
        ),
        in_specs=[vm] * 13,
        out_specs=[vm] * 4,
        scratch_shapes=[
            pltpu.VMEM((rows + 16, CONVW), f32),
            pltpu.VMEM((rows + 16, CONVW), f32),
            pltpu.VMEM((rows, 128), f32),
            pltpu.VMEM((128, rows), f32),
            pltpu.VMEM((8, wide), f32),
        ],
        compiler_params=pltpu.CompilerParams(vmem_limit_bytes=32 * 2**20),
        cost_estimate=pl.CostEstimate(
            flops=2 * MH * rows * rows * 1024, bytes_accessed=8 * 2**20, transcendentals=10**6
        ),
        name="ssm_backward",
    )(conv_low, edge, raw, taps, offset, rates, skip_wide, act,
      d_ssm, d_c, d_cum, later, start)


def allowed_keys(place_ref, rows, chips):
    core, chip = place_ref[1], place_ref[2]
    total = 2 * chips * rows
    key = lax.broadcasted_iota(jnp.int32, (rows, total), 1)
    query = (chip * 2 + core) * rows + lax.broadcasted_iota(jnp.int32, (rows, total), 0)
    block = key // rows
    side = block // chips
    key_chip = chip - block % chips
    parity = jnp.where(side == 0, core, 1 - core)
    position = (key_chip * 2 + parity) * rows + key % rows
    return (key_chip >= 0) & (position <= query)


def key_block(own_ref, sib_ref, rows, at):
    chips = own_ref.shape[0]
    parts = [own_ref[k, :rows, at : at + HEAD_SIZE] for k in range(chips)]
    parts += [sib_ref[k, :rows, at : at + HEAD_SIZE] for k in range(chips)]
    return jnp.concatenate(parts, axis=0)


def attend_kernel(place_ref, q_ref, own_ref, sib_ref, out_ref, top_ref, sum_ref):
    rows = q_ref.shape[0]
    allowed = allowed_keys(place_ref, rows, own_ref.shape[0])
    scale = HEAD_SIZE ** (-0.5)
    top_ref[...] = jnp.zeros_like(top_ref)
    sum_ref[...] = jnp.zeros_like(sum_ref)
    for g in range(VALUE_HEADS):
        keys = key_block(own_ref, sib_ref, rows, g * HEAD_SIZE)
        values = key_block(own_ref, sib_ref, rows, KW + g * HEAD_SIZE)
        for i in range(GROUP):
            h = g * GROUP + i
            cols = slice(h * HEAD_SIZE, (h + 1) * HEAD_SIZE)
            scores = dot_nt(q_ref[:, cols], keys) * scale
            scores = jnp.where(allowed, scores, -1e30)
            top = jnp.max(scores, axis=1, keepdims=True)
            raised = jnp.exp(scores - top)
            total = jnp.sum(raised, axis=1, keepdims=True)
            prob = (raised * (1.0 / total)).astype(bf16)
            out_ref[:, cols] = dot(prob, values).astype(bf16)
            top_ref[:, h : h + 1] = top
            sum_ref[:, h : h + 1] = 1.0 / total


def attend(where, queries, kv_own, kv_sib):
    rows = queries.shape[0]
    vm = pl.BlockSpec(memory_space=pltpu.VMEM)
    keys = 2 * kv_own.shape[0] * rows
    return pl.pallas_call(
        attend_kernel,
        out_shape=(
            jax.ShapeDtypeStruct((rows, QW), bf16),
            jax.ShapeDtypeStruct((rows, 128), f32),
            jax.ShapeDtypeStruct((rows, 128), f32),
        ),
        in_specs=[pl.BlockSpec(memory_space=pltpu.SMEM)] + [vm] * 3,
        out_specs=[vm] * 3,
        compiler_params=pltpu.CompilerParams(vmem_limit_bytes=48 * 2**20),
        cost_estimate=pl.CostEstimate(
            flops=4 * rows * keys * QW, bytes_accessed=4 * kv_own.size,
            transcendentals=rows * keys * QUERY_HEADS,
        ),
        name="attend",
    )(where, queries, kv_own, kv_sib)


def half_turned(x):
    lane = lax.broadcasted_iota(jnp.int32, x.shape, 1)
    first = lane % HEAD_SIZE < HEAD_SIZE // 2
    return jnp.where(
        first, pltpu.roll(x, 128 - HEAD_SIZE // 2, 1), pltpu.roll(x, HEAD_SIZE // 2, 1)
    )


def attend_back_kernel(
    place_ref, q_ref, own_ref, sib_ref, top_ref, sum_ref, dout_ref, cos_ref, sin_ref,
    dq_ref, down_ref, dsib_ref, dq_s,
):
    rows = q_ref.shape[0]
    chips = own_ref.shape[0]
    allowed = allowed_keys(place_ref, rows, chips)
    scale = HEAD_SIZE ** (-0.5)
    for g in range(VALUE_HEADS):
        keys = key_block(own_ref, sib_ref, rows, g * HEAD_SIZE)
        values = key_block(own_ref, sib_ref, rows, KW + g * HEAD_SIZE)
        d_keys = jnp.zeros(keys.shape, f32)
        d_values = jnp.zeros(keys.shape, f32)
        for i in range(GROUP):
            h = g * GROUP + i
            cols = slice(h * HEAD_SIZE, (h + 1) * HEAD_SIZE)
            q = q_ref[:, cols]
            d_out = dout_ref[:, cols]
            scores = dot_nt(q, keys) * scale
            scores = jnp.where(allowed, scores, -1e30)
            prob = jnp.exp(scores - top_ref[:, h : h + 1]) * sum_ref[:, h : h + 1]
            d_prob = dot_nt(d_out, values)
            delta = jnp.sum(prob * d_prob, axis=1, keepdims=True)
            d_score = (prob * (d_prob - delta)).astype(bf16)
            dq_s[:, cols] = dot(d_score, keys) * scale
            d_keys = d_keys + dot_tn(d_score, q)
            d_values = d_values + dot_tn(prob.astype(bf16), d_out)
        d_keys = d_keys * scale
        for k in range(chips):
            at = k * rows
            cols = slice(g * HEAD_SIZE, (g + 1) * HEAD_SIZE)
            more = slice(KW + g * HEAD_SIZE, KW + (g + 1) * HEAD_SIZE)
            down_ref[k, :, cols] = d_keys[at : at + rows]
            down_ref[k, :, more] = d_values[at : at + rows]
            at += chips * rows
            dsib_ref[k, :, cols] = d_keys[at : at + rows].astype(bf16)
            dsib_ref[k, :, more] = d_values[at : at + rows].astype(bf16)
    for at in range(0, QW, 128):
        x = dq_s[:, at : at + 128]
        turned = x * cos_ref[...] - half_turned(x) * sin_ref[...]
        dq_ref[:, at : at + 128] = turned.astype(bf16)


def attend_back(where, queries, kv_own, kv_sib, top, total, d_att, cosine, sine):
    rows = queries.shape[0]
    chips = kv_own.shape[0]
    vm = pl.BlockSpec(memory_space=pltpu.VMEM)
    keys = 2 * chips * rows
    return pl.pallas_call(
        attend_back_kernel,
        out_shape=(
            jax.ShapeDtypeStruct((rows, QW), bf16),
            jax.ShapeDtypeStruct((chips, rows, 2 * KW), f32),
            jax.ShapeDtypeStruct((chips, rows, 2 * KW), bf16),
        ),
        in_specs=[pl.BlockSpec(memory_space=pltpu.SMEM)] + [vm] * 8,
        out_specs=[vm] * 3,
        scratch_shapes=[pltpu.VMEM((rows, QW), f32)],
        compiler_params=pltpu.CompilerParams(vmem_limit_bytes=48 * 2**20),
        cost_estimate=pl.CostEstimate(
            flops=10 * rows * keys * QW, bytes_accessed=8 * kv_own.size,
            transcendentals=rows * keys * QUERY_HEADS,
        ),
        name="attend_back",
    )(where, queries, kv_own, kv_sib, top, total, d_att, cosine, sine)


def pack_kernel(
    dq_ref, dkv_ref, cos_ref, sin_ref, dgz_ref, dconv_ref, edge_ref, draw_ref, extra_ref, *refs
):
    arrived, out_ref, conv = refs[:-2], refs[-2], refs[-1]
    rows = dq_ref.shape[0]
    d_kv = dkv_ref[...]
    for ref in arrived:
        d_kv = d_kv + ref[...].astype(f32)
    d_k = d_kv[:, :KW]
    d_k = d_k * cos_ref[...] - half_turned(d_k) * sin_ref[...]
    out_ref[:rows, :QW] = dq_ref[...]
    out_ref[:rows, QW : QW + KW] = d_k.astype(bf16)
    out_ref[:rows, QW + KW : QW + 2 * KW] = d_kv[:, KW:].astype(bf16)
    at = QW + 2 * KW
    out_ref[:rows, at : at + INNER] = dgz_ref[...]
    at += INNER
    conv[...] = dconv_ref[...]
    more = edge_ref[0 : KC - 1, :]
    conv[rows - (KC - 1) :, :] = conv[rows - (KC - 1) :, :] + more
    out_ref[:rows, at : at + CONVW] = conv[...].astype(bf16)
    at += CONVW
    out_ref[:rows, at:] = draw_ref[...].astype(bf16)
    out_ref[rows:, :] = extra_ref[...]


def pack(d_q, d_kv, cosine, sine, d_gate_z, d_conv, edge, d_raw, extra, arrived):
    rows = d_q.shape[0]
    vm = pl.BlockSpec(memory_space=pltpu.VMEM)
    return pl.pallas_call(
        pack_kernel,
        out_shape=jax.ShapeDtypeStruct((rows + 16, extra.shape[1]), bf16),
        in_specs=[vm] * (9 + len(arrived)),
        out_specs=vm,
        scratch_shapes=[pltpu.VMEM((rows, CONVW), f32)],
        compiler_params=pltpu.CompilerParams(vmem_limit_bytes=32 * 2**20),
        cost_estimate=pl.CostEstimate(flops=10**6, bytes_accessed=4 * 2**20, transcendentals=0),
        name="pack",
    )(d_q, d_kv, cosine, sine, d_gate_z, d_conv, edge, d_raw, extra, *arrived)


def body(
    tokens,
    cotangent,
    gain_input,
    w_query,
    key_weight,
    value_weight,
    w_mixin,
    conv_taps,
    conv_bias,
    step_offset,
    decay_rate,
    skip_gain,
    gain_mixer,
    w_mixout,
    w_attnout,
    gain_feed,
    w_gate,
    w_up,
    w_down,
):
    rows, width = tokens.shape
    seqs = lax.axis_size("seq")
    ctxs = lax.axis_size("ctx")
    chips = ctxs // 2
    place = lax.axis_index("seq")
    ctx = lax.axis_index("ctx")
    chip, core = ctx // 2, ctx % 2
    ff = w_gate.shape[1]

    used = QW + 2 * KW + w_mixin.shape[1]
    wide = -(-used // 128) * 128
    cut = width // (4 * seqs)
    cut = cut if cut % 16 == 0 else 0
    in_parts = [w_query, key_weight, value_weight, w_mixin]

    def joined(parts):
        blank = jnp.zeros((parts[0].shape[0], wide - used), bf16)
        return jnp.concatenate([*parts, blank], axis=1)

    in_half = joined(lax.optimization_barrier([take_half(part, core) for part in in_parts]))
    near = first_phase(in_half)
    sizes = (gain_input.size, gain_feed.size, conv_bias.size, gain_mixer.size, conv_taps.size)
    small = jnp.concatenate(
        [gain_input, gain_feed, conv_bias, gain_mixer, conv_taps.reshape(-1)]
    )
    small = [small] + [seq_swap(small, k) for k in range(1, seqs)]
    near, small, in_parts = lax.optimization_barrier((near, small, in_parts))
    w_in = second_phase(near, cut)
    in_loc = joined(in_parts)
    bit = 1
    while bit < seqs:
        flip = (place & bit) != 0
        small = [jnp.where(flip, small[j ^ bit], small[j]) for j in range(seqs)]
        bit *= 2
    small = jnp.stack(small).astype(f32)
    at = 0
    pieces = []
    for size in sizes:
        pieces.append(small[:, at : at + size])
        at += size
    gin = pieces[0].reshape(-1)
    gfeed = pieces[1].reshape(-1)
    cbias = pieces[2].reshape(-1)
    gmix = pieces[3].reshape(-1)
    taps = pieces[4].reshape(seqs, KC, -1).transpose(1, 0, 2).reshape(KC, -1)

    out_loc = jnp.concatenate([w_mixout, w_attnout], axis=0)
    half_out = take_half(out_loc, core)
    half_dn = take_half(w_down, core)
    hr = half_out.shape[0] // 2
    rest = jnp.concatenate(
        [
            take_half(w_gate, core),
            take_half(w_up, core),
            half_out[:hr],
            half_out[hr:],
            half_dn[:hr],
            half_dn[hr:],
        ],
        axis=1,
    )
    where = jnp.stack([place, core, chip]).astype(jnp.int32)

    position = ctx * rows + jnp.arange(rows, dtype=jnp.int32)
    frequency = rope_base ** (
        -(jnp.arange(HEAD_SIZE // 2, dtype=f32) * 2.0 / HEAD_SIZE)
    )
    angles = position.astype(f32)[:, None] * jnp.tile(frequency, 4)[None, :]
    sign = jnp.tile(jnp.repeat(jnp.array([-1.0, 1.0], f32), HEAD_SIZE // 2), 2)
    cosine = jnp.cos(angles)
    sine = jnp.sin(angles) * sign[None, :]
    offset = jnp.pad(step_offset, (0, 128 - MH))[None, :]
    rates = jnp.pad(decay_rate, (0, 128 - MH))[None, :]
    skip_wide = jnp.repeat(skip_gain, MP)[None, :]

    rest, far_in = lax.optimization_barrier((rest, w_in[-1][2]))
    w_in[-1] = (*w_in[-1][:2], far_in)
    w_in = both_cores(w_in)
    near = first_phase(rest)
    normed, queries, message, gate_z, conv_low, raw_step = project(
        where, tokens, gin[None, :], cosine, sine, offset, rates, in_loc, w_in
    )
    mix0 = QW + 2 * KW

    edge = lax.ppermute(
        conv_low[rows - 16 :], "ctx", [(i, i + 1) for i in range(ctxs - 1)]
    )
    kv_own = jnp.stack([message] + [chip_shift(message, k, True) for k in range(1, chips)])
    kv_sib = swap_core(kv_own)
    dec_own = kv_own[:, rows, :MH].astype(f32) + kv_own[:, rows + 1, :MH].astype(f32)
    dec_sib = kv_sib[:, rows, :MH].astype(f32) + kv_sib[:, rows + 1, :MH].astype(f32)
    decays = jnp.stack(
        [jnp.where(core == 0, dec_own, dec_sib), jnp.where(core == 0, dec_sib, dec_own)], axis=1
    )
    by_chip = jnp.arange(chips, dtype=jnp.int32)
    picked = (chip - by_chip) % chips
    decays = jnp.stack(
        [
            sum(jnp.where(picked[c] == k, decays[k], 0.0) for k in range(chips))
            for c in range(chips)
        ]
    )

    act, out_zero, local_state, c_state, exp_cum = ssm_forward(
        conv_low, edge, raw_step, taps, cbias[None, :], offset, rates, skip_wide
    )
    start_state = ctx_state(local_state, decays, chips, chip, core, False)
    cots = [cotangent] + [p[2] for p in gather_pieces(cotangent, rows // 2)]
    queries, near = lax.optimization_barrier((queries, near))
    rest_far = second_phase(near, cut)
    w_rest = both_cores(rest_far)
    attn_b, top, total = attend(where, queries, kv_own, kv_sib)

    layer_out, msg1, msg2, d_gu, grad_res, d_att, d_ssm, d_gate_z, d_start, d_c, d_cum = middle(
        where, tokens, cotangent, normed, out_zero, gate_z, c_state, exp_cum, start_state, attn_b,
        gmix[None, :], gfeed[None, :], (w_gate, w_up, w_mixout, w_attnout, w_down), w_rest, seqs,
    )
    msgs1 = [msg1[0]] + [seq_swap(msg1[k], k) for k in range(1, seqs)]
    d_att, d_gu, msg2, msgs1 = lax.optimization_barrier((d_att, d_gu, msg2, msgs1))
    near = first_phase(d_gu)
    msgs2 = [msg2[0]] + [seq_swap(msg2[k], k) for k in range(1, seqs)]

    later_grad = ctx_state(d_start, decays, chips, chip, core, True)
    d_q, d_kv, d_kv_sib = attend_back(
        where, queries, kv_own, kv_sib, top, total, d_att, cosine, sine
    )
    d_kv = d_kv + swap_core(d_kv_sib).astype(f32)
    arrived = [chip_shift(d_kv[k].astype(bf16), -k, False) for k in range(1, chips)]
    later_grad, near = lax.optimization_barrier((later_grad, near))
    rights2 = [d_gu] + [p[2] for p in second_phase(near, rows // 2)]
    d_conv, d_edge, d_raw, extra = ssm_backward(
        conv_low, edge, raw_step, taps, offset, rates, skip_wide, act,
        d_ssm, d_c, d_cum, later_grad, start_state, wide,
    )
    edge_back = lax.ppermute(d_edge, "ctx", [(i + 1, i) for i in range(ctxs - 1)])
    back_msg = pack(
        d_q, d_kv[0], cosine, sine, d_gate_z, d_conv, edge_back, d_raw, extra, arrived
    )
    keep1, give1 = grads(grads_kernel, "out_grads", where, msgs1, cots, hr, 4 * width)
    back_msg, rights2, msgs2, give1 = lax.optimization_barrier((back_msg, rights2, msgs2, give1))
    total1, unused = sum_halves(keep1, swap_core(give1), chips, chip, None)
    keep2, give2 = grads(feed_grads_kernel, "feed_grads", where, msgs2, rights2, hr, 2 * ff)
    total2, unused = sum_halves(keep2, swap_core(give2), chips, chip, None)
    mine1 = spread_halves(total1, chips, chip)
    backs = [back_msg] + [p[2] for p in gather_pieces(back_msg, rows // 2)]
    backs[0], total2, mine1 = lax.optimization_barrier((backs[0], total2, mine1))
    keep3, give3, small = last_grads(where, msgs2, backs, hr, rows // 2)
    mine2 = spread_halves(total2, chips, chip)
    total3, small_sum = sum_halves(keep3, swap_core(give3), chips, chip, small)
    grad_tokens = unproject(where, tokens, gin[None, :], grad_res, back_msg, in_loc, w_in)
    sums_out = last_out(
        where, mine1, swap_core(mine1), w_mixout, gain_mixer[:, None], QW // seqs
    )
    total3, mine2, grad_tokens, sums_out = lax.optimization_barrier(
        (total3, mine2, grad_tokens, sums_out)
    )
    sum_mix, sum_att, sum_dn, grad_gmix = sums_out
    mine3 = spread_halves(total3, chips, chip)
    sums_feed = last_feed(where, mine2, swap_core(mine2), w_gate, w_up, gain_feed[:, None])
    mine3, sums_feed = lax.optimization_barrier((mine3, sums_feed))
    sum_gate, sum_up, grad_gfeed = sums_feed
    sum_q, sum_k, sum_v, sum_mixin, grad_gin = last_in(
        where, mine3, swap_core(mine3), in_loc, gain_input[:, None], used - mix0
    )
    small_taps = small_sum[:2, : 2 * CONVW].reshape(KC, CONVW)

    def own_share(vec):
        size = vec.shape[-1] // seqs
        return lax.dynamic_slice_in_dim(vec, place * size, size, vec.ndim - 1)

    heads = small_sum[2, CONVW:]
    return (
        layer_out,
        grad_tokens,
        grad_gin[:, 0],
        sum_q,
        sum_k,
        sum_v,
        sum_mixin.T,
        own_share(small_taps),
        own_share(small_sum[2, :CONVW]),
        heads[:MH],
        heads[128 : 128 + MH],
        heads[256 : 256 + MH],
        grad_gmix[:, 0],
        sum_mix,
        sum_att,
        grad_gfeed[:, 0],
        sum_gate,
        sum_up,
        sum_dn,
    )


def solution(mesh):
    rows = P(("seq", "ctx"), None)
    vec = P("seq")
    mat = P("seq", None)
    col = P(None, "seq")
    rep = P()
    in_specs = (
        rows, rows, vec, mat, mat, mat, mat, col, vec, rep, rep, rep, vec, mat, mat, vec, mat, mat, mat,
    )
    out_specs = (
        rows, rows, vec, mat, mat, mat, mat, col, vec, rep, rep, rep, vec, mat, mat, vec, mat, mat, mat,
    )
    return jax.shard_map(body, mesh=mesh, in_specs=in_specs, out_specs=out_specs, check_vma=False)
```
